32 devices in a mesh: dev: 32 (over z, y, x, core).
Axes of the slice: x: 2, y: 2, z: 4, core: 2. Of those that a mesh axis runs over, the one named last changes fastest.
Arguments:
- frames: bfloat16 [512, 20480], P('dev'), may hold values from -6 to 6
- norm1_gain: bfloat16 [512], P('dev'), may hold values from 0.099609375 to 1.8984375
- norm1_shift: bfloat16 [512], P('dev'), may hold values from -3 to 3
- kernel_query: bfloat16 [512, 3], P('dev'), may hold values from -3 to 3
- kernel_key: bfloat16 [512, 3], P('dev'), may hold values from -3 to 3
- kernel_value: bfloat16 [512, 3], P('dev'), may hold values from -3 to 3
- w_query: bfloat16 [512, 512], P('dev'), may hold values from -0.375 to 0.375
- w_key: bfloat16 [512, 512], P('dev'), may hold values from -0.375 to 0.375
- w_value: bfloat16 [512, 512], P('dev'), may hold values from -0.25 to 0.25
- w_out: bfloat16 [512, 512], P('dev'), may hold values from -0.5 to 0.5
- scale_attn: bfloat16 [512], P('dev'), may hold values from 0.5 to 1.5
- norm2_gain: bfloat16 [512], P('dev'), may hold values from 0.099609375 to 1.8984375
- norm2_shift: bfloat16 [512], P('dev'), may hold values from -3 to 3
- w_up: bfloat16 [512, 2048], P('dev'), may hold values from -0.25 to 0.25
- w_down: bfloat16 [2048, 512], P('dev'), may hold values from -0.1875 to 0.1875
- scale_mlp: bfloat16 [512], P('dev'), may hold values from 0.5 to 1.5
- cotangent: bfloat16 [512, 20480], P('dev'), may hold values from -6 to 6
Outputs:
- output: bfloat16 [512, 20480], P('dev')
- frames_grad: bfloat16 [512, 20480], P('dev')
- grad_norm1_gain: float32 [512], P('dev')
- grad_norm1_shift: float32 [512], P('dev')
- grad_kernel_query: float32 [512, 3], P('dev')
- grad_kernel_key: float32 [512, 3], P('dev')
- grad_kernel_value: float32 [512, 3], P('dev')
- grad_w_query: float32 [512, 512], P('dev')
- grad_w_key: float32 [512, 512], P('dev')
- grad_w_value: float32 [512, 512], P('dev')
- grad_w_out: float32 [512, 512], P('dev')
- grad_scale_attn: float32 [512], P('dev')
- grad_norm2_gain: float32 [512], P('dev')
- grad_norm2_shift: float32 [512], P('dev')
- grad_w_up: float32 [512, 2048], P('dev')
- grad_w_down: float32 [2048, 512], P('dev')
- grad_scale_mlp: float32 [512], P('dev')
The draws below stay inside these ranges and needn't reach their ends.
All inputs are finite; a program needn't handle non-finite values.
Results may differ from the reference program's by a relative error of at most 0.014.
The reference program's roundings to bfloat16 on the way count: a program that leaves them out, or rounds other values in their place, can miss the bound.
Values may be sent and summed in bfloat16 or wider, within the bound.
No kernel may reach another device: no remote copies, remote signals or barrier semaphores. Data moves between devices by JAX's collectives and lax.ppermute only.
A program may use at most 128 MiB of HBM per device.

```python
import jax
import jax.numpy as jnp
from jax import lax

WIDTH = 512
HEADS = 4
HEAD_DIM = 128
HIDDEN_SIZE = 2048
LENGTH = 160
WINDOW = 19
SEQ_DEV = 4
SEQS = 128


def block_scale(rng, extent, split, smallest, top_value):
    def one(axis_at, shards_of):
        steps = jax.random.uniform(jax.random.fold_in(jax.random.fold_in(rng, 6), axis_at), (shards_of,), jnp.float32, smallest / len(split), top_value / len(split))
        return jnp.repeat(jnp.exp(steps), extent[axis_at] // shards_of).reshape((-1,) + (1,) * (len(extent) - axis_at - 1))

    gain = one(*split[0])
    for cut in split[1:]:
        gain = gain * one(*cut)
    return gain


def gaussian(key, extent, scale, most, split=(), kind=jnp.bfloat16):
    loudness = block_scale(key, extent, split, -0.22, 0.18) if split else 1.0
    drawn = jax.random.normal(key, extent, jnp.float32) * scale * loudness
    return jnp.minimum(jnp.maximum(drawn, -most), most).astype(kind)


def setup_inputs(seed: int = 0) -> dict:
    key_of = jax.random.split(jax.random.key(seed), 18)
    frames = gaussian(key_of[0], (WIDTH, SEQS * LENGTH), 1.0, 6.0, ((0, 32),))
    norm1_gain = jnp.clip(1.0 + 0.18 * jax.random.normal(key_of[1], (WIDTH,), jnp.float32), 0.099609375, 1.8984375).astype(jnp.bfloat16)
    norm1_shift = gaussian(key_of[2], (WIDTH,), 0.3, 3.0, ((0, 32),))
    kernel_query = gaussian(key_of[3], (WIDTH, 3), 0.6, 3.0, ((0, 32),))
    kernel_key = gaussian(key_of[4], (WIDTH, 3), 0.6, 3.0, ((0, 32),))
    kernel_value = gaussian(key_of[5], (WIDTH, 3), 0.6, 3.0, ((0, 32),))
    w_query = gaussian(key_of[6], (WIDTH, WIDTH), (WIDTH // 2) ** -0.5, 0.375, ((0, 32),))
    w_key = gaussian(key_of[7], (WIDTH, WIDTH), (WIDTH // 2) ** -0.5, 0.375, ((0, 32),))
    w_value = gaussian(key_of[8], (WIDTH, WIDTH), WIDTH ** -0.5, 0.25, ((0, 32),))
    w_out = gaussian(key_of[9], (WIDTH, WIDTH), (WIDTH // 4) ** -0.5, 0.5, ((0, 32),))
    scale_attn = jnp.clip(0.5 + 1.0 * jax.random.uniform(key_of[10], (WIDTH,), jnp.float32) ** block_scale(key_of[10], (WIDTH,), ((0, 32),), -0.2, 0.2), 0.5, 1.5).astype(jnp.bfloat16)
    norm2_gain = jnp.clip(1.0 + 0.18 * jax.random.normal(key_of[11], (WIDTH,), jnp.float32), 0.099609375, 1.8984375).astype(jnp.bfloat16)
    norm2_shift = gaussian(key_of[12], (WIDTH,), 0.3, 3.0, ((0, 32),))
    w_up = gaussian(key_of[13], (WIDTH, HIDDEN_SIZE), WIDTH ** -0.5, 0.25, ((0, 32),))
    w_down = gaussian(key_of[14], (HIDDEN_SIZE, WIDTH), (HIDDEN_SIZE // 2) ** -0.5, 0.1875, ((0, 32),))
    scale_mlp = jnp.clip(0.5 + 1.0 * jax.random.uniform(key_of[15], (WIDTH,), jnp.float32) ** block_scale(key_of[15], (WIDTH,), ((0, 32),), -0.2, 0.2), 0.5, 1.5).astype(jnp.bfloat16)
    cotangent = gaussian(key_of[16], (WIDTH, SEQS * LENGTH), 1.0, 6.0, ((0, 32),))
    return {"frames": frames, "norm1_gain": norm1_gain, "norm1_shift": norm1_shift, "kernel_query": kernel_query, "kernel_key": kernel_key, "kernel_value": kernel_value, "w_query": w_query, "w_key": w_key, "w_value": w_value, "w_out": w_out, "scale_attn": scale_attn, "norm2_gain": norm2_gain, "norm2_shift": norm2_shift, "w_up": w_up, "w_down": w_down, "scale_mlp": scale_mlp, "cotangent": cotangent}


epsilon = 1e-05

@jax.custom_vjp
def low(v):
    return lax.optimization_barrier(v.astype(jnp.bfloat16)).astype(jnp.float32)

@jax.custom_vjp
def low_back(v):
    return v

def low_keep(v):
    return (low(v), None)

def low_pass(kept, grad):
    return (grad,)

def back_keep(v):
    return (v, None)

def back_low(kept, grad):
    return (low(grad),)
low.defvjp(low_keep, low_pass)
low_back.defvjp(back_keep, back_low)

def layer_norm(values, norm_gain, norm_shift):
    center = lax.optimization_barrier(jnp.mean(values, axis=0, keepdims=True))
    centered = values - center
    spread = lax.optimization_barrier(jnp.mean(centered * centered, axis=0, keepdims=True))
    return centered * lax.rsqrt(spread + epsilon) * norm_gain[:, None, None] + norm_shift[:, None, None]

def depthwise(values, kernel):
    padded = jnp.pad(values, ((0, 0), (0, 0), (1, 1)))
    return kernel[:, 0, None, None] * padded[:, :, :-2] + kernel[:, 1, None, None] * values + kernel[:, 2, None, None] * padded[:, :, 2:]

def project(matrix, values):
    return jnp.einsum('cd,csl->dsl', matrix, values, precision=lax.Precision.HIGHEST)

def split_heads(values):
    return values.reshape(HEADS, values.shape[0] // HEADS, values.shape[1], values.shape[2])

def attend(query, key, value):
    places = jnp.arange(query.shape[2])
    nearby = jnp.abs(places[:, None] - places[None, :]) <= WINDOW // 2
    scores = jnp.einsum('hdsl,hdsm->hslm', split_heads(query), split_heads(key), precision=lax.Precision.HIGHEST) * HEAD_DIM ** (-0.5)
    scores = low_back(jnp.where(nearby, scores, -1e+30))
    top = lax.optimization_barrier(jnp.max(scores, axis=-1, keepdims=True))
    weights = jnp.exp(scores - top)
    probs = low(weights / lax.optimization_barrier(jnp.sum(weights, axis=-1, keepdims=True)))
    heads = jnp.einsum('hslm,hdsm->hdsl', probs, split_heads(value), precision=lax.Precision.HIGHEST)
    return heads.reshape(query.shape)

def layer(values, norm1_gain, norm1_shift, kernel_query, kernel_key, kernel_value, w_query, w_key, w_value, w_out, scale_attn, norm2_gain, norm2_shift, w_up, w_down, scale_mlp):
    normed = layer_norm(values, norm1_gain, norm1_shift)
    conv_q = low(depthwise(normed, kernel_query))
    conv_k = low(depthwise(normed, kernel_key))
    conv_v = low(depthwise(normed, kernel_value))
    query = low(low_back(project(w_query, conv_q)))
    key = low(low_back(project(w_key, conv_k)))
    value = low(low_back(project(w_value, conv_v)))
    heads = low(low_back(attend(query, key, value)))
    attn = low_back(project(w_out, heads))
    resid = values + scale_attn[:, None, None] * attn
    normed2 = low(layer_norm(resid, norm2_gain, norm2_shift))
    hidden = low_back(project(w_up, normed2))
    active = low(jax.nn.gelu(hidden, approximate=False))
    branch = low_back(project(w_down, active))
    return resid + scale_mlp[:, None, None] * branch

def reference(frames, norm1_gain, norm1_shift, kernel_query, kernel_key, kernel_value, w_query, w_key, w_value, w_out, scale_attn, norm2_gain, norm2_shift, w_up, w_down, scale_mlp, cotangent):
    params = tuple((weight.astype(jnp.float32) for weight in (norm1_gain, norm1_shift, kernel_query, kernel_key, kernel_value, w_query, w_key, w_value, w_out, scale_attn, norm2_gain, norm2_shift, w_up, w_down, scale_mlp)))
    width, columns = frames.shape
    length = LENGTH
    total_seqs = columns // length
    groups = total_seqs // SEQ_DEV
    grouped_x = frames.astype(jnp.float32).reshape(width, groups, SEQ_DEV, length).transpose(1, 0, 2, 3)
    grouped_c = cotangent.astype(jnp.float32).reshape(width, groups, SEQ_DEV, length).transpose(1, 0, 2, 3)

    def advance(totals, pair):
        block_x, block_c = pair
        result, pullback = jax.vjp(layer, block_x, *params)
        grads = pullback(block_c)
        totals = tuple((acc + grad for acc, grad in zip(totals, grads[1:])))
        return (totals, (result.astype(jnp.bfloat16), grads[0].astype(jnp.bfloat16)))
    starts = tuple((jnp.zeros_like(weight) for weight in params))
    totals, (results, front_grads) = lax.scan(advance, starts, (grouped_x, grouped_c))
    output = results.transpose(1, 0, 2, 3).reshape(width, columns)
    frames_grad = front_grads.transpose(1, 0, 2, 3).reshape(width, columns)
    return (output, frames_grad, totals[0], totals[1], totals[2], totals[3], totals[4], totals[5], totals[6], totals[7], totals[8], totals[9], totals[10], totals[11], totals[12], totals[13], totals[14])
```

```python
import jax
import jax.numpy as jnp
from jax import lax
from jax.sharding import PartitionSpec as P

HEADS = 4
HEAD_DIM = 128
LENGTH = 160
WINDOW = 19


epsilon = 1e-05


def layer_norm(values, norm_gain, norm_shift):
    center = jnp.mean(values, axis=0, keepdims=True)
    centered = values - center
    spread = jnp.mean(centered * centered, axis=0, keepdims=True)
    return (
        centered * lax.rsqrt(spread + epsilon) * norm_gain[:, None, None]
        + norm_shift[:, None, None]
    )


def depthwise(values, kernel):
    padded = jnp.pad(values, ((0, 0), (0, 0), (1, 1)))
    return (
        kernel[:, 0, None, None] * padded[:, :, :-2]
        + kernel[:, 1, None, None] * values
        + kernel[:, 2, None, None] * padded[:, :, 2:]
    )


def front_part(values, norm_gain, norm_shift, kernel_query, kernel_key, kernel_value):
    normed = layer_norm(values, norm_gain, norm_shift)
    return (
        depthwise(normed, kernel_query),
        depthwise(normed, kernel_key),
        depthwise(normed, kernel_value),
    )


def gelu_exact(values):
    return jax.nn.gelu(values, approximate=False)


def project(matrix, values):
    return jnp.einsum("cd,csl->dsl", matrix, values, preferred_element_type=jnp.float32)


def back_project(matrix, grads):
    return jnp.einsum("cd,dsl->csl", matrix, grads, preferred_element_type=jnp.float32)


def outer_sum(left, right):
    return jnp.einsum("csl,dsl->cd", left, right, preferred_element_type=jnp.float32)


def split_heads(values):
    return values.reshape(HEADS, values.shape[0] // HEADS, values.shape[1], values.shape[2])


def attend_forward(query, key, value):
    places = jnp.arange(query.shape[2])
    nearby = jnp.abs(places[:, None] - places[None, :]) <= WINDOW // 2
    factor = HEAD_DIM ** (-0.5)
    scores = (
        jnp.einsum(
            "hdsl,hdsm->hslm",
            split_heads(query),
            split_heads(key),
            preferred_element_type=jnp.float32,
        )
        * factor
    )
    scores = jnp.where(nearby, scores, -1e30)
    top = jnp.max(scores, axis=-1, keepdims=True)
    weights = jnp.exp(scores - top)
    probs = weights / jnp.sum(weights, axis=-1, keepdims=True)
    probs_low = probs.astype(jnp.bfloat16)
    heads = jnp.einsum(
        "hslm,hdsm->hdsl", probs_low, split_heads(value), preferred_element_type=jnp.float32
    )
    return (probs, probs_low, heads.reshape(query.shape))


def attend_backward(query, key, value, probs, probs_low, d_heads):
    factor = HEAD_DIM ** (-0.5)
    grad_heads = split_heads(d_heads)
    d_probs = jnp.einsum(
        "hdsl,hdsm->hslm", grad_heads, split_heads(value), preferred_element_type=jnp.float32
    )
    d_value = jnp.einsum(
        "hslm,hdsl->hdsm", probs_low, grad_heads, preferred_element_type=jnp.float32
    )
    d_scores = probs * (d_probs - jnp.sum(probs * d_probs, axis=-1, keepdims=True))
    d_scores = d_scores.astype(jnp.bfloat16)
    d_query = (
        jnp.einsum(
            "hslm,hdsm->hdsl", d_scores, split_heads(key), preferred_element_type=jnp.float32
        )
        * factor
    )
    d_key = (
        jnp.einsum(
            "hslm,hdsl->hdsm", d_scores, split_heads(query), preferred_element_type=jnp.float32
        )
        * factor
    )
    return tuple(
        (grad.reshape(query.shape).astype(jnp.bfloat16) for grad in (d_query, d_key, d_value))
    )


def local_step(params, local_x, local_c):
    (
        norm1_gain,
        norm1_shift,
        kernel_query,
        kernel_key,
        kernel_value,
        w_query,
        w_key,
        w_value,
        w_out,
        scale_attn,
        norm2_gain,
        norm2_shift,
        w_up,
        w_down,
        scale_mlp,
    ) = params
    values = local_x.astype(jnp.float32)
    small_front = tuple(
        (
            weight.astype(jnp.float32)
            for weight in (norm1_gain, norm1_shift, kernel_query, kernel_key, kernel_value)
        )
    )
    front_out, front_pull = jax.vjp(front_part, values, *small_front)
    conv_q, conv_k, conv_v = (piece.astype(jnp.bfloat16) for piece in front_out)
    query = project(w_query, conv_q).astype(jnp.bfloat16)
    key = project(w_key, conv_k).astype(jnp.bfloat16)
    value = project(w_value, conv_v).astype(jnp.bfloat16)
    probs, probs_low, heads_f = attend_forward(query, key, value)
    heads = heads_f.astype(jnp.bfloat16)
    attn = project(w_out, heads)
    attn_scale = scale_attn.astype(jnp.float32)[:, None, None]
    mlp_scale = scale_mlp.astype(jnp.float32)[:, None, None]
    resid = values + attn_scale * attn
    normed_f, norm_pull = jax.vjp(
        layer_norm, resid, norm2_gain.astype(jnp.float32), norm2_shift.astype(jnp.float32)
    )
    normed2 = normed_f.astype(jnp.bfloat16)
    hidden = project(w_up, normed2)
    active_f, gelu_pull = jax.vjp(gelu_exact, hidden)
    active = active_f.astype(jnp.bfloat16)
    branch = project(w_down, active)
    result = resid + mlp_scale * branch
    grad_out = local_c.astype(jnp.float32)
    grad_scale_mlp = jnp.sum(grad_out * branch, axis=(1, 2))
    d_branch = (mlp_scale * grad_out).astype(jnp.bfloat16)
    grad_w_down = outer_sum(active, d_branch)
    (d_hidden_f,) = gelu_pull(back_project(w_down, d_branch))
    d_hidden = d_hidden_f.astype(jnp.bfloat16)
    grad_w_up = outer_sum(normed2, d_hidden)
    d_resid_norm, grad_norm2_gain, grad_norm2_shift = norm_pull(back_project(w_up, d_hidden))
    d_resid = grad_out + d_resid_norm
    grad_scale_attn = jnp.sum(d_resid * attn, axis=(1, 2))
    d_attn = (attn_scale * d_resid).astype(jnp.bfloat16)
    grad_w_out = outer_sum(heads, d_attn)
    d_heads = back_project(w_out, d_attn).astype(jnp.bfloat16)
    d_query, d_key, d_value = attend_backward(query, key, value, probs, probs_low, d_heads)
    grad_w_query = outer_sum(conv_q, d_query)
    grad_w_key = outer_sum(conv_k, d_key)
    grad_w_value = outer_sum(conv_v, d_value)
    front_grads = front_pull(
        (back_project(w_query, d_query), back_project(w_key, d_key), back_project(w_value, d_value))
    )
    d_frames = d_resid + front_grads[0]
    grads = (
        front_grads[1],
        front_grads[2],
        front_grads[3],
        front_grads[4],
        front_grads[5],
        grad_w_query,
        grad_w_key,
        grad_w_value,
        grad_w_out,
        grad_scale_attn,
        grad_norm2_gain,
        grad_norm2_shift,
        grad_w_up,
        grad_w_down,
        grad_scale_mlp,
    )
    return (result.astype(jnp.bfloat16), d_frames.astype(jnp.bfloat16), grads)


def permute(values, flip):
    count = lax.axis_size("dev")
    return lax.ppermute(values, "dev", [(at, at ^ flip) for at in range(count)])


def pick(bit, first, second):
    return jnp.where(bit == 0, first, second)


def pair_gather(values, flip, axis):
    bit = lax.axis_index("dev") & flip
    other = permute(values, flip)
    return jnp.stack((pick(bit, values, other), pick(bit, other, values)), axis=axis)


def gather_all(shard):
    count = lax.axis_size("dev")
    planes = count // 8
    me = lax.axis_index("dev")
    blocks = jnp.stack([shard] + [permute(shard, 8 * k) for k in range(1, planes)])
    step = 1
    while step < planes:
        split = blocks.reshape((planes // (2 * step), 2, step) + shard.shape)
        blocks = pick(me & (8 * step), split, split[:, ::-1]).reshape(blocks.shape)
        step *= 2
    half = shard.shape[0] // 32 * 16
    first = pair_gather(blocks[:, :half], 2, 1)
    second = pair_gather(blocks[:, half:], 4, 1)
    first = pair_gather(first, 4, 1)
    second = pair_gather(second, 2, 2)
    whole = jnp.concatenate((first, second), axis=3)
    whole = pair_gather(whole, 1, 3)
    return whole.reshape((count,) + shard.shape)


def pair_sum(values, flip, axis):
    bit = lax.axis_index("dev") & flip
    lower = lax.index_in_dim(values, 0, axis, keepdims=False)
    upper = lax.index_in_dim(values, 1, axis, keepdims=False)
    arrived = permute(pick(bit, upper, lower).astype(jnp.bfloat16), flip)
    return pick(bit, lower, upper) + arrived.astype(jnp.float32)


def scatter_sum(blocks):
    count, rows, width = blocks.shape
    planes = count // 8
    me = lax.axis_index("dev")
    values = pair_sum(blocks.reshape(planes, 2, 2, 2, rows, width), 1, 3)
    half = rows // 32 * 16
    first = pair_sum(values[:, :, :, :half], 2, 2)
    second = pair_sum(values[:, :, :, half:], 4, 1)
    first = pair_sum(first, 4, 1)
    second = pair_sum(second, 2, 1)
    values = jnp.concatenate((first, second), axis=1)
    plane = me // 8
    total = lax.dynamic_index_in_dim(values, plane, 0, keepdims=False)
    low = values.astype(jnp.bfloat16)
    for k in range(1, planes):
        sent = lax.dynamic_index_in_dim(low, plane ^ k, 0, keepdims=False)
        total = total + permute(sent, 8 * k).astype(jnp.float32)
    return total


def columns_apart(matrix):
    return jnp.concatenate([matrix[:, 512 * k : 512 * k + 512] for k in range(4)], axis=0)


def local(
    frames,
    norm1_gain,
    norm1_shift,
    kernel_query,
    kernel_key,
    kernel_value,
    w_query,
    w_key,
    w_value,
    w_out,
    scale_attn,
    norm2_gain,
    norm2_shift,
    w_up,
    w_down,
    scale_mlp,
    cotangent,
):
    count = lax.axis_size("dev")
    own = frames.shape[0]
    channels = own * count
    columns = frames.shape[1] // count
    scalars = (norm1_gain, norm1_shift, scale_attn, norm2_gain, norm2_shift, scale_mlp)
    small = jnp.concatenate(
        [one[:, None] for one in scalars] + [kernel_query, kernel_key, kernel_value], axis=1
    )
    small = jnp.pad(small, ((0, 0), (0, 512 - small.shape[1])))

    def to_crops(values):
        split = values.reshape(own, count, columns).transpose(1, 0, 2)
        return lax.all_to_all(split, "dev", 0, 0).reshape(channels, -1, LENGTH)

    def to_channels(values):
        split = values.reshape(count, own, columns)
        return lax.all_to_all(split, "dev", 0, 0).transpose(1, 0, 2).reshape(own, -1)

    attn_all = gather_all(jnp.concatenate((w_query, w_key, w_value, w_out, small), axis=0))
    local_x = to_crops(frames)
    mlp_all = gather_all(jnp.concatenate((columns_apart(w_up), w_down), axis=0))
    local_c = to_crops(cotangent)

    def part(blocks, at, rows):
        return blocks[:, at * own : at * own + rows].reshape(count * rows, 512)

    full_query, full_key, full_value, full_out = (part(attn_all, k, own) for k in range(4))
    full_small = part(attn_all, 4, own)
    full_up = jnp.concatenate([part(mlp_all, k, own) for k in range(4)], axis=1)
    full_down = mlp_all[:, 4 * own :].reshape(-1, 512)
    params = (
        full_small[:, 0],
        full_small[:, 1],
        full_small[:, 6:9],
        full_small[:, 9:12],
        full_small[:, 12:15],
        full_query,
        full_key,
        full_value,
        full_out,
        full_small[:, 2],
        full_small[:, 3],
        full_small[:, 4],
        full_up,
        full_down,
        full_small[:, 5],
    )
    result, d_frames, grads = local_step(params, local_x, local_c)
    output = to_channels(result)
    frames_grad = to_channels(d_frames)
    mlp_grads = jnp.concatenate(
        [grads[12][:, 512 * k : 512 * k + 512].reshape(count, own, 512) for k in range(4)]
        + [grads[13].reshape(count, -1, 512)],
        axis=1,
    )
    small_grads = jnp.concatenate(
        [grads[k][:, None] for k in (0, 1, 9, 10, 11, 14)] + [grads[k] for k in (2, 3, 4)], axis=1
    )
    small_grads = jnp.pad(small_grads, ((0, 0), (0, 512 - small_grads.shape[1])))
    attn_grads = jnp.concatenate(
        [grads[k].reshape(count, own, 512) for k in (5, 6, 7, 8)]
        + [small_grads.reshape(count, own, 512)],
        axis=1,
    )
    mlp_sum = scatter_sum(mlp_grads)
    attn_sum = scatter_sum(attn_grads)
    small_sum = attn_sum[4 * own :]
    return (
        output,
        frames_grad,
        small_sum[:, 0],
        small_sum[:, 1],
        small_sum[:, 6:9],
        small_sum[:, 9:12],
        small_sum[:, 12:15],
        attn_sum[:own],
        attn_sum[own : 2 * own],
        attn_sum[2 * own : 3 * own],
        attn_sum[3 * own : 4 * own],
        small_sum[:, 2],
        small_sum[:, 3],
        small_sum[:, 4],
        jnp.concatenate([mlp_sum[k * own : k * own + own] for k in range(4)], axis=1),
        mlp_sum[4 * own :],
        small_sum[:, 5],
    )


def solution(mesh):
    in_specs = (
        P("dev", None),
        P("dev"),
        P("dev"),
        P("dev", None),
        P("dev", None),
        P("dev", None),
        P("dev", None),
        P("dev", None),
        P("dev", None),
        P("dev", None),
        P("dev"),
        P("dev"),
        P("dev"),
        P("dev", None),
        P("dev", None),
        P("dev"),
        P("dev", None),
    )
    out_specs = (
        P("dev", None),
        P("dev", None),
        P("dev"),
        P("dev"),
        P("dev", None),
        P("dev", None),
        P("dev", None),
        P("dev", None),
        P("dev", None),
        P("dev", None),
        P("dev", None),
        P("dev"),
        P("dev"),
        P("dev"),
        P("dev", None),
        P("dev", None),
        P("dev"),
    )
    return jax.shard_map(local, mesh=mesh, in_specs=in_specs, out_specs=out_specs, check_vma=False)
```

```python
import math

import jax
import jax.numpy as jnp
from jax import lax
from jax.experimental import pallas as pl
from jax.experimental.pallas import tpu as pltpu
from jax.sharding import PartitionSpec as P

HEADS = 4
HEAD_DIM = 128
LENGTH = 160
WINDOW = 19
WIDTH = 512
HIDDEN = 2048
FACTOR = HEAD_DIM ** (-0.5)
EPSILON = 1e-05
ROWS = 16
BLOCKS = WIDTH // ROWS
CHUNKS = HIDDEN // WIDTH
LOW = jnp.bfloat16
FULL = jnp.float32

VMEM = pl.BlockSpec(memory_space=pltpu.VMEM)
ANY = pl.BlockSpec(memory_space=pl.ANY)
SMEM = pl.BlockSpec(memory_space=pltpu.SMEM)

GAIN1, SHIFT1, SCALE_ATTN, GAIN2, SHIFT2, SCALE_MLP, KERNEL_Q, KERNEL_K, KERNEL_V = (
    0, 1, 2, 3, 4, 5, 6, 9, 12,
)


def nn(left, right):
    return jnp.dot(left, right, preferred_element_type=FULL)


def nt(left, right):
    return lax.dot_general(left, right, (((1,), (1,)), ((), ())), preferred_element_type=FULL)


def tn(left, right):
    return lax.dot_general(left, right, (((0,), (0,)), ((), ())), preferred_element_type=FULL)


def place(block, me):
    far = block ^ me
    x, y, z = (far >> 1) & 1, (far >> 2) & 1, far >> 3
    return far & 1, 8 * y + 4 * x + z, 8 * x + 4 * y + z


def block_rows(block, rows=ROWS):
    return pl.ds(pl.multiple_of(block * rows, rows), rows)


def whole_wait(ref, sem):
    pltpu.make_async_copy(ref, ref, sem).wait()


def down_one(values):
    at = lax.broadcasted_iota(jnp.int32, values.shape, 0)
    return jnp.where(at == 0, 0.0, pltpu.roll(values, 1, 0))


def up_one(values):
    at = lax.broadcasted_iota(jnp.int32, values.shape, 0)
    last = values.shape[0] - 1
    return jnp.where(at == last, 0.0, pltpu.roll(values, last, 0))


def normalise(values):
    center = jnp.mean(values, axis=1, keepdims=True)
    centered = values - center
    scale = lax.rsqrt(jnp.mean(centered * centered, axis=1, keepdims=True) + EPSILON)
    return centered * scale, scale


def row(table, index):
    return table[index : index + 1, :]


def front_kernel(
    me_ref, x_ref, own1, far1, own2, far2,
    table, n1, scale1, conv, qkv, probs, heads, attn, resid, n2, scale2, normed2,
    weights, x_rows, sems,
):
    me = me_ref[0]
    tokens = x_ref.shape[1]
    crops = tokens // LENGTH

    def fetch(block, carry):
        core, first, second = place(block, me)
        for side, (one, two) in enumerate(((own1, own2), (far1, far2))):
            @pl.when(core == side)
            def _(one=one, two=two):
                rows = block_rows(block)
                pltpu.make_async_copy(one.at[first], weights.at[0:3, rows], sems.at[0]).start()
                pltpu.make_async_copy(two.at[second], weights.at[3:5, rows], sems.at[1]).start()
        return carry

    lax.fori_loop(0, BLOCKS, fetch, 0)
    for at in range(0, tokens, 128):
        x_rows[at : at + 128, :] = x_ref[:, at : at + 128].T.astype(FULL)
    whole_wait(weights.at[0:3], sems.at[0])
    table[...] = weights[2, :, 0:128].astype(FULL).T[0:16, :]

    def norm_one(at, carry):
        rows = pl.ds(pl.multiple_of(at * 80, 80), 80)
        n1[rows, :], scale1[rows, :] = normalise(x_rows[rows, :])
        return carry

    lax.fori_loop(0, tokens // 80, norm_one, 0)

    def convolve(crop, carry):
        rows = pl.ds(pl.multiple_of(crop * LENGTH, LENGTH), LENGTH)
        for at in range(0, WIDTH, 128):
            lanes = slice(at, at + 128)
            normed = n1[rows, lanes] * table[GAIN1 : GAIN1 + 1, lanes] + table[SHIFT1 : SHIFT1 + 1, lanes]
            before, after = down_one(normed), up_one(normed)
            for k, start in enumerate((KERNEL_Q, KERNEL_K, KERNEL_V)):
                conv[k, rows, lanes] = (
                    table[start : start + 1, lanes] * before
                    + table[start + 1 : start + 2, lanes] * normed
                    + table[start + 2 : start + 3, lanes] * after
                ).astype(LOW)
        return carry

    lax.fori_loop(0, crops, convolve, 0)
    whole_wait(weights.at[3:5], sems.at[1])
    for k, w in enumerate((0, 1, 3)):
        qkv[k] = nn(conv[k], weights[w]).astype(LOW)

    near_t = lax.broadcasted_iota(jnp.int32, (LENGTH, LENGTH), 0)
    near_u = lax.broadcasted_iota(jnp.int32, (LENGTH, LENGTH), 1)
    nearby = jnp.abs(near_t - near_u) <= WINDOW // 2

    def attend(crop, carry):
        rows = pl.ds(pl.multiple_of(crop * LENGTH, LENGTH), LENGTH)
        for h in range(HEADS):
            lanes = slice(h * HEAD_DIM, (h + 1) * HEAD_DIM)
            scores = jnp.where(nearby, nt(qkv[0, rows, lanes], qkv[1, rows, lanes]) * FACTOR, -1e30)
            powers = jnp.exp(scores - jnp.max(scores, axis=1, keepdims=True))
            shares = powers / jnp.sum(powers, axis=1, keepdims=True)
            probs[crop, h] = shares
            heads[rows, lanes] = nn(shares.astype(LOW), qkv[2, rows, lanes]).astype(LOW)
        return carry

    lax.fori_loop(0, crops, attend, 0)
    attn[...] = nn(heads[...], weights[4])

    def norm_two(at, carry):
        rows = pl.ds(pl.multiple_of(at * 80, 80), 80)
        mixed = x_rows[rows, :] + row(table, SCALE_ATTN) * attn[rows, :]
        resid[rows, :] = mixed
        normal, scale = normalise(mixed)
        n2[rows, :], scale2[rows, :] = normal, scale
        normed2[rows, :] = (normal * row(table, GAIN2) + row(table, SHIFT2)).astype(LOW)
        return carry

    lax.fori_loop(0, tokens // 80, norm_two, 0)


def shape(*dims, kind=FULL):
    return jax.ShapeDtypeStruct(dims, kind)


def front(me, x, own1, far1, own2, far2):
    tokens = x.shape[1]
    crops = tokens // LENGTH
    return pl.pallas_call(
        front_kernel,
        in_specs=[SMEM, VMEM, ANY, ANY, ANY, ANY],
        out_specs=[VMEM] * 12,
        out_shape=[
            shape(16, WIDTH),
            shape(tokens, WIDTH),
            shape(tokens, 1),
            shape(3, tokens, WIDTH, kind=LOW),
            shape(3, tokens, WIDTH, kind=LOW),
            shape(crops, HEADS, LENGTH, LENGTH),
            shape(tokens, WIDTH, kind=LOW),
            shape(tokens, WIDTH),
            shape(tokens, WIDTH),
            shape(tokens, WIDTH),
            shape(tokens, 1),
            shape(tokens, WIDTH, kind=LOW),
        ],
        scratch_shapes=[
            pltpu.VMEM((5, WIDTH, WIDTH), LOW),
            pltpu.VMEM((tokens, WIDTH), FULL),
            pltpu.SemaphoreType.DMA((2,)),
        ],
        compiler_params=pltpu.CompilerParams(vmem_limit_bytes=24 << 20),
        cost_estimate=pl.CostEstimate(flops=8 * tokens * WIDTH * WIDTH, bytes_accessed=16 << 20, transcendentals=0),
        name="front",
    )(me, x, own1, far1, own2, far2)


ERF_P = 0.3275911
ERF_A = (0.254829592, -0.284496736, 1.421413741, -1.453152027, 1.061405429)


def gelu_both(values):
    size = jnp.abs(values)
    near = 1.0 / (1.0 + (ERF_P * math.sqrt(0.5)) * size)
    bell = jnp.exp(-0.5 * values * values)
    series = ERF_A[4]
    for coefficient in ERF_A[3::-1]:
        series = series * near + coefficient
    tail = (0.5 * series) * near * bell
    below = jnp.where(values < 0, tail, 1.0 - tail)
    return values * below, below + values * bell * (0.5 * math.sqrt(2 / math.pi))


def mlp_kernel(
    me_ref, cot_ref, normed2, resid, table, own_up, far_up, own_down, far_down,
    out, cot_rows, d_normed2, grad_scale, keep_up, keep_down, send,
    up, down, normed2_t, d_branch, branch, active, slope, d_hidden, grads, sems, out_sems,
):
    me = me_ref[0]
    tokens = cot_ref.shape[1]

    def fetch(block, carry):
        core, first, second = place(block, me)
        for side, (one, two) in enumerate(((own_up, own_down), (far_up, far_down))):
            @pl.when(core == side)
            def _(one=one, two=two):
                pltpu.make_async_copy(one.at[first], up.at[:, block_rows(block)], sems.at[0]).start()
                pltpu.make_async_copy(
                    two.at[second], down.at[block_rows(block, ROWS * CHUNKS)], sems.at[1]
                ).start()
        return carry

    lax.fori_loop(0, BLOCKS, fetch, 0)
    for at in range(0, tokens, 128):
        cot_rows[at : at + 128, :] = cot_ref[:, at : at + 128].T
        normed2_t[:, at : at + 128] = normed2[at : at + 128, :].T
    scale_mlp = row(table, SCALE_MLP)
    d_branch[...] = (scale_mlp * cot_rows[...].astype(FULL)).astype(LOW)
    whole_wait(up, sems.at[0])
    whole_wait(down, sems.at[1])

    def store(chunk):
        def up_one(block, carry):
            core, first, _ = place(block, me)
            piece = grads.at[0, block_rows(block)]
            rows = block_rows(chunk)
            @pl.when(core == 0)
            def _():
                pltpu.make_async_copy(piece, keep_up.at[first, rows], out_sems.at[0]).start()
            @pl.when(core == 1)
            def _():
                pltpu.make_async_copy(piece, send.at[0, first, rows], out_sems.at[0]).start()
            return carry

        lax.fori_loop(0, BLOCKS, up_one, 0)

        def down_one(at, carry):
            core, _, second = place(chunk * (BLOCKS // CHUNKS) + at, me)
            piece = grads.at[1, block_rows(at, ROWS * CHUNKS)]
            @pl.when(core == 0)
            def _():
                pltpu.make_async_copy(piece, keep_down.at[second], out_sems.at[0]).start()
            @pl.when(core == 1)
            def _():
                pltpu.make_async_copy(piece, send.at[1, second], out_sems.at[0]).start()
            return carry

        lax.fori_loop(0, BLOCKS // CHUNKS, down_one, 0)

    def chunk_step(chunk, carry):
        rows = pl.ds(pl.multiple_of(chunk * WIDTH, WIDTH), WIDTH)
        hidden = nn(normed2[...], up[chunk])
        value, slope[...] = gelu_both(hidden)
        active[...] = value.astype(LOW)
        d_active = nt(d_branch[...], down[rows, :])
        d_hidden[...] = (d_active * slope[...]).astype(LOW)
        added = nn(active[...], down[rows, :])
        back = nt(d_hidden[...], up[chunk])

        @pl.when(chunk == 0)
        def _():
            branch[...] = added
            d_normed2[...] = back

        @pl.when(chunk > 0)
        def _():
            branch[...] += added
            d_normed2[...] += back
            whole_wait(grads, out_sems.at[0])

        grads[0] = nn(normed2_t[...], d_hidden[...]).astype(LOW)
        grads[1] = tn(active[...], d_branch[...]).astype(LOW)
        store(chunk)
        return carry

    lax.fori_loop(0, CHUNKS, chunk_step, 0)
    grad_scale[...] = jnp.sum(cot_rows[...].astype(FULL) * branch[...], axis=0, keepdims=True)
    for at in range(0, tokens, 128):
        rows = slice(at, at + 128)
        out[:, rows] = (resid[rows, :] + scale_mlp * branch[rows, :]).astype(LOW).T
    whole_wait(grads, out_sems.at[0])


def mlp(me, cot, normed2, resid, table, own_up, far_up, own_down, far_down):
    tokens = cot.shape[1]
    half = BLOCKS // 2
    return pl.pallas_call(
        mlp_kernel,
        in_specs=[SMEM, VMEM, VMEM, VMEM, VMEM, ANY, ANY, ANY, ANY],
        out_specs=[VMEM] * 4 + [ANY] * 3,
        out_shape=[
            shape(WIDTH, tokens, kind=LOW),
            shape(tokens, WIDTH, kind=LOW),
            shape(tokens, WIDTH),
            shape(1, WIDTH),
            shape(half, ROWS * CHUNKS, WIDTH, kind=LOW),
            shape(half, ROWS * CHUNKS, WIDTH, kind=LOW),
            shape(2, half, ROWS * CHUNKS, WIDTH, kind=LOW),
        ],
        scratch_shapes=[
            pltpu.VMEM((CHUNKS, WIDTH, WIDTH), LOW),
            pltpu.VMEM((HIDDEN, WIDTH), LOW),
            pltpu.VMEM((WIDTH, tokens), LOW),
            pltpu.VMEM((tokens, WIDTH), LOW),
            pltpu.VMEM((tokens, WIDTH), FULL),
            pltpu.VMEM((tokens, WIDTH), LOW),
            pltpu.VMEM((tokens, WIDTH), FULL),
            pltpu.VMEM((tokens, WIDTH), LOW),
            pltpu.VMEM((2, WIDTH, WIDTH), LOW),
            pltpu.SemaphoreType.DMA((2,)),
            pltpu.SemaphoreType.DMA((1,)),
        ],
        compiler_params=pltpu.CompilerParams(vmem_limit_bytes=32 << 20),
        cost_estimate=pl.CostEstimate(flops=12 * tokens * WIDTH * HIDDEN, bytes_accessed=16 << 20, transcendentals=0),
        name="mlp",
    )(me, cot, normed2, resid, table, own_up, far_up, own_down, far_down)


def attend_back_kernel(
    me_ref, table, cot_rows, d_normed2, n2, scale2, attn, heads, qkv, probs, own2, far2,
    d_resid, d_qkv, grad_out, small,
    w_out, d_attn, d_heads, sems,
):
    me = me_ref[0]
    tokens = attn.shape[0]
    crops = tokens // LENGTH

    def fetch(block, carry):
        core, _, second = place(block, me)
        for side, two in enumerate((own2, far2)):
            @pl.when(core == side)
            def _(two=two):
                pltpu.make_async_copy(two.at[second, 1], w_out.at[block_rows(block)], sems.at[0]).start()
        return carry

    lax.fori_loop(0, BLOCKS, fetch, 0)

    def norm_back(at, sums):
        rows = pl.ds(pl.multiple_of(at * 80, 80), 80)
        grad, normal = d_normed2[rows, :], n2[rows, :]
        s = row(table, GAIN2) * grad
        along = jnp.mean(s * normal, axis=1, keepdims=True)
        middle = jnp.mean(s, axis=1, keepdims=True)
        total = cot_rows[rows, :].astype(FULL) + (s - middle - normal * along) * scale2[rows, :]
        d_resid[rows, :] = total
        d_attn[rows, :] = (row(table, SCALE_ATTN) * total).astype(LOW)
        return tuple(
            one + jnp.sum(more, axis=0, keepdims=True)
            for one, more in zip(sums, (grad * normal, grad, total * attn[rows, :]))
        )

    zero = jnp.zeros((1, WIDTH), FULL)
    gain, shift, scale = lax.fori_loop(0, tokens // 80, norm_back, (zero, zero, zero))
    small[0:1, :], small[1:2, :], small[2:3, :] = gain, shift, scale
    grad_out[...] = tn(heads[...], d_attn[...]).astype(LOW)
    whole_wait(w_out, sems.at[0])
    d_heads[...] = nt(d_attn[...], w_out[...]).astype(LOW)

    def attend(crop, carry):
        rows = pl.ds(pl.multiple_of(crop * LENGTH, LENGTH), LENGTH)
        for h in range(HEADS):
            lanes = slice(h * HEAD_DIM, (h + 1) * HEAD_DIM)
            shares, grad = probs[crop, h], d_heads[rows, lanes]
            d_probs = nt(grad, qkv[2, rows, lanes])
            d_qkv[2, rows, lanes] = tn(shares.astype(LOW), grad).astype(LOW)
            d_scores = shares * (d_probs - jnp.sum(shares * d_probs, axis=1, keepdims=True))
            d_scores = d_scores.astype(LOW)
            d_qkv[0, rows, lanes] = (nn(d_scores, qkv[1, rows, lanes]) * FACTOR).astype(LOW)
            d_qkv[1, rows, lanes] = (tn(d_scores, qkv[0, rows, lanes]) * FACTOR).astype(LOW)
        return carry

    lax.fori_loop(0, crops, attend, 0)


def attend_back(me, table, cot_rows, d_normed2, n2, scale2, attn, heads, qkv, probs, own2, far2):
    tokens = attn.shape[0]
    return pl.pallas_call(
        attend_back_kernel,
        in_specs=[SMEM] + [VMEM] * 9 + [ANY] * 2,
        out_specs=[VMEM] * 4,
        out_shape=[
            shape(tokens, WIDTH),
            shape(3, tokens, WIDTH, kind=LOW),
            shape(WIDTH, WIDTH, kind=LOW),
            shape(8, WIDTH),
        ],
        scratch_shapes=[
            pltpu.VMEM((WIDTH, WIDTH), LOW),
            pltpu.VMEM((tokens, WIDTH), LOW),
            pltpu.VMEM((tokens, WIDTH), LOW),
            pltpu.SemaphoreType.DMA((1,)),
        ],
        compiler_params=pltpu.CompilerParams(vmem_limit_bytes=24 << 20),
        cost_estimate=pl.CostEstimate(flops=6 * tokens * WIDTH * WIDTH, bytes_accessed=16 << 20, transcendentals=0),
        name="attend_back",
    )(me, table, cot_rows, d_normed2, n2, scale2, attn, heads, qkv, probs, own2, far2)


def front_back_kernel(
    me_ref, table, d_resid, d_qkv, conv, n1, scale1, grad_out, small, grad_scale,
    own1, far1, own2, far2,
    d_frames, keep1, keep2, send1, send2,
    weights, d_conv, grads, sums, sems, out_sems,
):
    me = me_ref[0]
    tokens = n1.shape[0]
    crops = tokens // LENGTH

    def fetch(block, carry):
        core, first, second = place(block, me)
        rows = block_rows(block)
        for side, (one, two) in enumerate(((own1, own2), (far1, far2))):
            @pl.when(core == side)
            def _(one=one, two=two):
                pltpu.make_async_copy(one.at[first, 0:2], weights.at[0:2, rows], sems.at[0]).start()
                pltpu.make_async_copy(two.at[second, 0], weights.at[2, rows], sems.at[0]).start()
        return carry

    lax.fori_loop(0, BLOCKS, fetch, 0)
    for k, slot in enumerate((0, 1, 3)):
        grads[slot] = tn(conv[k], d_qkv[k]).astype(LOW)
    grads[4] = grad_out[...]
    whole_wait(weights, sems.at[0])
    for k in range(3):
        d_conv[k] = nt(d_qkv[k], weights[k])

    sums[...] = jnp.zeros_like(sums)

    def back(crop, carry):
        rows = pl.ds(pl.multiple_of(crop * LENGTH, LENGTH), LENGTH)
        middle = jnp.zeros((LENGTH, 1), FULL)
        along = jnp.zeros((LENGTH, 1), FULL)
        pieces = []
        for at in range(0, WIDTH, 128):
            lanes = slice(at, at + 128)
            gain = table[GAIN1 : GAIN1 + 1, lanes]
            normal = n1[rows, lanes]
            normed = normal * gain + table[SHIFT1 : SHIFT1 + 1, lanes]
            before, after = down_one(normed), up_one(normed)
            parts = [0.0, 0.0, 0.0]
            for k, start in enumerate((KERNEL_Q, KERNEL_K, KERNEL_V)):
                grad = d_conv[k, rows, lanes]
                for j, seen in enumerate((before, normed, after)):
                    sums[start + j : start + j + 1, lanes] += jnp.sum(grad * seen, axis=0, keepdims=True)
                    parts[j] = parts[j] + table[start + j : start + j + 1, lanes] * grad
            total = up_one(parts[0]) + parts[1] + down_one(parts[2])
            sums[GAIN1 : GAIN1 + 1, lanes] += jnp.sum(total * normal, axis=0, keepdims=True)
            sums[SHIFT1 : SHIFT1 + 1, lanes] += jnp.sum(total, axis=0, keepdims=True)
            s = gain * total
            d_conv[0, rows, lanes] = s
            middle += jnp.sum(s, axis=1, keepdims=True)
            along += jnp.sum(s * normal, axis=1, keepdims=True)
        middle, along = middle / WIDTH, along / WIDTH
        for at in range(0, WIDTH, 128):
            lanes = slice(at, at + 128)
            d_conv[1, rows, lanes] = d_resid[rows, lanes] + (
                d_conv[0, rows, lanes] - middle - n1[rows, lanes] * along
            ) * scale1[rows, :]
        return carry

    lax.fori_loop(0, crops, back, 0)
    for at in range(0, tokens, 128):
        d_frames[:, at : at + 128] = d_conv[1, at : at + 128, :].astype(LOW).T
    sums[GAIN2 : SHIFT2 + 1, :] = small[0:2, :]
    sums[SCALE_ATTN : SCALE_ATTN + 1, :] = small[2:3, :]
    sums[SCALE_MLP : SCALE_MLP + 1, :] = grad_scale[...]
    grads[2] = jnp.zeros((WIDTH, WIDTH), LOW)
    grads[2, :, 0:128] = sums[...].T.astype(LOW)

    def store(block, carry):
        core, first, second = place(block, me)
        rows = block_rows(block)
        for side, (one, two) in enumerate(((keep1, keep2), (send1, send2))):
            @pl.when(core == side)
            def _(one=one, two=two):
                pltpu.make_async_copy(grads.at[0:3, rows], one.at[first], out_sems.at[0]).start()
                pltpu.make_async_copy(grads.at[3:5, rows], two.at[second], out_sems.at[0]).start()
        return carry

    lax.fori_loop(0, BLOCKS, store, 0)
    whole_wait(grads, out_sems.at[0])


def front_back(me, table, d_resid, d_qkv, conv, n1, scale1, grad_out, small, grad_scale, own1, far1, own2, far2):
    tokens = n1.shape[0]
    half = BLOCKS // 2
    return pl.pallas_call(
        front_back_kernel,
        in_specs=[SMEM] + [VMEM] * 9 + [ANY] * 4,
        out_specs=[VMEM] + [ANY] * 4,
        out_shape=[
            shape(WIDTH, tokens, kind=LOW),
            shape(half, 3, ROWS, WIDTH, kind=LOW),
            shape(half, 2, ROWS, WIDTH, kind=LOW),
            shape(half, 3, ROWS, WIDTH, kind=LOW),
            shape(half, 2, ROWS, WIDTH, kind=LOW),
        ],
        scratch_shapes=[
            pltpu.VMEM((3, WIDTH, WIDTH), LOW),
            pltpu.VMEM((3, tokens, WIDTH), FULL),
            pltpu.VMEM((5, WIDTH, WIDTH), LOW),
            pltpu.VMEM((128, WIDTH), FULL),
            pltpu.SemaphoreType.DMA((1,)),
            pltpu.SemaphoreType.DMA((1,)),
        ],
        compiler_params=pltpu.CompilerParams(vmem_limit_bytes=24 << 20),
        cost_estimate=pl.CostEstimate(flops=12 * tokens * WIDTH * WIDTH, bytes_accessed=16 << 20, transcendentals=0),
        name="front_back",
    )(me, table, d_resid, d_qkv, conv, n1, scale1, grad_out, small, grad_scale, own1, far1, own2, far2)


def pack_kernel(
    gain1, shift1, scale_attn, gain2, shift2, scale_mlp, kernel_q, kernel_k, kernel_v,
    w_query, w_key, w_value, w_out, w_up, w_down,
    attn_shard, mlp_shard, table,
):
    table[...] = jnp.zeros_like(table)
    for at, one in enumerate((gain1, shift1, scale_attn, gain2, shift2, scale_mlp)):
        table[at : at + 1, 0:ROWS] = one[...].astype(FULL)
    for at, one in ((KERNEL_Q, kernel_q), (KERNEL_K, kernel_k), (KERNEL_V, kernel_v)):
        table[at : at + 3, 0:ROWS] = one[...].astype(FULL)
    attn_shard[2] = jnp.zeros((ROWS, WIDTH), LOW)
    attn_shard[2, :, 0:128] = table[...].T[0:ROWS, :].astype(LOW)
    for at, one in ((0, w_query), (1, w_key), (3, w_value), (4, w_out)):
        attn_shard[at] = one[...]
    for chunk in range(CHUNKS):
        mlp_shard[chunk] = w_up[:, chunk * WIDTH : (chunk + 1) * WIDTH]
        mlp_shard[CHUNKS + chunk] = w_down[chunk * ROWS : (chunk + 1) * ROWS, :]


def pack(vectors, kernels, matrices):
    return pl.pallas_call(
        pack_kernel,
        in_specs=[VMEM] * 15,
        out_specs=[VMEM] * 2,
        out_shape=[
            shape(5, ROWS, WIDTH, kind=LOW),
            shape(2 * CHUNKS, ROWS, WIDTH, kind=LOW),
        ],
        scratch_shapes=[pltpu.VMEM((128, 128), FULL)],
        name="pack",
    )(*[one.reshape(1, -1) for one in vectors], *[one.T for one in kernels], *matrices)


def permute(values, flip):
    count = lax.axis_size("dev")
    return lax.ppermute(values, "dev", [(at, at ^ flip) for at in range(count)])


def gather_half(blocks, flips):
    for flip in flips:
        blocks = jnp.stack((blocks, permute(blocks, flip)))
    own = blocks.reshape((BLOCKS // 2,) + blocks.shape[3:])
    return own, permute(own, 1)


def gather(shard, cut):
    planes = [shard] + [permute(shard, 8 * k) for k in range(1, 4)]
    first = jnp.stack([one[:cut] for one in planes])
    second = jnp.stack([one[cut:] for one in planes])
    return gather_half(first, (2, 4)) + gather_half(second, (4, 2))


def added(kept, arrived):
    return kept.astype(FULL) + arrived.astype(FULL)


def scatter_half(kept, arrived, flips):
    total = added(kept, arrived)
    for flip in flips:
        half = total.shape[0] // 2
        total = added(total[:half], permute(total[half:].astype(LOW), flip))
    own = total[0]
    for k in range(1, 4):
        own = own + permute(total[k].astype(LOW), 8 * k).astype(FULL)
    return own


def gather_plain(pieces):
    whole = [lax.all_gather(one, "dev", axis=0, tiled=True) for one in pieces]
    return jnp.stack([one.reshape(BLOCKS, ROWS, WIDTH) for one in whole], axis=1)


def apart(blocks, order):
    split = blocks.reshape((4, 2, 2, 2) + blocks.shape[1:])
    split = split.transpose(order + tuple(range(4, split.ndim)))
    return split.reshape((2, BLOCKS // 2) + blocks.shape[1:])


def together(kept, sent, order):
    split = jnp.stack((kept, sent)).reshape((2, 2, 2, 4) + kept.shape[1:])
    back = tuple(order.index(axis) for axis in range(4))
    split = split.transpose(back + tuple(range(4, split.ndim)))
    return split.reshape((BLOCKS,) + kept.shape[1:])


FIRST, SECOND = (3, 1, 2, 0), (3, 2, 1, 0)


def scatter_plain(matrix):
    return lax.psum_scatter(matrix.astype(FULL), "dev", scatter_dimension=0, tiled=True)


def compute(me, x, cot, attn_weights, mlp_weights):
    own1, far1, own2, far2 = attn_weights
    table, n1, scale1, conv, qkv, probs, heads, attn, resid, n2, scale2, normed2 = front(
        me, x, own1, far1, own2, far2
    )
    out, cot_rows, d_normed2, grad_scale, keep_up, keep_down, send = mlp(
        me, cot, normed2, resid, table, *mlp_weights
    )
    d_resid, d_qkv, grad_out, small = attend_back(
        me, table, cot_rows, d_normed2, n2, scale2, attn, heads, qkv, probs, own2, far2
    )
    d_frames, keep1, keep2, send1, send2 = front_back(
        me, table, d_resid, d_qkv, conv, n1, scale1, grad_out, small, grad_scale,
        own1, far1, own2, far2,
    )
    return out, d_frames, (keep_up, keep_down, send), (keep1, keep2, send1, send2)


def local(
    frames,
    norm1_gain,
    norm1_shift,
    kernel_query,
    kernel_key,
    kernel_value,
    w_query,
    w_key,
    w_value,
    w_out,
    scale_attn,
    norm2_gain,
    norm2_shift,
    w_up,
    w_down,
    scale_mlp,
    cotangent,
):
    count = lax.axis_size("dev")
    own, columns = frames.shape[0], frames.shape[1] // count
    fast = own == ROWS and own * count == WIDTH
    vectors = (norm1_gain, norm1_shift, scale_attn, norm2_gain, norm2_shift, scale_mlp)
    kernels = (kernel_query, kernel_key, kernel_value)

    def to_crops(values):
        split = values.reshape(own, count, columns).transpose(1, 0, 2)
        return lax.all_to_all(split, "dev", 0, 0).reshape(WIDTH, columns)

    def to_channels(values):
        split = values.reshape(count, own, columns)
        return lax.all_to_all(split, "dev", 0, 0).transpose(1, 0, 2).reshape(own, -1)

    x = to_crops(frames)
    if fast:
        me = lax.axis_index("dev").astype(jnp.int32).reshape(1)
        attn_shard, mlp_shard = pack(
            vectors, kernels, (w_query, w_key, w_value, w_out, w_up, w_down)
        )
        attn_weights = gather(attn_shard, 3)
        own_up, far_up, own_down, far_down = gather(mlp_shard, CHUNKS)
    else:
        me = jnp.zeros((1,), jnp.int32)
        small = jnp.concatenate([one[:, None] for one in vectors] + list(kernels), axis=1)
        small = jnp.pad(small, ((0, 0), (0, WIDTH - small.shape[1])))
        attn_weights = tuple(apart(gather_plain((w_query, w_key, small)), FIRST)) + tuple(
            apart(gather_plain((w_value, w_out)), SECOND)
        )
        parts = [w_up[:, k * WIDTH : (k + 1) * WIDTH] for k in range(CHUNKS)]
        own_up, far_up = apart(gather_plain(parts), FIRST)
        whole = lax.all_gather(w_down, "dev", axis=0, tiled=True)
        own_down, far_down = apart(whole.reshape(BLOCKS, CHUNKS, ROWS, WIDTH), SECOND)
    cot = to_crops(cotangent)
    flat = (BLOCKS // 2, CHUNKS * ROWS, WIDTH)
    mlp_weights = (own_up, far_up, own_down.reshape(flat), far_down.reshape(flat))
    out, d_frames, mlp_grads, attn_grads = compute(me, x, cot, attn_weights, mlp_weights)
    output = to_channels(out)
    frames_grad = to_channels(d_frames)
    keep_up, keep_down, send = mlp_grads
    keep1, keep2, send1, send2 = attn_grads
    if fast:
        arrived = permute(send, 1)
        grad_up = scatter_half(keep_up, arrived[0], (4, 2))
        grad_down = scatter_half(keep_down, arrived[1], (2, 4))
        grad1 = scatter_half(keep1, permute(send1, 1), (4, 2))
        grad2 = scatter_half(keep2, permute(send2, 1), (2, 4))
        grad_up = jnp.concatenate([grad_up[k * ROWS : (k + 1) * ROWS] for k in range(CHUNKS)], axis=1)
        grad_query, grad_key, grad_small = grad1[0], grad1[1], grad1[2]
        grad_value, grad_out = grad2[0], grad2[1]
    else:
        ups = together(keep_up, send[0], FIRST).reshape(BLOCKS, CHUNKS, ROWS, WIDTH)
        grad_up = scatter_plain(ups.transpose(0, 2, 1, 3).reshape(WIDTH, HIDDEN))
        grad_down = scatter_plain(together(keep_down, send[1], SECOND).reshape(HIDDEN, WIDTH))
        firsts, seconds = together(keep1, send1, FIRST), together(keep2, send2, SECOND)
        grad_query, grad_key, grad_small = (
            scatter_plain(firsts[:, k].reshape(WIDTH, WIDTH)) for k in range(3)
        )
        grad_value, grad_out = (
            scatter_plain(seconds[:, k].reshape(WIDTH, WIDTH)) for k in range(2)
        )
    return (
        output,
        frames_grad,
        grad_small[:, GAIN1],
        grad_small[:, SHIFT1],
        grad_small[:, KERNEL_Q : KERNEL_Q + 3],
        grad_small[:, KERNEL_K : KERNEL_K + 3],
        grad_small[:, KERNEL_V : KERNEL_V + 3],
        grad_query,
        grad_key,
        grad_value,
        grad_out,
        grad_small[:, SCALE_ATTN],
        grad_small[:, GAIN2],
        grad_small[:, SHIFT2],
        grad_up,
        grad_down,
        grad_small[:, SCALE_MLP],
    )


def solution(mesh):
    in_specs = (
        P("dev", None),
        P("dev"),
        P("dev"),
        P("dev", None),
        P("dev", None),
        P("dev", None),
        P("dev", None),
        P("dev", None),
        P("dev", None),
        P("dev", None),
        P("dev"),
        P("dev"),
        P("dev"),
        P("dev", None),
        P("dev", None),
        P("dev"),
        P("dev", None),
    )
    out_specs = (
        P("dev", None),
        P("dev", None),
        P("dev"),
        P("dev"),
        P("dev", None),
        P("dev", None),
        P("dev", None),
        P("dev", None),
        P("dev", None),
        P("dev", None),
        P("dev", None),
        P("dev"),
        P("dev"),
        P("dev"),
        P("dev", None),
        P("dev", None),
        P("dev"),
    )
    return jax.shard_map(local, mesh=mesh, in_specs=in_specs, out_specs=out_specs, check_vma=False)
```

```python
import math

import jax
import jax.numpy as jnp
from jax import lax
from jax.experimental import pallas as pl
from jax.experimental.pallas import tpu as pltpu
from jax.sharding import PartitionSpec as P

HEADS = 4
HEAD_DIM = 128
LENGTH = 160
WINDOW = 19
WIDTH = 512
HIDDEN = 2048
FACTOR = HEAD_DIM ** (-0.5)
EPSILON = 1e-05
ROWS = 16
BLOCKS = WIDTH // ROWS
CHUNKS = HIDDEN // WIDTH
LOW = jnp.bfloat16
FULL = jnp.float32

VMEM = pl.BlockSpec(memory_space=pltpu.VMEM)
ANY = pl.BlockSpec(memory_space=pl.ANY)
HBM = pl.BlockSpec(memory_space=pltpu.HBM)
SMEM = pl.BlockSpec(memory_space=pltpu.SMEM)

GAIN1, SHIFT1, SCALE_ATTN, GAIN2, SHIFT2, SCALE_MLP, KERNEL_Q, KERNEL_K, KERNEL_V = (
    0, 1, 2, 3, 4, 5, 6, 9, 12,
)


def nn(left, right):
    return jnp.dot(left, right, preferred_element_type=FULL)


def nt(left, right):
    return lax.dot_general(left, right, (((1,), (1,)), ((), ())), preferred_element_type=FULL)


def tn(left, right):
    return lax.dot_general(left, right, (((0,), (0,)), ((), ())), preferred_element_type=FULL)


def place(block, me):
    far = block ^ me
    x, y, z = (far >> 1) & 1, (far >> 2) & 1, far >> 3
    return far & 1, jnp.where(block & 1 == 0, 8 * y + 4 * x, 8 * x + 4 * y) + z


def block_rows(block, rows=ROWS):
    return pl.ds(pl.multiple_of(block * rows, rows), rows)


def whole_wait(ref, sem):
    pltpu.make_async_copy(ref, ref, sem).wait()


def move(source, target, sem):
    copy = pltpu.make_async_copy(source, target, sem)
    copy.start()
    return copy


def down_one(values):
    at = lax.broadcasted_iota(jnp.int32, values.shape, 0)
    return jnp.where(at == 0, 0.0, pltpu.roll(values, 1, 0))


def up_one(values):
    at = lax.broadcasted_iota(jnp.int32, values.shape, 0)
    last = values.shape[0] - 1
    return jnp.where(at == last, 0.0, pltpu.roll(values, last, 0))


def normalise(values):
    center = jnp.mean(values, axis=1, keepdims=True)
    centered = values - center
    scale = lax.rsqrt(jnp.mean(centered * centered, axis=1, keepdims=True) + EPSILON)
    return centered * scale, scale


def row(table, index):
    return table[index : index + 1, :]


def front_kernel(
    me_ref, x_ref, own, far,
    table_out, n1_out, scale1_out, conv_out, qkv_out, probs_out, heads_out, attn_out, resid_out,
    n2_out, scale2_out, normed2_out,
    weights, x_rows, table, n1, scale1, conv, qkv, probs, heads, attn, resid, n2, scale2, normed2,
    in_sem, sems,
):
    me = me_ref[0]
    tokens = x_ref.shape[1]
    crops = tokens // LENGTH
    copies = []

    def send(source, target):
        copies.append(move(source, target, sems.at[len(copies)]))

    def fetch(block, carry):
        core, at = place(block, me)
        rows = block_rows(block)
        for side, blocks in enumerate((own, far)):
            @pl.when(core == side)
            def _(blocks=blocks):
                pltpu.make_async_copy(blocks.at[at], weights.at[:, rows], in_sem.at[0]).start()
        return carry

    lax.fori_loop(0, BLOCKS, fetch, 0)
    for at in range(0, tokens, 128):
        x_rows[at : at + 128, :] = x_ref[:, at : at + 128].T.astype(FULL)

    def norm_one(at, carry):
        rows = pl.ds(pl.multiple_of(at * 80, 80), 80)
        n1[rows, :], scale1[rows, :] = normalise(x_rows[rows, :])
        return carry

    lax.fori_loop(0, tokens // 80, norm_one, 0)
    send(n1, n1_out)
    send(scale1, scale1_out)
    whole_wait(weights, in_sem.at[0])
    table[...] = weights[4, :, 0:128].astype(FULL).T[0:16, :]
    send(table, table_out)

    def convolve(crop, carry):
        rows = pl.ds(pl.multiple_of(crop * LENGTH, LENGTH), LENGTH)
        for at in range(0, WIDTH, 128):
            lanes = slice(at, at + 128)
            normed = n1[rows, lanes] * table[GAIN1 : GAIN1 + 1, lanes] + table[SHIFT1 : SHIFT1 + 1, lanes]
            before, after = down_one(normed), up_one(normed)
            for k, start in enumerate((KERNEL_Q, KERNEL_K, KERNEL_V)):
                conv[k, rows, lanes] = (
                    table[start : start + 1, lanes] * before
                    + table[start + 1 : start + 2, lanes] * normed
                    + table[start + 2 : start + 3, lanes] * after
                ).astype(LOW)
        return carry

    lax.fori_loop(0, crops, convolve, 0)
    send(conv, conv_out)
    for k in range(3):
        qkv[k] = nn(conv[k], weights[k]).astype(LOW)
    send(qkv, qkv_out)

    near_t = lax.broadcasted_iota(jnp.int32, (LENGTH, LENGTH), 0)
    near_u = lax.broadcasted_iota(jnp.int32, (LENGTH, LENGTH), 1)
    nearby = jnp.abs(near_t - near_u) <= WINDOW // 2

    def attend(crop, carry):
        rows = pl.ds(pl.multiple_of(crop * LENGTH, LENGTH), LENGTH)
        for h in range(HEADS):
            lanes = slice(h * HEAD_DIM, (h + 1) * HEAD_DIM)
            scores = jnp.where(nearby, nt(qkv[0, rows, lanes], qkv[1, rows, lanes]) * FACTOR, -1e30)
            powers = jnp.exp(scores - jnp.max(scores, axis=1, keepdims=True))
            shares = powers / jnp.sum(powers, axis=1, keepdims=True)
            probs[crop, h] = shares
            heads[rows, lanes] = nn(shares.astype(LOW), qkv[2, rows, lanes]).astype(LOW)
        return carry

    lax.fori_loop(0, crops, attend, 0)
    send(probs, probs_out)
    send(heads, heads_out)
    attn[...] = nn(heads[...], weights[3])
    send(attn, attn_out)

    def norm_two(at, carry):
        rows = pl.ds(pl.multiple_of(at * 80, 80), 80)
        mixed = x_rows[rows, :] + row(table, SCALE_ATTN) * attn[rows, :]
        resid[rows, :] = mixed
        normal, scale = normalise(mixed)
        n2[rows, :], scale2[rows, :] = normal, scale
        normed2[rows, :] = (normal * row(table, GAIN2) + row(table, SHIFT2)).astype(LOW)
        return carry

    lax.fori_loop(0, tokens // 80, norm_two, 0)
    send(normed2, normed2_out)
    send(resid, resid_out)
    send(n2, n2_out)
    send(scale2, scale2_out)
    for copy in copies:
        copy.wait()


def front(me, x, own, far):
    tokens = x.shape[1]
    crops = tokens // LENGTH
    shapes = [
        shape(16, WIDTH),
        shape(tokens, WIDTH),
        shape(tokens, 1),
        shape(3, tokens, WIDTH, kind=LOW),
        shape(3, tokens, WIDTH, kind=LOW),
        shape(crops, HEADS, LENGTH, LENGTH),
        shape(tokens, WIDTH, kind=LOW),
        shape(tokens, WIDTH),
        shape(tokens, WIDTH),
        shape(tokens, WIDTH),
        shape(tokens, 1),
        shape(tokens, WIDTH, kind=LOW),
    ]
    return pl.pallas_call(
        front_kernel,
        in_specs=[SMEM, VMEM, ANY, ANY],
        out_specs=[HBM] * 12,
        out_shape=shapes,
        scratch_shapes=[
            pltpu.VMEM((5, WIDTH, WIDTH), LOW),
            pltpu.VMEM((tokens, WIDTH), FULL),
        ]
        + [pltpu.VMEM(one.shape, one.dtype) for one in shapes]
        + [pltpu.SemaphoreType.DMA((1,)), pltpu.SemaphoreType.DMA((12,))],
        compiler_params=pltpu.CompilerParams(vmem_limit_bytes=56 << 20),
        cost_estimate=spent(12),
        name="front",
    )(me, x, own, far)


def spent(microseconds):
    return pl.CostEstimate(flops=int(microseconds * 1.15e9), bytes_accessed=0, transcendentals=0)


def shape(*dims, kind=FULL):
    return jax.ShapeDtypeStruct(dims, kind)


ERF_P = 0.3275911
ERF_A = (0.254829592, -0.284496736, 1.421413741, -1.453152027, 1.061405429)


def gelu_both(values):
    size = jnp.abs(values)
    near = 1.0 / (1.0 + (ERF_P * math.sqrt(0.5)) * size)
    bell = jnp.exp(-0.5 * values * values)
    series = ERF_A[4]
    for coefficient in ERF_A[3::-1]:
        series = series * near + coefficient
    tail = (0.5 * series) * near * bell
    below = jnp.where(values < 0, tail, 1.0 - tail)
    return values * below, below + values * bell * (0.5 * math.sqrt(2 / math.pi))


def mlp_kernel(
    me_ref, cot_ref, normed2, resid_in, table, blocks,
    out, cot_out, d_out, grad_scale, keep, send,
    up, down, normed2_t, d_branch, branch, active, slope, d_hidden, grads, cot_rows, d_normed2,
    resid, sems, out_sems,
):
    me = me_ref[0]
    tokens = cot_ref.shape[1]

    def fetch(block, carry):
        pltpu.make_async_copy(
            blocks.at[block, 0:CHUNKS], up.at[:, block_rows(block)], sems.at[0]
        ).start()
        pltpu.make_async_copy(
            blocks.at[block, CHUNKS : 2 * CHUNKS],
            down.at[pl.ds(pl.multiple_of(block * CHUNKS, CHUNKS), CHUNKS)],
            sems.at[1],
        ).start()
        return carry

    lax.fori_loop(0, BLOCKS, fetch, 0)
    late = move(resid_in, resid, sems.at[2])
    for at in range(0, tokens, 128):
        cot_rows[at : at + 128, :] = cot_ref[:, at : at + 128].T
        normed2_t[:, at : at + 128] = normed2[at : at + 128, :].T
    scale_mlp = row(table, SCALE_MLP)
    cots = move(cot_rows, cot_out, sems.at[3])
    d_branch[...] = (scale_mlp * cot_rows[...].astype(FULL)).astype(LOW)
    whole_wait(up, sems.at[0])
    whole_wait(down, sems.at[1])

    def store(chunk):
        def put(source, at, core, place_in):
            for side, target in enumerate((keep, send)):
                @pl.when(core == side)
                def _(target=target):
                    pltpu.make_async_copy(source, target.at[at, place_in], out_sems.at[0]).start()

        def up_one(block, carry):
            core, at = place(block, me)
            put(grads.at[0, block_rows(block)], at, core, chunk)
            return carry

        lax.fori_loop(0, BLOCKS, up_one, 0)

        def down_one(number, carry):
            core, at = place(chunk * (BLOCKS // CHUNKS) + number, me)
            for k in range(CHUNKS):
                put(grads.at[1, block_rows(number * CHUNKS + k)], at, core, CHUNKS + k)
            return carry

        lax.fori_loop(0, BLOCKS // CHUNKS, down_one, 0)

    def down_of(chunk):
        return down[pl.ds(pl.multiple_of(chunk * BLOCKS, BLOCKS), BLOCKS)].reshape(WIDTH, WIDTH)

    def chunk_step(chunk, carry):
        hidden = nn(normed2[...], up[chunk])
        value, slope[...] = gelu_both(hidden)
        active[...] = value.astype(LOW)
        d_active = nt(d_branch[...], down_of(chunk))
        d_hidden[...] = (d_active * slope[...]).astype(LOW)
        added = nn(active[...], down_of(chunk))
        back = nt(d_hidden[...], up[chunk])

        @pl.when(chunk == 0)
        def _():
            branch[...] = added
            d_normed2[...] = back

        @pl.when(chunk > 0)
        def _():
            branch[...] += added
            d_normed2[...] += back
            whole_wait(grads, out_sems.at[0])

        grads[0] = nn(normed2_t[...], d_hidden[...]).astype(LOW)
        grads[1] = tn(active[...], d_branch[...]).astype(LOW)
        store(chunk)
        return carry

    lax.fori_loop(0, CHUNKS, chunk_step, 0)
    back = move(d_normed2, d_out, sems.at[4])
    late.wait()
    grad_scale[...] = jnp.sum(cot_rows[...].astype(FULL) * branch[...], axis=0, keepdims=True)
    for at in range(0, tokens, 128):
        rows = slice(at, at + 128)
        out[:, rows] = (resid[rows, :] + scale_mlp * branch[rows, :]).astype(LOW).T
    whole_wait(grads, out_sems.at[0])
    cots.wait()
    back.wait()


def mlp(me, cot, normed2, resid, table, blocks):
    tokens = cot.shape[1]
    pieces = (BLOCKS // 2, 2 * CHUNKS, ROWS, WIDTH)
    return pl.pallas_call(
        mlp_kernel,
        in_specs=[SMEM, VMEM, VMEM, HBM, VMEM, ANY],
        out_specs=[VMEM, HBM, HBM, VMEM, HBM, HBM],
        out_shape=[
            shape(WIDTH, tokens, kind=LOW),
            shape(tokens, WIDTH, kind=LOW),
            shape(tokens, WIDTH),
            shape(1, WIDTH),
            shape(*pieces, kind=LOW),
            shape(*pieces, kind=LOW),
        ],
        scratch_shapes=[
            pltpu.VMEM((CHUNKS, WIDTH, WIDTH), LOW),
            pltpu.VMEM((HIDDEN // ROWS, ROWS, WIDTH), LOW),
            pltpu.VMEM((WIDTH, tokens), LOW),
            pltpu.VMEM((tokens, WIDTH), LOW),
            pltpu.VMEM((tokens, WIDTH), FULL),
            pltpu.VMEM((tokens, WIDTH), LOW),
            pltpu.VMEM((tokens, WIDTH), FULL),
            pltpu.VMEM((tokens, WIDTH), LOW),
            pltpu.VMEM((2, WIDTH, WIDTH), LOW),
            pltpu.VMEM((tokens, WIDTH), LOW),
            pltpu.VMEM((tokens, WIDTH), FULL),
            pltpu.VMEM((tokens, WIDTH), FULL),
            pltpu.SemaphoreType.DMA((5,)),
            pltpu.SemaphoreType.DMA((1,)),
        ],
        compiler_params=pltpu.CompilerParams(vmem_limit_bytes=56 << 20),
        cost_estimate=spent(22),
        name="mlp",
    )(me, cot, normed2, resid, table, blocks)


def attend_back_kernel(
    me_ref, table, cot_rows, d_normed2, n2, scale2, attn, heads, qkv_in, probs_in, own, far,
    d_resid_out, d_qkv_out, grad_out, small,
    w_out, d_attn, d_heads, qkv, probs, d_resid, d_qkv, sems,
):
    me = me_ref[0]
    tokens = attn.shape[0]
    crops = tokens // LENGTH

    def fetch(block, carry):
        core, at = place(block, me)
        for side, blocks in enumerate((own, far)):
            @pl.when(core == side)
            def _(blocks=blocks):
                pltpu.make_async_copy(blocks.at[at, 3], w_out.at[block_rows(block)], sems.at[0]).start()
        return carry

    lax.fori_loop(0, BLOCKS, fetch, 0)
    arrivals = [move(qkv_in, qkv, sems.at[1]), move(probs_in, probs, sems.at[2])]

    def norm_back(at, sums):
        rows = pl.ds(pl.multiple_of(at * 80, 80), 80)
        grad, normal = d_normed2[rows, :], n2[rows, :]
        s = row(table, GAIN2) * grad
        along = jnp.mean(s * normal, axis=1, keepdims=True)
        middle = jnp.mean(s, axis=1, keepdims=True)
        total = cot_rows[rows, :].astype(FULL) + (s - middle - normal * along) * scale2[rows, :]
        d_resid[rows, :] = total
        d_attn[rows, :] = (row(table, SCALE_ATTN) * total).astype(LOW)
        return tuple(
            one + jnp.sum(more, axis=0, keepdims=True)
            for one, more in zip(sums, (grad * normal, grad, total * attn[rows, :]))
        )

    zero = jnp.zeros((1, WIDTH), FULL)
    gain, shift, scale = lax.fori_loop(0, tokens // 80, norm_back, (zero, zero, zero))
    resids = move(d_resid, d_resid_out, sems.at[3])
    small[0:1, :], small[1:2, :], small[2:3, :] = gain, shift, scale
    grad_out[...] = tn(heads[...], d_attn[...]).astype(LOW)
    whole_wait(w_out, sems.at[0])
    d_heads[...] = nt(d_attn[...], w_out[...]).astype(LOW)

    for copy in arrivals:
        copy.wait()

    def attend(crop, carry):
        rows = pl.ds(pl.multiple_of(crop * LENGTH, LENGTH), LENGTH)
        for h in range(HEADS):
            lanes = slice(h * HEAD_DIM, (h + 1) * HEAD_DIM)
            shares, grad = probs[crop, h], d_heads[rows, lanes]
            d_probs = nt(grad, qkv[2, rows, lanes])
            d_qkv[2, rows, lanes] = tn(shares.astype(LOW), grad).astype(LOW)
            d_scores = shares * (d_probs - jnp.sum(shares * d_probs, axis=1, keepdims=True))
            d_scores = d_scores.astype(LOW)
            d_qkv[0, rows, lanes] = (nn(d_scores, qkv[1, rows, lanes]) * FACTOR).astype(LOW)
            d_qkv[1, rows, lanes] = (tn(d_scores, qkv[0, rows, lanes]) * FACTOR).astype(LOW)
        return carry

    lax.fori_loop(0, crops, attend, 0)
    grads = move(d_qkv, d_qkv_out, sems.at[4])
    resids.wait()
    grads.wait()


def attend_back(me, table, cot_rows, d_normed2, n2, scale2, attn, heads, qkv, probs, own, far):
    tokens = attn.shape[0]
    return pl.pallas_call(
        attend_back_kernel,
        in_specs=[SMEM] + [VMEM] * 7 + [HBM] * 2 + [ANY] * 2,
        out_specs=[HBM, HBM, VMEM, VMEM],
        out_shape=[
            shape(tokens, WIDTH),
            shape(3, tokens, WIDTH, kind=LOW),
            shape(WIDTH, WIDTH, kind=LOW),
            shape(8, WIDTH),
        ],
        scratch_shapes=[
            pltpu.VMEM((WIDTH, WIDTH), LOW),
            pltpu.VMEM((tokens, WIDTH), LOW),
            pltpu.VMEM((tokens, WIDTH), LOW),
            pltpu.VMEM(qkv.shape, LOW),
            pltpu.VMEM(probs.shape, FULL),
            pltpu.VMEM((tokens, WIDTH), FULL),
            pltpu.VMEM(qkv.shape, LOW),
            pltpu.SemaphoreType.DMA((5,)),
        ],
        compiler_params=pltpu.CompilerParams(vmem_limit_bytes=56 << 20),
        cost_estimate=spent(9),
        name="attend_back",
    )(me, table, cot_rows, d_normed2, n2, scale2, attn, heads, qkv, probs, own, far)


def front_back_kernel(
    me_ref, table, d_resid_in, d_qkv, conv, n1_in, scale1, grad_out, small, grad_scale, own, far,
    d_frames, keep, send,
    weights, d_conv, grads, sums, d_resid, n1, sems, out_sems,
):
    me = me_ref[0]
    tokens = d_qkv.shape[1]
    crops = tokens // LENGTH

    def fetch(block, carry):
        core, at = place(block, me)
        rows = block_rows(block)
        for side, blocks in enumerate((own, far)):
            @pl.when(core == side)
            def _(blocks=blocks):
                pltpu.make_async_copy(blocks.at[at, 0:3], weights.at[:, rows], sems.at[0]).start()
        return carry

    lax.fori_loop(0, BLOCKS, fetch, 0)
    arrivals = [move(n1_in, n1, sems.at[1]), move(d_resid_in, d_resid, sems.at[2])]
    for k in range(3):
        grads[k] = tn(conv[k], d_qkv[k]).astype(LOW)
    grads[3] = grad_out[...]
    whole_wait(weights, sems.at[0])
    for k in range(3):
        d_conv[k] = nt(d_qkv[k], weights[k])

    sums[...] = jnp.zeros_like(sums)
    for copy in arrivals:
        copy.wait()

    def back(crop, carry):
        rows = pl.ds(pl.multiple_of(crop * LENGTH, LENGTH), LENGTH)
        middle = jnp.zeros((LENGTH, 1), FULL)
        along = jnp.zeros((LENGTH, 1), FULL)
        pieces = []
        for at in range(0, WIDTH, 128):
            lanes = slice(at, at + 128)
            gain = table[GAIN1 : GAIN1 + 1, lanes]
            normal = n1[rows, lanes]
            normed = normal * gain + table[SHIFT1 : SHIFT1 + 1, lanes]
            before, after = down_one(normed), up_one(normed)
            parts = [0.0, 0.0, 0.0]
            for k, start in enumerate((KERNEL_Q, KERNEL_K, KERNEL_V)):
                grad = d_conv[k, rows, lanes]
                for j, seen in enumerate((before, normed, after)):
                    sums[start + j : start + j + 1, lanes] += jnp.sum(grad * seen, axis=0, keepdims=True)
                    parts[j] = parts[j] + table[start + j : start + j + 1, lanes] * grad
            total = up_one(parts[0]) + parts[1] + down_one(parts[2])
            sums[GAIN1 : GAIN1 + 1, lanes] += jnp.sum(total * normal, axis=0, keepdims=True)
            sums[SHIFT1 : SHIFT1 + 1, lanes] += jnp.sum(total, axis=0, keepdims=True)
            s = gain * total
            d_conv[0, rows, lanes] = s
            middle += jnp.sum(s, axis=1, keepdims=True)
            along += jnp.sum(s * normal, axis=1, keepdims=True)
        middle, along = middle / WIDTH, along / WIDTH
        for at in range(0, WIDTH, 128):
            lanes = slice(at, at + 128)
            d_conv[1, rows, lanes] = d_resid[rows, lanes] + (
                d_conv[0, rows, lanes] - middle - n1[rows, lanes] * along
            ) * scale1[rows, :]
        return carry

    lax.fori_loop(0, crops, back, 0)
    for at in range(0, tokens, 128):
        d_frames[:, at : at + 128] = d_conv[1, at : at + 128, :].astype(LOW).T
    sums[GAIN2 : SHIFT2 + 1, :] = small[0:2, :]
    sums[SCALE_ATTN : SCALE_ATTN + 1, :] = small[2:3, :]
    sums[SCALE_MLP : SCALE_MLP + 1, :] = grad_scale[...]
    grads[4] = jnp.zeros((WIDTH, WIDTH), LOW)
    grads[4, :, 0:128] = sums[...].T.astype(LOW)

    def store(block, carry):
        core, at = place(block, me)
        for side, target in enumerate((keep, send)):
            @pl.when(core == side)
            def _(target=target):
                pltpu.make_async_copy(
                    grads.at[:, block_rows(block)], target.at[at], out_sems.at[0]
                ).start()
        return carry

    lax.fori_loop(0, BLOCKS, store, 0)
    whole_wait(grads, out_sems.at[0])


def front_back(me, table, d_resid, d_qkv, conv, n1, scale1, grad_out, small, grad_scale, own, far):
    tokens = n1.shape[0]
    pieces = (BLOCKS // 2, 5, ROWS, WIDTH)
    return pl.pallas_call(
        front_back_kernel,
        in_specs=[SMEM, VMEM, HBM, VMEM, VMEM, HBM] + [VMEM] * 4 + [ANY] * 2,
        out_specs=[VMEM, HBM, HBM],
        out_shape=[
            shape(WIDTH, tokens, kind=LOW),
            shape(*pieces, kind=LOW),
            shape(*pieces, kind=LOW),
        ],
        scratch_shapes=[
            pltpu.VMEM((3, WIDTH, WIDTH), LOW),
            pltpu.VMEM((3, tokens, WIDTH), FULL),
            pltpu.VMEM((5, WIDTH, WIDTH), LOW),
            pltpu.VMEM((128, WIDTH), FULL),
            pltpu.VMEM((tokens, WIDTH), FULL),
            pltpu.VMEM((tokens, WIDTH), FULL),
            pltpu.SemaphoreType.DMA((3,)),
            pltpu.SemaphoreType.DMA((1,)),
        ],
        compiler_params=pltpu.CompilerParams(vmem_limit_bytes=56 << 20),
        cost_estimate=spent(10),
        name="front_back",
    )(me, table, d_resid, d_qkv, conv, n1, scale1, grad_out, small, grad_scale, own, far)


def pack_kernel(
    gain1, shift1, scale_attn, gain2, shift2, scale_mlp, kernel_q, kernel_k, kernel_v,
    w_query, w_key, w_value, w_out, w_up, w_down,
    attn_shard, mlp_shard, table,
):
    table[...] = jnp.zeros_like(table)
    for at, one in enumerate((gain1, shift1, scale_attn, gain2, shift2, scale_mlp)):
        table[at : at + 1, 0:ROWS] = one[...].astype(FULL)
    for at, one in ((KERNEL_Q, kernel_q), (KERNEL_K, kernel_k), (KERNEL_V, kernel_v)):
        table[at : at + 3, 0:ROWS] = one[...].astype(FULL)
    attn_shard[4] = jnp.zeros((ROWS, WIDTH), LOW)
    attn_shard[4, :, 0:128] = table[...].T[0:ROWS, :].astype(LOW)
    for at, one in ((0, w_query), (1, w_key), (2, w_value), (3, w_out)):
        attn_shard[at] = one[...]
    for chunk in range(CHUNKS):
        mlp_shard[chunk] = w_up[:, chunk * WIDTH : (chunk + 1) * WIDTH]
        mlp_shard[CHUNKS + chunk] = w_down[chunk * ROWS : (chunk + 1) * ROWS, :]


def pack(vectors, kernels, matrices):
    return pl.pallas_call(
        pack_kernel,
        in_specs=[VMEM] * 15,
        out_specs=[VMEM] * 2,
        out_shape=[
            shape(5, ROWS, WIDTH, kind=LOW),
            shape(2 * CHUNKS, ROWS, WIDTH, kind=LOW),
        ],
        scratch_shapes=[pltpu.VMEM((128, 128), FULL)],
        name="pack",
    )(*[one.reshape(1, -1) for one in vectors], *[one.T for one in kernels], *matrices)


def permute(values, even, odd):
    count = lax.axis_size("dev")
    return lax.ppermute(
        values, "dev", [(at, at ^ (odd if at & 1 else even)) for at in range(count)]
    )


def after(first, *others):
    return lax.optimization_barrier((first,) + others)


def gather_planes(shard):
    blocks = jnp.stack([shard] + [permute(shard, 8 * k, 8 * k) for k in range(1, 4)])
    blocks = jnp.concatenate((blocks, permute(blocks, 2, 4)))
    return jnp.concatenate((blocks, permute(blocks, 4, 2)))


def added(kept, arrived):
    return kept.astype(FULL) + arrived.astype(FULL)


def halve(kept, arrived):
    half = kept.shape[0] // 2
    return added(kept[:half], arrived[:half]), added(kept[half:], arrived[half:]).astype(LOW)


def across(total):
    own = total[0]
    for k in range(1, 4):
        own = own + permute(total[k].astype(LOW), 8 * k, 8 * k).astype(FULL)
    return own


def gather_plain(pieces):
    whole = [lax.all_gather(one, "dev", axis=0, tiled=True) for one in pieces]
    return jnp.stack([one.reshape(BLOCKS, ROWS, WIDTH) for one in whole], axis=1)


def places_plain():
    sides = ([0] * (BLOCKS // 2), [0] * (BLOCKS // 2))
    for block in range(BLOCKS):
        x, y, z = (block >> 1) & 1, (block >> 2) & 1, block >> 3
        sides[block & 1][(8 * x + 4 * y if block & 1 else 8 * y + 4 * x) + z] = block
    return sides


def apart(blocks):
    return tuple(jnp.stack([blocks[k] for k in side]) for side in places_plain())


def together(kept, sent):
    order = places_plain()
    found = {block: (side, at) for side in range(2) for at, block in enumerate(order[side])}
    return jnp.stack([(kept, sent)[found[k][0]][found[k][1]] for k in range(BLOCKS)])


def scatter_plain(matrix):
    return lax.psum_scatter(matrix.astype(FULL), "dev", scatter_dimension=0, tiled=True)


def local(
    frames,
    norm1_gain,
    norm1_shift,
    kernel_query,
    kernel_key,
    kernel_value,
    w_query,
    w_key,
    w_value,
    w_out,
    scale_attn,
    norm2_gain,
    norm2_shift,
    w_up,
    w_down,
    scale_mlp,
    cotangent,
):
    count = lax.axis_size("dev")
    own, columns = frames.shape[0], frames.shape[1] // count
    fast = own == ROWS and own * count == WIDTH
    vectors = (norm1_gain, norm1_shift, scale_attn, norm2_gain, norm2_shift, scale_mlp)
    kernels = (kernel_query, kernel_key, kernel_value)

    def to_crops(values):
        split = values.reshape(own, count, columns).transpose(1, 0, 2)
        return lax.all_to_all(split, "dev", 0, 0).reshape(WIDTH, columns)

    def to_channels(values):
        split = values.reshape(count, own, columns)
        return lax.all_to_all(split, "dev", 0, 0).transpose(1, 0, 2).reshape(own, -1)

    matrices = (w_query, w_key, w_value, w_out)
    matrices = (w_query, w_key, w_value, w_out)
    x = to_crops(frames)
    if fast:
        me = lax.axis_index("dev").astype(jnp.int32).reshape(1)
        attn_shard, mlp_shard = pack(vectors, kernels, matrices + (w_up, w_down))
        mlp_blocks = lax.all_gather(mlp_shard, "dev", axis=0, tiled=True)
        mlp_blocks = mlp_blocks.reshape((BLOCKS,) + mlp_shard.shape)
        own_blocks = gather_planes(attn_shard)
        x, own_blocks, cotangent = after(x, own_blocks, cotangent)
        far_blocks = permute(own_blocks, 1, 1)
    else:
        me = jnp.zeros((1,), jnp.int32)
        small = jnp.concatenate([one[:, None] for one in vectors] + list(kernels), axis=1)
        small = jnp.pad(small, ((0, 0), (0, WIDTH - small.shape[1])))
        own_blocks, far_blocks = apart(gather_plain(matrices + (small,)))
        ups = gather_plain([w_up[:, k * WIDTH : (k + 1) * WIDTH] for k in range(CHUNKS)])
        downs = lax.all_gather(w_down, "dev", axis=0, tiled=True)
        downs = downs.reshape(BLOCKS, CHUNKS, ROWS, WIDTH)
        mlp_blocks = jnp.concatenate((ups, downs), axis=1)
    cot = to_crops(cotangent)
    table, n1, scale1, conv, qkv, probs, heads, attn, resid, n2, scale2, normed2 = front(
        me, x, own_blocks, far_blocks
    )
    out, cot_rows, d_normed2, grad_scale, keep_mlp, send_mlp = mlp(
        me, cot, normed2, resid, table, mlp_blocks
    )
    output = to_channels(out)
    d_resid, d_qkv, grad_out, small = attend_back(
        me, table, cot_rows, d_normed2, n2, scale2, attn, heads, qkv, probs, own_blocks, far_blocks
    )
    if fast:
        mlp_kept, mlp_sent = halve(keep_mlp, permute(send_mlp, 1, 1))
        mlp_kept, mlp_sent, d_qkv = after(mlp_kept, mlp_sent, d_qkv)
    d_frames, keep, send = front_back(
        me, table, d_resid, d_qkv, conv, n1, scale1, grad_out, small, grad_scale,
        own_blocks, far_blocks,
    )
    frames_grad = to_channels(d_frames)
    if fast:
        kept, sent = halve(keep, permute(send, 1, 1))
        mlp_kept, mlp_sent = halve(mlp_kept, permute(mlp_sent, 4, 2))
        kept, sent = halve(kept, permute(sent, 4, 2))
        total = across(added(mlp_kept, permute(mlp_sent, 2, 4)))
        grad_up = jnp.concatenate([total[k] for k in range(CHUNKS)], axis=1)
        grad_down = total[CHUNKS:].reshape(-1, WIDTH)
        grad_query, grad_key, grad_value, grad_out, grad_small = across(
            added(kept, permute(sent, 2, 4))
        )
    else:
        blocks = together(keep_mlp, send_mlp)
        ups = blocks[:, :CHUNKS].transpose(0, 2, 1, 3).reshape(WIDTH, HIDDEN)
        grad_up = scatter_plain(ups)
        grad_down = scatter_plain(blocks[:, CHUNKS:].reshape(HIDDEN, WIDTH))
        blocks = together(keep, send)
        grad_query, grad_key, grad_value, grad_out, grad_small = (
            scatter_plain(blocks[:, k].reshape(WIDTH, WIDTH)) for k in range(5)
        )
    return (
        output,
        frames_grad,
        grad_small[:, GAIN1],
        grad_small[:, SHIFT1],
        grad_small[:, KERNEL_Q : KERNEL_Q + 3],
        grad_small[:, KERNEL_K : KERNEL_K + 3],
        grad_small[:, KERNEL_V : KERNEL_V + 3],
        grad_query,
        grad_key,
        grad_value,
        grad_out,
        grad_small[:, SCALE_ATTN],
        grad_small[:, GAIN2],
        grad_small[:, SHIFT2],
        grad_up,
        grad_down,
        grad_small[:, SCALE_MLP],
    )


def solution(mesh):
    in_specs = (
        P("dev", None),
        P("dev"),
        P("dev"),
        P("dev", None),
        P("dev", None),
        P("dev", None),
        P("dev", None),
        P("dev", None),
        P("dev", None),
        P("dev", None),
        P("dev"),
        P("dev"),
        P("dev"),
        P("dev", None),
        P("dev", None),
        P("dev"),
        P("dev", None),
    )
    out_specs = (
        P("dev", None),
        P("dev", None),
        P("dev"),
        P("dev"),
        P("dev", None),
        P("dev", None),
        P("dev", None),
        P("dev", None),
        P("dev", None),
        P("dev", None),
        P("dev", None),
        P("dev"),
        P("dev"),
        P("dev"),
        P("dev", None),
        P("dev", None),
        P("dev"),
    )
    return jax.shard_map(local, mesh=mesh, in_specs=in_specs, out_specs=out_specs, check_vma=False)
```

```python
import math

import jax
import jax.numpy as jnp
from jax import lax
from jax.experimental import pallas as pl
from jax.experimental.pallas import tpu as pltpu
from jax.sharding import PartitionSpec as P

HEADS = 4
HEAD_DIM = 128
LENGTH = 160
WINDOW = 19
WIDTH = 512
HIDDEN = 2048
FACTOR = HEAD_DIM ** (-0.5)
EPSILON = 1e-05
ROWS = 16
BLOCKS = WIDTH // ROWS
CHUNKS = HIDDEN // WIDTH
LOW = jnp.bfloat16
FULL = jnp.float32

VMEM = pl.BlockSpec(memory_space=pltpu.VMEM)
ANY = pl.BlockSpec(memory_space=pl.ANY)
HBM = pl.BlockSpec(memory_space=pltpu.HBM)
SMEM = pl.BlockSpec(memory_space=pltpu.SMEM)

GAIN1, SHIFT1, SCALE_ATTN, GAIN2, SHIFT2, SCALE_MLP, KERNEL_Q, KERNEL_K, KERNEL_V = (
    0, 1, 2, 3, 4, 5, 6, 9, 12,
)


def nn(left, right):
    return jnp.dot(left, right, preferred_element_type=FULL)


def nt(left, right):
    return lax.dot_general(left, right, (((1,), (1,)), ((), ())), preferred_element_type=FULL)


def tn(left, right):
    return lax.dot_general(left, right, (((0,), (0,)), ((), ())), preferred_element_type=FULL)


def place(block, me):
    far = block ^ me
    x, y, near_z, far_z = (far >> 1) & 1, (far >> 2) & 1, (far >> 3) & 1, far >> 4
    across = jnp.where(block & 1 == 0, 8 * y + 4 * x, 8 * x + 4 * y)
    return far & 1, across + 2 * near_z + far_z


def block_rows(block, rows=ROWS):
    return pl.ds(pl.multiple_of(block * rows, rows), rows)


def fetch_blocks(sources, me, pieces, copy_to):
    def fetch(block, carry):
        core, at = place(block, me)
        for number, source in enumerate(sources):
            side, late = number // 2, number % 2
            @pl.when((core == side) & (at >> 3 == late))
            def _(source=source, late=late):
                for piece, (target, sem) in zip(pieces, copy_to(block)):
                    pltpu.make_async_copy(source.at[at - 8 * late, piece], target, sem).start()
        return carry

    lax.fori_loop(0, BLOCKS, fetch, 0)


def whole_wait(ref, sem):
    pltpu.make_async_copy(ref, ref, sem).wait()


def move(source, target, sem):
    copy = pltpu.make_async_copy(source, target, sem)
    copy.start()
    return copy


def down_one(values):
    at = lax.broadcasted_iota(jnp.int32, values.shape, 0)
    return jnp.where(at == 0, 0.0, pltpu.roll(values, 1, 0))


def up_one(values):
    at = lax.broadcasted_iota(jnp.int32, values.shape, 0)
    last = values.shape[0] - 1
    return jnp.where(at == last, 0.0, pltpu.roll(values, last, 0))


def normalise(values):
    center = jnp.mean(values, axis=1, keepdims=True)
    centered = values - center
    scale = lax.rsqrt(jnp.mean(centered * centered, axis=1, keepdims=True) + EPSILON)
    return centered * scale, scale


def row(table, index):
    return table[index : index + 1, :]


def front_kernel(
    me_ref, x_ref, source0, source1, source2, source3,
    table_out, n1_out, scale1_out, conv_out, qkv_out, probs_out, heads_out, attn_out, resid_out,
    n2_out, scale2_out, normed2_out,
    weights, x_rows, table, n1, scale1, conv, qkv, probs, heads, attn, resid, n2, scale2, normed2,
    in_sem, sems,
):
    me = me_ref[0]
    tokens = x_ref.shape[1]
    crops = tokens // LENGTH
    copies = []

    def send(source, target):
        copies.append(move(source, target, sems.at[len(copies)]))

    fetch_blocks(
        (source0, source1, source2, source3), me, (slice(None),),
        lambda block: ((weights.at[:, block_rows(block)], in_sem.at[0]),),
    )
    for at in range(0, tokens, 128):
        x_rows[at : at + 128, :] = x_ref[:, at : at + 128].T.astype(FULL)

    def norm_one(at, carry):
        rows = pl.ds(pl.multiple_of(at * 80, 80), 80)
        n1[rows, :], scale1[rows, :] = normalise(x_rows[rows, :])
        return carry

    lax.fori_loop(0, tokens // 80, norm_one, 0)
    send(n1, n1_out)
    send(scale1, scale1_out)
    whole_wait(weights, in_sem.at[0])
    table[...] = weights[4, :, 0:128].astype(FULL).T[0:16, :]
    send(table, table_out)

    def convolve(crop, carry):
        rows = pl.ds(pl.multiple_of(crop * LENGTH, LENGTH), LENGTH)
        for at in range(0, WIDTH, 128):
            lanes = slice(at, at + 128)
            normed = n1[rows, lanes] * table[GAIN1 : GAIN1 + 1, lanes] + table[SHIFT1 : SHIFT1 + 1, lanes]
            before, after = down_one(normed), up_one(normed)
            for k, start in enumerate((KERNEL_Q, KERNEL_K, KERNEL_V)):
                conv[k, rows, lanes] = (
                    table[start : start + 1, lanes] * before
                    + table[start + 1 : start + 2, lanes] * normed
                    + table[start + 2 : start + 3, lanes] * after
                ).astype(LOW)
        return carry

    lax.fori_loop(0, crops, convolve, 0)
    send(conv, conv_out)
    for k in range(3):
        qkv[k] = nn(conv[k], weights[k]).astype(LOW)
    send(qkv, qkv_out)

    near_t = lax.broadcasted_iota(jnp.int32, (LENGTH, LENGTH), 0)
    near_u = lax.broadcasted_iota(jnp.int32, (LENGTH, LENGTH), 1)
    nearby = jnp.abs(near_t - near_u) <= WINDOW // 2

    def attend(crop, carry):
        rows = pl.ds(pl.multiple_of(crop * LENGTH, LENGTH), LENGTH)
        for h in range(HEADS):
            lanes = slice(h * HEAD_DIM, (h + 1) * HEAD_DIM)
            scores = jnp.where(nearby, nt(qkv[0, rows, lanes], qkv[1, rows, lanes]) * FACTOR, -1e30)
            powers = jnp.exp(scores - jnp.max(scores, axis=1, keepdims=True))
            shares = powers / jnp.sum(powers, axis=1, keepdims=True)
            probs[crop, h] = shares
            heads[rows, lanes] = nn(shares.astype(LOW), qkv[2, rows, lanes]).astype(LOW)
        return carry

    lax.fori_loop(0, crops, attend, 0)
    send(probs, probs_out)
    send(heads, heads_out)
    attn[...] = nn(heads[...], weights[3])
    send(attn, attn_out)

    def norm_two(at, carry):
        rows = pl.ds(pl.multiple_of(at * 80, 80), 80)
        mixed = x_rows[rows, :] + row(table, SCALE_ATTN) * attn[rows, :]
        resid[rows, :] = mixed
        normal, scale = normalise(mixed)
        n2[rows, :], scale2[rows, :] = normal, scale
        normed2[rows, :] = (normal * row(table, GAIN2) + row(table, SHIFT2)).astype(LOW)
        return carry

    lax.fori_loop(0, tokens // 80, norm_two, 0)
    send(normed2, normed2_out)
    send(resid, resid_out)
    send(n2, n2_out)
    send(scale2, scale2_out)
    for copy in copies:
        copy.wait()


def front(me, x, sources):
    tokens = x.shape[1]
    crops = tokens // LENGTH
    shapes = [
        shape(16, WIDTH),
        shape(tokens, WIDTH),
        shape(tokens, 1),
        shape(3, tokens, WIDTH, kind=LOW),
        shape(3, tokens, WIDTH, kind=LOW),
        shape(crops, HEADS, LENGTH, LENGTH),
        shape(tokens, WIDTH, kind=LOW),
        shape(tokens, WIDTH),
        shape(tokens, WIDTH),
        shape(tokens, WIDTH),
        shape(tokens, 1),
        shape(tokens, WIDTH, kind=LOW),
    ]
    return pl.pallas_call(
        front_kernel,
        in_specs=[SMEM, VMEM] + [ANY] * 4,
        out_specs=[HBM] * 12,
        out_shape=shapes,
        scratch_shapes=[
            pltpu.VMEM((5, WIDTH, WIDTH), LOW),
            pltpu.VMEM((tokens, WIDTH), FULL),
        ]
        + [pltpu.VMEM(one.shape, one.dtype) for one in shapes]
        + [pltpu.SemaphoreType.DMA((1,)), pltpu.SemaphoreType.DMA((12,))],
        compiler_params=pltpu.CompilerParams(vmem_limit_bytes=56 << 20),
        cost_estimate=spent(0.5),
        name="front",
    )(me, x, *sources)


def spent(microseconds):
    return pl.CostEstimate(flops=int(microseconds * 1.15e9), bytes_accessed=0, transcendentals=0)


def shape(*dims, kind=FULL):
    return jax.ShapeDtypeStruct(dims, kind)


ERF_P = 0.3275911
ERF_A = (0.254829592, -0.284496736, 1.421413741, -1.453152027, 1.061405429)


def gelu_both(values):
    size = jnp.abs(values)
    near = 1.0 / (1.0 + (ERF_P * math.sqrt(0.5)) * size)
    bell = jnp.exp(-0.5 * values * values)
    series = ERF_A[4]
    for coefficient in ERF_A[3::-1]:
        series = series * near + coefficient
    tail = (0.5 * series) * near * bell
    below = jnp.where(values < 0, tail, 1.0 - tail)
    return values * below, below + values * bell * (0.5 * math.sqrt(2 / math.pi))


def mlp_kernel(
    me_ref, cot_ref, normed2, table, resid_in, n2_in, scale2_in, attn_in, source0, source1, source2, source3,
    out, d_resid_out, d_attn_out, small, keep, send,
    up, down, normed2_t, cot_rows, d_branch, branch, active, slope, d_hidden, d_normed2, grad_up,
    grad_down, resid, n2, scale2, attn, d_resid, d_attn, sems,
):
    me = me_ref[0]
    tokens = cot_ref.shape[1]
    quarter = BLOCKS // CHUNKS

    fetch_blocks(
        (source0, source1, source2, source3), me, (slice(0, CHUNKS), slice(CHUNKS, 2 * CHUNKS)),
        lambda block: (
            (up.at[:, block_rows(block)], sems.at[0]),
            (down.at[block_rows(block, CHUNKS)], sems.at[1]),
        ),
    )
    arrivals = [
        move(source, target, sems.at[4 + at])
        for at, (source, target) in enumerate(
            ((resid_in, resid), (n2_in, n2), (scale2_in, scale2), (attn_in, attn))
        )
    ]
    scale_mlp = row(table, SCALE_MLP)
    for at in range(0, tokens, 128):
        rows = slice(at, at + 128)
        cot_rows[rows, :] = cot_ref[:, rows].T
        d_branch[rows, :] = (scale_mlp * cot_rows[rows, :].astype(FULL)).astype(LOW)
        normed2_t[:, rows] = normed2[rows, :].T
    whole_wait(up, sems.at[0])
    whole_wait(down, sems.at[1])

    def put(source, at, core, places, sem):
        for side, target in enumerate((keep, send)):
            @pl.when(core == side)
            def _(target=target):
                pltpu.make_async_copy(source, target.at[at, places], sem).start()

    def chunk_step(chunk, carry):
        rows = block_rows(chunk, BLOCKS)
        hidden = nn(normed2[...], up[chunk])
        value, slope[...] = gelu_both(hidden)
        active[...] = value.astype(LOW)
        down_rows = down[rows].reshape(WIDTH, WIDTH)
        d_active = nt(d_branch[...], down_rows)
        d_hidden[...] = (d_active * slope[...]).astype(LOW)
        added = nn(active[...], down_rows)
        back = nt(d_hidden[...], up[chunk])

        @pl.when(chunk == 0)
        def _():
            branch[...] = added
            d_normed2[...] = back

        @pl.when(chunk > 0)
        def _():
            branch[...] += added
            d_normed2[...] += back

        grad_up[chunk] = nn(normed2_t[...], d_hidden[...]).astype(LOW)
        grad_down[rows] = tn(active[...], d_branch[...]).astype(LOW).reshape(BLOCKS, ROWS, WIDTH)

        def store(number, carry):
            block = chunk * quarter + number
            core, at = place(block, me)
            put(grad_down.at[block_rows(block, CHUNKS)], at, core, pl.ds(CHUNKS, CHUNKS), sems.at[2])
            return carry

        return lax.fori_loop(0, quarter, store, carry)

    lax.fori_loop(0, CHUNKS, chunk_step, 0)

    def store(block, carry):
        core, at = place(block, me)
        put(grad_up.at[:, block_rows(block)], at, core, pl.ds(0, CHUNKS), sems.at[3])
        return carry

    lax.fori_loop(0, BLOCKS, store, 0)
    for copy in arrivals:
        copy.wait()

    def norm_back(at, sums):
        rows = pl.ds(pl.multiple_of(at * 80, 80), 80)
        grad, normal, cot = d_normed2[rows, :], n2[rows, :], cot_rows[rows, :].astype(FULL)
        s = row(table, GAIN2) * grad
        along = jnp.mean(s * normal, axis=1, keepdims=True)
        middle = jnp.mean(s, axis=1, keepdims=True)
        total = cot + (s - middle - normal * along) * scale2[rows, :]
        d_resid[rows, :] = total
        d_attn[rows, :] = (row(table, SCALE_ATTN) * total).astype(LOW)
        terms = (grad * normal, grad, total * attn[rows, :], cot * branch[rows, :])
        return tuple(one + jnp.sum(more, axis=0, keepdims=True) for one, more in zip(sums, terms))

    sums = lax.fori_loop(0, tokens // 80, norm_back, (jnp.zeros((1, WIDTH), FULL),) * 4)
    leaving = [
        move(d_attn, d_attn_out, sems.at[8]),
        move(d_resid, d_resid_out, sems.at[9]),
    ]
    for at, one in enumerate(sums):
        small[at : at + 1, :] = one
    for at in range(0, tokens, 128):
        rows = slice(at, at + 128)
        out[:, rows] = (resid[rows, :] + scale_mlp * branch[rows, :]).astype(LOW).T
    whole_wait(grad_down, sems.at[2])
    whole_wait(grad_up, sems.at[3])
    for copy in leaving:
        copy.wait()


def mlp(me, cot, normed2, table, resid, n2, scale2, attn, sources):
    tokens = cot.shape[1]
    pieces = (BLOCKS // 2, 2 * CHUNKS, ROWS, WIDTH)
    rows_full, rows_low = pltpu.VMEM((tokens, WIDTH), FULL), pltpu.VMEM((tokens, WIDTH), LOW)
    return pl.pallas_call(
        mlp_kernel,
        in_specs=[SMEM, VMEM, VMEM, VMEM] + [HBM] * 4 + [ANY] * 4,
        out_specs=[VMEM, HBM, HBM, VMEM, HBM, HBM],
        out_shape=[
            shape(WIDTH, tokens, kind=LOW),
            shape(tokens, WIDTH),
            shape(tokens, WIDTH, kind=LOW),
            shape(8, WIDTH),
            shape(*pieces, kind=LOW),
            shape(*pieces, kind=LOW),
        ],
        scratch_shapes=[
            pltpu.VMEM((CHUNKS, WIDTH, WIDTH), LOW),
            pltpu.VMEM((HIDDEN // ROWS, ROWS, WIDTH), LOW),
            pltpu.VMEM((WIDTH, tokens), LOW),
            rows_low,
            rows_low,
            rows_full,
            rows_low,
            rows_full,
            rows_low,
            rows_full,
            pltpu.VMEM((CHUNKS, WIDTH, WIDTH), LOW),
            pltpu.VMEM((HIDDEN // ROWS, ROWS, WIDTH), LOW),
            rows_full,
            rows_full,
            pltpu.VMEM((tokens, 1), FULL),
            rows_full,
            rows_full,
            rows_low,
            pltpu.SemaphoreType.DMA((10,)),
        ],
        compiler_params=pltpu.CompilerParams(vmem_limit_bytes=56 << 20),
        cost_estimate=spent(0.5),
        name="mlp",
    )(me, cot, normed2, table, resid, n2, scale2, attn, *sources)


def attend_back_kernel(
    me_ref, d_attn, heads, qkv_in, probs_in, conv_in, source0, source1, source2, source3,
    d_qkv_out, keep, send,
    w_out, d_heads, qkv, probs, conv, d_qkv, grads, sems,
):
    me = me_ref[0]
    crops = d_attn.shape[0] // LENGTH

    fetch_blocks(
        (source0, source1, source2, source3), me, (3,),
        lambda block: ((w_out.at[block_rows(block)], sems.at[0]),),
    )
    arrivals = [move(qkv_in, qkv, sems.at[1]), move(probs_in, probs, sems.at[2])]
    convs = move(conv_in, conv, sems.at[3])
    grads[3] = tn(heads[...], d_attn[...]).astype(LOW)
    whole_wait(w_out, sems.at[0])
    d_heads[...] = nt(d_attn[...], w_out[...]).astype(LOW)
    for copy in arrivals:
        copy.wait()

    def attend(crop, carry):
        rows = pl.ds(pl.multiple_of(crop * LENGTH, LENGTH), LENGTH)
        for h in range(HEADS):
            lanes = slice(h * HEAD_DIM, (h + 1) * HEAD_DIM)
            shares, grad = probs[crop, h], d_heads[rows, lanes]
            d_probs = nt(grad, qkv[2, rows, lanes])
            d_qkv[2, rows, lanes] = tn(shares.astype(LOW), grad).astype(LOW)
            d_scores = shares * (d_probs - jnp.sum(shares * d_probs, axis=1, keepdims=True))
            d_scores = d_scores.astype(LOW)
            d_qkv[0, rows, lanes] = (nn(d_scores, qkv[1, rows, lanes]) * FACTOR).astype(LOW)
            d_qkv[1, rows, lanes] = (tn(d_scores, qkv[0, rows, lanes]) * FACTOR).astype(LOW)
        return carry

    lax.fori_loop(0, crops, attend, 0)
    leaving = move(d_qkv, d_qkv_out, sems.at[4])
    convs.wait()
    for k in range(3):
        grads[k] = tn(conv[k], d_qkv[k]).astype(LOW)

    def store(block, carry):
        core, at = place(block, me)
        for side, target in enumerate((keep, send)):
            @pl.when(core == side)
            def _(target=target):
                pltpu.make_async_copy(
                    grads.at[:, block_rows(block)], target.at[at], sems.at[5]
                ).start()
        return carry

    lax.fori_loop(0, BLOCKS, store, 0)
    whole_wait(grads, sems.at[5])
    leaving.wait()


def attend_back(me, d_attn, heads, qkv, probs, conv, sources):
    tokens = heads.shape[0]
    pieces = (BLOCKS // 2, 4, ROWS, WIDTH)
    return pl.pallas_call(
        attend_back_kernel,
        in_specs=[SMEM, VMEM, VMEM] + [HBM] * 3 + [ANY] * 4,
        out_specs=[HBM] * 3,
        out_shape=[
            shape(3, tokens, WIDTH, kind=LOW),
            shape(*pieces, kind=LOW),
            shape(*pieces, kind=LOW),
        ],
        scratch_shapes=[
            pltpu.VMEM((WIDTH, WIDTH), LOW),
            pltpu.VMEM((tokens, WIDTH), LOW),
            pltpu.VMEM(qkv.shape, LOW),
            pltpu.VMEM(probs.shape, FULL),
            pltpu.VMEM(conv.shape, LOW),
            pltpu.VMEM(qkv.shape, LOW),
            pltpu.VMEM((4, WIDTH, WIDTH), LOW),
            pltpu.SemaphoreType.DMA((6,)),
        ],
        compiler_params=pltpu.CompilerParams(vmem_limit_bytes=56 << 20),
        cost_estimate=spent(0.5),
        name="attend_back",
    )(me, d_attn, heads, qkv, probs, conv, *sources)


def front_back_kernel(
    me_ref, table, d_qkv, scale1, small, n1_in, d_resid_in, source0, source1, source2, source3,
    both,
    weights, d_conv, sums, d_resid, n1, sems,
):
    me = me_ref[0]
    tokens = d_qkv.shape[1]
    crops = tokens // LENGTH

    fetch_blocks(
        (source0, source1, source2, source3), me, (slice(0, 3),),
        lambda block: ((weights.at[:, block_rows(block)], sems.at[0]),),
    )
    arrivals = [move(n1_in, n1, sems.at[1]), move(d_resid_in, d_resid, sems.at[2])]
    sums[...] = jnp.zeros_like(sums)
    whole_wait(weights, sems.at[0])
    for k in range(3):
        d_conv[k] = nt(d_qkv[k], weights[k])
    for copy in arrivals:
        copy.wait()

    def back(crop, carry):
        rows = pl.ds(pl.multiple_of(crop * LENGTH, LENGTH), LENGTH)
        middle = jnp.zeros((LENGTH, 1), FULL)
        along = jnp.zeros((LENGTH, 1), FULL)
        for at in range(0, WIDTH, 128):
            lanes = slice(at, at + 128)
            gain = table[GAIN1 : GAIN1 + 1, lanes]
            normal = n1[rows, lanes]
            normed = normal * gain + table[SHIFT1 : SHIFT1 + 1, lanes]
            before, after = down_one(normed), up_one(normed)
            parts = [0.0, 0.0, 0.0]
            for k, start in enumerate((KERNEL_Q, KERNEL_K, KERNEL_V)):
                grad = d_conv[k, rows, lanes]
                for j, seen in enumerate((before, normed, after)):
                    sums[start + j : start + j + 1, lanes] += jnp.sum(grad * seen, axis=0, keepdims=True)
                    parts[j] = parts[j] + table[start + j : start + j + 1, lanes] * grad
            total = up_one(parts[0]) + parts[1] + down_one(parts[2])
            sums[GAIN1 : GAIN1 + 1, lanes] += jnp.sum(total * normal, axis=0, keepdims=True)
            sums[SHIFT1 : SHIFT1 + 1, lanes] += jnp.sum(total, axis=0, keepdims=True)
            s = gain * total
            d_conv[0, rows, lanes] = s
            middle += jnp.sum(s, axis=1, keepdims=True)
            along += jnp.sum(s * normal, axis=1, keepdims=True)
        middle, along = middle / WIDTH, along / WIDTH
        for at in range(0, WIDTH, 128):
            lanes = slice(at, at + 128)
            d_conv[1, rows, lanes] = d_resid[rows, lanes] + (
                d_conv[0, rows, lanes] - middle - n1[rows, lanes] * along
            ) * scale1[rows, :]
        return carry

    lax.fori_loop(0, crops, back, 0)
    for at in range(0, tokens, 128):
        both[:, at : at + 128] = d_conv[1, at : at + 128, :].astype(LOW).T
    sums[GAIN2 : SHIFT2 + 1, :] = small[0:2, :]
    sums[SCALE_ATTN : SCALE_ATTN + 1, :] = small[2:3, :]
    sums[SCALE_MLP : SCALE_MLP + 1, :] = small[3:4, :]
    high = sums[0:16, :].astype(LOW).astype(FULL)
    sums[16:32, :] = sums[0:16, :] - high
    both[:, tokens : tokens + 128] = sums[...].astype(LOW).T


def front_back(me, table, d_qkv, scale1, small, n1, d_resid, sources):
    tokens = n1.shape[0]
    return pl.pallas_call(
        front_back_kernel,
        in_specs=[SMEM] + [VMEM] * 4 + [HBM] * 2 + [ANY] * 4,
        out_specs=VMEM,
        out_shape=shape(WIDTH, tokens + 128, kind=LOW),
        scratch_shapes=[
            pltpu.VMEM((3, WIDTH, WIDTH), LOW),
            pltpu.VMEM((3, tokens, WIDTH), FULL),
            pltpu.VMEM((128, WIDTH), FULL),
            pltpu.VMEM((tokens, WIDTH), FULL),
            pltpu.VMEM((tokens, WIDTH), FULL),
            pltpu.SemaphoreType.DMA((3,)),
        ],
        compiler_params=pltpu.CompilerParams(vmem_limit_bytes=56 << 20),
        cost_estimate=spent(0.5),
        name="front_back",
    )(me, table, d_qkv, scale1, small, n1, d_resid, *sources)


def unpack_kernel(arrived, frames, *rest):
    vectors, kernels, square = rest[:6], rest[6:9], rest[9]
    count, _, columns = arrived.shape
    columns -= 128
    total = jnp.zeros((ROWS, 128), FULL)
    for at in range(count):
        frames[:, at * columns : (at + 1) * columns] = arrived[at, :, 0:columns]
        total += arrived[at, :, columns : columns + 128].astype(FULL)
    square[...] = jnp.zeros_like(square)
    square[0:ROWS, :] = total
    sums = square[...].T
    sums = sums[0:16, :] + sums[16:32, :]
    for at, one in enumerate(vectors):
        one[...] = sums[at : at + 1, 0:ROWS]
    for at, one in zip((KERNEL_Q, KERNEL_K, KERNEL_V), kernels):
        one[...] = sums[at : at + 3, 0:ROWS]


def unpack(arrived):
    count, rows, columns = arrived.shape
    found = pl.pallas_call(
        unpack_kernel,
        in_specs=[VMEM],
        out_specs=[VMEM] * 10,
        out_shape=[shape(rows, count * (columns - 128), kind=LOW)]
        + [shape(1, rows)] * 6
        + [shape(3, rows)] * 3,
        scratch_shapes=[pltpu.VMEM((128, 128), FULL)],
        cost_estimate=spent(0.5),
        name="unpack",
    )(arrived)
    return found[0], [one.reshape(rows) for one in found[1:7]], [one.T for one in found[7:]]


def pack_kernel(
    gain1, shift1, scale_attn, gain2, shift2, scale_mlp, kernel_q, kernel_k, kernel_v,
    w_query, w_key, w_value, w_out, w_up, w_down,
    attn_shard, mlp_shard, table,
):
    table[...] = jnp.zeros_like(table)
    for at, one in enumerate((gain1, shift1, scale_attn, gain2, shift2, scale_mlp)):
        table[at : at + 1, 0:ROWS] = one[...].astype(FULL)
    for at, one in ((KERNEL_Q, kernel_q), (KERNEL_K, kernel_k), (KERNEL_V, kernel_v)):
        table[at : at + 3, 0:ROWS] = one[...].astype(FULL)
    attn_shard[4] = jnp.zeros((ROWS, WIDTH), LOW)
    attn_shard[4, :, 0:128] = table[...].T[0:ROWS, :].astype(LOW)
    for at, one in ((0, w_query), (1, w_key), (2, w_value), (3, w_out)):
        attn_shard[at] = one[...]
    for chunk in range(CHUNKS):
        mlp_shard[chunk] = w_up[:, chunk * WIDTH : (chunk + 1) * WIDTH]
        mlp_shard[CHUNKS + chunk] = w_down[chunk * ROWS : (chunk + 1) * ROWS, :]


def pack(vectors, kernels, matrices):
    return pl.pallas_call(
        pack_kernel,
        in_specs=[VMEM] * 15,
        out_specs=[VMEM] * 2,
        out_shape=[
            shape(5, ROWS, WIDTH, kind=LOW),
            shape(2 * CHUNKS, ROWS, WIDTH, kind=LOW),
        ],
        scratch_shapes=[pltpu.VMEM((128, 128), FULL)],
        name="pack",
    )(*[one.reshape(1, -1) for one in vectors], *[one.T for one in kernels], *matrices)


FIVE = 6


def permute(values, even, odd):
    count = lax.axis_size("dev")
    return lax.ppermute(
        values, "dev", [(at, at ^ (odd if at & 1 else even)) for at in range(count)]
    )


def after(first, *others):
    return lax.optimization_barrier((first,) + others)


def grown(blocks, even, odd, before=None):
    others = permute(blocks, even, odd)
    if before is not None:
        others = after(before, others)[1]
    return jnp.concatenate((blocks, others))


def upper(*parts):
    count = parts[-1].shape[0]
    return sum(one[count // 2 : count].astype(FULL) for one in parts).astype(LOW)


def step(before, parts, even, odd, late=False):
    if late:
        _, parts[-1] = after(before, parts[-1])
    sent = upper(*parts)
    if not late:
        before, sent = after(before, sent)
    return sent if late else before, parts + [permute(sent, even, odd)]


def finish_kernel(*refs):
    arrivals, outputs = refs[:FIVE], refs[FIVE:]
    done = 0
    for one in outputs:
        for at in range(one.shape[0] // ROWS * (one.shape[1] // WIDTH)):
            total = sum(more[0, done].astype(FULL) for more in arrivals)
            if one.shape[1] > WIDTH:
                one[:, at * WIDTH : (at + 1) * WIDTH] = total
            else:
                one[at * ROWS : (at + 1) * ROWS, :] = total
            done += 1


def finish(parts, shapes):
    spec = pl.BlockSpec((1,) + parts[0].shape[1:], lambda _: (0, 0, 0, 0))
    return pl.pallas_call(
        finish_kernel,
        grid=(1,),
        in_specs=[spec] * FIVE,
        out_specs=[pl.BlockSpec(one, lambda _: (0, 0)) for one in shapes],
        out_shape=[shape(*one) for one in shapes],
        cost_estimate=spent(0.5),
        name="finish",
    )(*parts)


def gather_plain(pieces):
    whole = [lax.all_gather(one, "dev", axis=0, tiled=True) for one in pieces]
    return jnp.stack([one.reshape(BLOCKS, ROWS, WIDTH) for one in whole], axis=1)


def places_plain():
    sides = ([0] * (BLOCKS // 2), [0] * (BLOCKS // 2))
    for block in range(BLOCKS):
        x, y, near_z, far_z = (block >> 1) & 1, (block >> 2) & 1, (block >> 3) & 1, block >> 4
        across = 8 * x + 4 * y if block & 1 else 8 * y + 4 * x
        sides[block & 1][across + 2 * near_z + far_z] = block
    return sides


def apart(blocks):
    return tuple(
        jnp.stack([blocks[k] for k in half])
        for side in places_plain()
        for half in (side[: BLOCKS // 4], side[BLOCKS // 4 :])
    )


def together(kept, sent):
    order = places_plain()
    found = {block: (side, at) for side in range(2) for at, block in enumerate(order[side])}
    return jnp.stack([(kept, sent)[found[k][0]][found[k][1]] for k in range(BLOCKS)])


def scatter_plain(matrix):
    return lax.psum_scatter(matrix.astype(FULL), "dev", scatter_dimension=0, tiled=True)


def local(
    frames,
    norm1_gain,
    norm1_shift,
    kernel_query,
    kernel_key,
    kernel_value,
    w_query,
    w_key,
    w_value,
    w_out,
    scale_attn,
    norm2_gain,
    norm2_shift,
    w_up,
    w_down,
    scale_mlp,
    cotangent,
):
    count = lax.axis_size("dev")
    own, columns = frames.shape[0], frames.shape[1] // count
    fast = own == ROWS and own * count == WIDTH
    vectors = (norm1_gain, norm1_shift, scale_attn, norm2_gain, norm2_shift, scale_mlp)
    kernels = (kernel_query, kernel_key, kernel_value)

    def to_crops(values):
        split = values.reshape(own, count, columns).transpose(1, 0, 2)
        return lax.all_to_all(split, "dev", 0, 0).reshape(WIDTH, columns)

    def to_devices(values):
        return lax.all_to_all(values.reshape(count, own, -1), "dev", 0, 0)

    def by_channels(blocks):
        return blocks.transpose(1, 0, 2).reshape(own, -1)

    matrices = (w_query, w_key, w_value, w_out)
    matrices = (w_query, w_key, w_value, w_out)
    x = to_crops(frames)
    if fast:
        me = lax.axis_index("dev").astype(jnp.int32).reshape(1)
        attn_shard, mlp_shard = pack(vectors, kernels, matrices + (w_up, w_down))
        blocks = grown(attn_shard[None], 16, 16)
        mlp_shard = after(blocks, mlp_shard)[1]
        blocks = grown(blocks, 8, 8)
        mlp_blocks = grown(mlp_shard[None], 16, 16, blocks)
        blocks = grown(blocks, 2, 4)
        cotangent = after(blocks, cotangent)[1]
        mlp_blocks = grown(mlp_blocks, 8, 8, blocks)
        others = permute(blocks, 4, 2)
        attn_sources = (blocks, others, permute(blocks, 1, 1), permute(others, 1, 1))
        mlp_blocks = grown(mlp_blocks, 2, 4, others)
        mlp_others = permute(mlp_blocks, 4, 2)
        x = after(mlp_blocks, x)[1]
    else:
        me = jnp.zeros((1,), jnp.int32)
        small = jnp.concatenate([one[:, None] for one in vectors] + list(kernels), axis=1)
        small = jnp.pad(small, ((0, 0), (0, WIDTH - small.shape[1])))
        attn_sources = apart(gather_plain(matrices + (small,)))
        ups = gather_plain([w_up[:, k * WIDTH : (k + 1) * WIDTH] for k in range(CHUNKS)])
        downs = lax.all_gather(w_down, "dev", axis=0, tiled=True)
        downs = downs.reshape(BLOCKS, CHUNKS, ROWS, WIDTH)
        mlp_sources = apart(jnp.concatenate((ups, downs), axis=1))
    cot = to_crops(cotangent)
    table, n1, scale1, conv, qkv, probs, heads, attn, resid, n2, scale2, normed2 = front(
        me, x, attn_sources
    )
    if fast:
        mlp_others = after(normed2, mlp_others)[1]
        mlp_sources = (
            mlp_blocks, mlp_others, permute(mlp_blocks, 1, 1), permute(mlp_others, 1, 1),
        )
    out, d_resid, d_attn, small, keep_mlp, send_mlp = mlp(
        me, cot, normed2, table, resid, n2, scale2, attn, mlp_sources
    )
    out = to_devices(out)
    if fast:
        mlp_parts = [keep_mlp, permute(send_mlp, 1, 1)]
        d_attn, mlp_parts = step(d_attn, mlp_parts, 4, 2)
    d_qkv, keep, send = attend_back(
        me, d_attn, heads, qkv, probs, conv, attn_sources
    )
    if fast:
        parts = [keep, permute(send, 1, 1)]
        now, mlp_parts = step(d_qkv, mlp_parts, 2, 4, True)
        now, parts = step(now, parts, 4, 2, True)
        _, d_qkv = after(now, d_qkv)
    both = front_back(me, table, d_qkv, scale1, small, n1, d_resid, attn_sources)
    arrived = to_devices(both)
    if fast:
        _, out = after(both, out)
        now, mlp_parts = step(both, mlp_parts, 8, 8, True)
        now, parts = step(now, parts, 2, 4, True)
        now, mlp_parts = step(now, mlp_parts, 16, 16, True)
        now, parts = step(now, parts, 8, 8, True)
        now, parts = step(now, parts, 16, 16, True)
        _, out = after(now, out)
        output = by_channels(out)
        _, mlp_parts[-1] = after(output, mlp_parts[-1])
        grad_up, grad_down = finish(mlp_parts, ((own, HIDDEN), (CHUNKS * own, WIDTH)))
        _, parts[-1] = after(grad_up, parts[-1])
        grad_query, grad_key, grad_value, grad_out = finish(parts, ((own, WIDTH),) * 4)
        _, arrived = after(grad_query, arrived)
        frames_grad, vector_grads, kernel_grads = unpack(arrived)
    else:
        output = by_channels(out)
        blocks = together(keep_mlp, send_mlp)
        ups = blocks[:, :CHUNKS].transpose(0, 2, 1, 3).reshape(WIDTH, HIDDEN)
        grad_up = scatter_plain(ups)
        grad_down = scatter_plain(blocks[:, CHUNKS:].reshape(HIDDEN, WIDTH))
        blocks = together(keep, send)
        grad_query, grad_key, grad_value, grad_out = (
            scatter_plain(blocks[:, k].reshape(WIDTH, WIDTH)) for k in range(4)
        )
        frames_grad = by_channels(arrived[:, :, :columns])
        sums = jnp.sum(arrived[:, :, columns:].astype(FULL), axis=0)
        sums = sums[:, 0:16] + sums[:, 16:32]
        vector_grads = [sums[:, k] for k in range(6)]
        kernel_grads = [sums[:, k : k + 3] for k in (KERNEL_Q, KERNEL_K, KERNEL_V)]
    return (
        output,
        frames_grad,
        vector_grads[GAIN1],
        vector_grads[SHIFT1],
        *kernel_grads,
        grad_query,
        grad_key,
        grad_value,
        grad_out,
        vector_grads[SCALE_ATTN],
        vector_grads[GAIN2],
        vector_grads[SHIFT2],
        grad_up,
        grad_down,
        vector_grads[SCALE_MLP],
    )


def solution(mesh):
    in_specs = (
        P("dev", None),
        P("dev"),
        P("dev"),
        P("dev", None),
        P("dev", None),
        P("dev", None),
        P("dev", None),
        P("dev", None),
        P("dev", None),
        P("dev", None),
        P("dev"),
        P("dev"),
        P("dev"),
        P("dev", None),
        P("dev", None),
        P("dev"),
        P("dev", None),
    )
    out_specs = (
        P("dev", None),
        P("dev", None),
        P("dev"),
        P("dev"),
        P("dev", None),
        P("dev", None),
        P("dev", None),
        P("dev", None),
        P("dev", None),
        P("dev", None),
        P("dev", None),
        P("dev"),
        P("dev"),
        P("dev"),
        P("dev", None),
        P("dev", None),
        P("dev"),
    )
    return jax.shard_map(local, mesh=mesh, in_specs=in_specs, out_specs=out_specs, check_vma=False)
```

```python
import functools
import math

import jax
import jax.numpy as jnp
from jax import lax
from jax.experimental import pallas as pl
from jax.experimental.pallas import tpu as pltpu
from jax.sharding import PartitionSpec as P

HEADS = 4
HEAD_DIM = 128
LENGTH = 160
WINDOW = 19
WIDTH = 512
HIDDEN = 2048
FACTOR = HEAD_DIM ** (-0.5)
EPSILON = 1e-05
ROWS = 16
BLOCKS = WIDTH // ROWS
CHUNKS = HIDDEN // WIDTH
LOW = jnp.bfloat16
FULL = jnp.float32

VMEM = pl.BlockSpec(memory_space=pltpu.VMEM)
ANY = pl.BlockSpec(memory_space=pl.ANY)
HBM = pl.BlockSpec(memory_space=pltpu.HBM)
SMEM = pl.BlockSpec(memory_space=pltpu.SMEM)

GAIN1, SHIFT1, SCALE_ATTN, GAIN2, SHIFT2, SCALE_MLP, KERNEL_Q, KERNEL_K, KERNEL_V = (
    0, 1, 2, 3, 4, 5, 6, 9, 12,
)


def nn(left, right):
    return jnp.dot(left, right, preferred_element_type=FULL)


def nt(left, right):
    return lax.dot_general(left, right, (((1,), (1,)), ((), ())), preferred_element_type=FULL)


def tn(left, right):
    return lax.dot_general(left, right, (((0,), (0,)), ((), ())), preferred_element_type=FULL)


def block_at(side, at, me):
    far = 16 * (at & 1) + 8 * (at >> 1 & 1)
    low, high = at >> 2 & 1, at >> 3
    first, second = 2 * low + 4 * high, 4 * low + 2 * high
    return me ^ (jnp.where((me & 1) ^ side == 0, first, second) + far + side)


def block_rows(block, rows=ROWS):
    return pl.ds(pl.multiple_of(block * rows, rows), rows)


def fetch_blocks(sources, me, pieces, copy_to):
    for piece, target in zip(pieces, copy_to):
        for number, source in enumerate(sources):
            for at in range(BLOCKS // 4):
                block = block_at(number // 2, number % 2 * (BLOCKS // 4) + at, me)
                into, sem = target(block)
                pltpu.make_async_copy(source.at[at, piece], into, sem).start()


def store_blocks(targets, me, piece, copy_from, sem):
    for side, target in enumerate(targets):
        for at in range(BLOCKS // 2):
            source = copy_from(block_at(side, at, me))
            pltpu.make_async_copy(source, target.at[at, piece], sem).start()


def whole_wait(ref, sem):
    pltpu.make_async_copy(ref, ref, sem).wait()


def move(source, target, sem):
    copy = pltpu.make_async_copy(source, target, sem)
    copy.start()
    return copy


def down_one(values):
    at = lax.broadcasted_iota(jnp.int32, values.shape, 0)
    return jnp.where(at == 0, 0.0, pltpu.roll(values, 1, 0))


def up_one(values):
    at = lax.broadcasted_iota(jnp.int32, values.shape, 0)
    last = values.shape[0] - 1
    return jnp.where(at == last, 0.0, pltpu.roll(values, last, 0))


def normalise(values):
    center = jnp.mean(values, axis=1, keepdims=True)
    centered = values - center
    scale = lax.rsqrt(jnp.mean(centered * centered, axis=1, keepdims=True) + EPSILON)
    return centered * scale, scale


def row(table, index):
    return table[index : index + 1, :]


def front_kernel(
    me_ref, x_ref, source0, source1, source2, source3,
    table_out, n1_out, scale1_out, conv_out, qkv_out, probs_out, heads_out, attn_out, resid_out,
    n2_out, scale2_out, normed2_out,
    weights, x_rows, table, n1, scale1, conv, qkv, probs, heads, attn, resid, n2, scale2, normed2,
    in_sem, sems,
):
    me = me_ref[0]
    tokens = x_ref.shape[1]
    crops = tokens // LENGTH
    copies = []

    def send(source, target):
        copies.append(move(source, target, sems.at[len(copies)]))

    fetch_blocks(
        (source0, source1, source2, source3), me, (slice(None),),
        (lambda block: (weights.at[:, block_rows(block)], in_sem.at[0]),),
    )
    for at in range(0, tokens, 128):
        x_rows[at : at + 128, :] = x_ref[:, at : at + 128].T.astype(FULL)

    def norm_one(at, carry):
        rows = pl.ds(pl.multiple_of(at * 80, 80), 80)
        n1[rows, :], scale1[rows, :] = normalise(x_rows[rows, :])
        return carry

    lax.fori_loop(0, tokens // 80, norm_one, 0, unroll=True)
    send(n1, n1_out)
    send(scale1, scale1_out)
    whole_wait(weights, in_sem.at[0])
    table[...] = weights[4, :, 0:128].astype(FULL).T[0:16, :]
    send(table, table_out)

    def convolve(crop, carry):
        rows = pl.ds(pl.multiple_of(crop * LENGTH, LENGTH), LENGTH)
        for at in range(0, WIDTH, 128):
            lanes = slice(at, at + 128)
            normed = n1[rows, lanes] * table[GAIN1 : GAIN1 + 1, lanes] + table[SHIFT1 : SHIFT1 + 1, lanes]
            before, after = down_one(normed), up_one(normed)
            for k, start in enumerate((KERNEL_Q, KERNEL_K, KERNEL_V)):
                conv[k, rows, lanes] = (
                    table[start : start + 1, lanes] * before
                    + table[start + 1 : start + 2, lanes] * normed
                    + table[start + 2 : start + 3, lanes] * after
                ).astype(LOW)
        return carry

    lax.fori_loop(0, crops, convolve, 0, unroll=True)
    send(conv, conv_out)
    for k in range(3):
        qkv[k] = nn(conv[k], weights[k]).astype(LOW)
    send(qkv, qkv_out)

    near_t = lax.broadcasted_iota(jnp.int32, (LENGTH, LENGTH), 0)
    near_u = lax.broadcasted_iota(jnp.int32, (LENGTH, LENGTH), 1)
    nearby = jnp.abs(near_t - near_u) <= WINDOW // 2

    def attend(crop, carry):
        rows = pl.ds(pl.multiple_of(crop * LENGTH, LENGTH), LENGTH)
        for h in range(HEADS):
            lanes = slice(h * HEAD_DIM, (h + 1) * HEAD_DIM)
            scores = jnp.where(nearby, nt(qkv[0, rows, lanes], qkv[1, rows, lanes]) * FACTOR, -1e30)
            powers = jnp.exp(scores - jnp.max(scores, axis=1, keepdims=True))
            shares = powers / jnp.sum(powers, axis=1, keepdims=True)
            probs[crop, h] = shares
            heads[rows, lanes] = nn(shares.astype(LOW), qkv[2, rows, lanes]).astype(LOW)
        return carry

    lax.fori_loop(0, crops, attend, 0, unroll=True)
    send(probs, probs_out)
    send(heads, heads_out)
    attn[...] = nn(heads[...], weights[3])
    send(attn, attn_out)

    def norm_two(at, carry):
        rows = pl.ds(pl.multiple_of(at * 80, 80), 80)
        mixed = x_rows[rows, :] + row(table, SCALE_ATTN) * attn[rows, :]
        resid[rows, :] = mixed
        normal, scale = normalise(mixed)
        n2[rows, :], scale2[rows, :] = normal, scale
        normed2[rows, :] = (normal * row(table, GAIN2) + row(table, SHIFT2)).astype(LOW)
        return carry

    lax.fori_loop(0, tokens // 80, norm_two, 0, unroll=True)
    send(normed2, normed2_out)
    send(resid, resid_out)
    send(n2, n2_out)
    send(scale2, scale2_out)
    for copy in copies:
        copy.wait()


def front(me, x, sources):
    tokens = x.shape[1]
    crops = tokens // LENGTH
    shapes = [
        shape(16, WIDTH),
        shape(tokens, WIDTH),
        shape(tokens, 1),
        shape(3, tokens, WIDTH, kind=LOW),
        shape(3, tokens, WIDTH, kind=LOW),
        shape(crops, HEADS, LENGTH, LENGTH),
        shape(tokens, WIDTH, kind=LOW),
        shape(tokens, WIDTH),
        shape(tokens, WIDTH),
        shape(tokens, WIDTH),
        shape(tokens, 1),
        shape(tokens, WIDTH, kind=LOW),
    ]
    return pl.pallas_call(
        front_kernel,
        in_specs=[SMEM, VMEM] + [ANY] * 4,
        out_specs=[HBM] * 12,
        out_shape=shapes,
        scratch_shapes=[
            pltpu.VMEM((5, WIDTH, WIDTH), LOW),
            pltpu.VMEM((tokens, WIDTH), FULL),
        ]
        + [pltpu.VMEM(one.shape, one.dtype) for one in shapes]
        + [pltpu.SemaphoreType.DMA((1,)), pltpu.SemaphoreType.DMA((12,))],
        compiler_params=pltpu.CompilerParams(vmem_limit_bytes=56 << 20),
        cost_estimate=spent(0.5),
        name="front",
    )(me, x, *sources)


def spent(microseconds):
    return pl.CostEstimate(flops=int(microseconds * 1.15e9), bytes_accessed=0, transcendentals=0)


def shape(*dims, kind=FULL):
    return jax.ShapeDtypeStruct(dims, kind)


def gelu_both(values):
    below = 0.5 + 0.5 * lax.erf(values * math.sqrt(0.5))
    bell = jnp.exp(-0.5 * values * values)
    return values * below, below + values * bell * (0.5 * math.sqrt(2 / math.pi))


def mlp_kernel(
    me_ref, cot_in, normed2_in, table, resid_in, n2_in, scale2_in, attn_in, source0, source1, source2, source3,
    out, d_resid_out, d_attn_out, small, keep, send,
    up, down, normed2_t, cot_rows, d_branch, branch, active, slope, d_hidden, d_normed2, grad_up,
    grad_down, resid, n2, scale2, attn, d_resid, d_attn, cot_ref, normed2, sems,
):
    me = me_ref[0]
    tokens = cot_ref.shape[1]
    first = move(normed2_in, normed2, sems.at[10])
    second = move(cot_in, cot_ref, sems.at[11])

    fetch_blocks(
        (source0, source1, source2, source3), me, (slice(0, CHUNKS), slice(CHUNKS, 2 * CHUNKS)),
        (
            lambda block: (up.at[:, block_rows(block)], sems.at[0]),
            lambda block: (down.at[block_rows(block, CHUNKS)], sems.at[1]),
        ),
    )
    scale_mlp = row(table, SCALE_MLP)
    first.wait()
    second.wait()
    for at in range(0, tokens, 128):
        rows = slice(at, at + 128)
        cot_rows[rows, :] = cot_ref[:, rows].T
        d_branch[rows, :] = (scale_mlp * cot_rows[rows, :].astype(FULL)).astype(LOW)
        normed2_t[:, rows] = normed2[rows, :].T
    whole_wait(up, sems.at[0])

    for chunk in range(CHUNKS):
        rows = slice(chunk * BLOCKS, (chunk + 1) * BLOCKS)
        hidden = nn(normed2[...], up[chunk])
        value, slope[...] = gelu_both(hidden)
        active[...] = value.astype(LOW)
        if chunk == 0:
            whole_wait(down, sems.at[1])
            arrivals = [
                move(source, target, sems.at[4 + at])
                for at, (source, target) in enumerate(
                    ((resid_in, resid), (n2_in, n2), (scale2_in, scale2), (attn_in, attn))
                )
            ]
        down_rows = down[rows].reshape(WIDTH, WIDTH)
        d_active = nt(d_branch[...], down_rows)
        d_hidden[...] = (d_active * slope[...]).astype(LOW)
        added = nn(active[...], down_rows)
        back = nt(d_hidden[...], up[chunk])
        branch[...] = added if chunk == 0 else branch[...] + added
        d_normed2[...] = back if chunk == 0 else d_normed2[...] + back
        grad_up[chunk] = nn(normed2_t[...], d_hidden[...]).astype(LOW)
        grad_down[rows] = tn(active[...], d_branch[...]).astype(LOW).reshape(BLOCKS, ROWS, WIDTH)

    store_blocks(
        (keep, send), me, slice(0, CHUNKS), lambda block: grad_up.at[:, block_rows(block)],
        sems.at[3],
    )
    store_blocks(
        (keep, send), me, slice(CHUNKS, 2 * CHUNKS),
        lambda block: grad_down.at[block_rows(block, CHUNKS)], sems.at[2],
    )
    for copy in arrivals:
        copy.wait()

    def norm_back(at, sums):
        rows = pl.ds(pl.multiple_of(at * 80, 80), 80)
        grad, normal, cot = d_normed2[rows, :], n2[rows, :], cot_rows[rows, :].astype(FULL)
        s = row(table, GAIN2) * grad
        along = jnp.mean(s * normal, axis=1, keepdims=True)
        middle = jnp.mean(s, axis=1, keepdims=True)
        total = cot + (s - middle - normal * along) * scale2[rows, :]
        d_resid[rows, :] = total
        d_attn[rows, :] = (row(table, SCALE_ATTN) * total).astype(LOW)
        terms = (grad * normal, grad, total * attn[rows, :], cot * branch[rows, :])
        return tuple(one + jnp.sum(more, axis=0, keepdims=True) for one, more in zip(sums, terms))

    sums = lax.fori_loop(0, tokens // 80, norm_back, (jnp.zeros((1, WIDTH), FULL),) * 4, unroll=True)
    leaving = [
        move(d_attn, d_attn_out, sems.at[8]),
        move(d_resid, d_resid_out, sems.at[9]),
    ]
    for at, one in enumerate(sums):
        small[at : at + 1, :] = one
    for at in range(0, tokens, 128):
        rows = slice(at, at + 128)
        out[:, rows] = (resid[rows, :] + scale_mlp * branch[rows, :]).astype(LOW).T
    whole_wait(grad_down, sems.at[2])
    whole_wait(grad_up, sems.at[3])
    for copy in leaving:
        copy.wait()


def mlp(me, cot, normed2, table, resid, n2, scale2, attn, sources):
    tokens = cot.shape[1]
    pieces = (BLOCKS // 2, 2 * CHUNKS, ROWS, WIDTH)
    rows_full, rows_low = pltpu.VMEM((tokens, WIDTH), FULL), pltpu.VMEM((tokens, WIDTH), LOW)
    return pl.pallas_call(
        mlp_kernel,
        in_specs=[SMEM, HBM, HBM, VMEM] + [HBM] * 4 + [ANY] * 4,
        out_specs=[VMEM, HBM, HBM, VMEM, HBM, HBM],
        out_shape=[
            shape(WIDTH, tokens, kind=LOW),
            shape(tokens, WIDTH),
            shape(tokens, WIDTH, kind=LOW),
            shape(8, WIDTH),
            shape(*pieces, kind=LOW),
            shape(*pieces, kind=LOW),
        ],
        scratch_shapes=[
            pltpu.VMEM((CHUNKS, WIDTH, WIDTH), LOW),
            pltpu.VMEM((HIDDEN // ROWS, ROWS, WIDTH), LOW),
            pltpu.VMEM((WIDTH, tokens), LOW),
            rows_low,
            rows_low,
            rows_full,
            rows_low,
            rows_full,
            rows_low,
            rows_full,
            pltpu.VMEM((CHUNKS, WIDTH, WIDTH), LOW),
            pltpu.VMEM((HIDDEN // ROWS, ROWS, WIDTH), LOW),
            rows_full,
            rows_full,
            pltpu.VMEM((tokens, 1), FULL),
            rows_full,
            rows_full,
            rows_low,
            pltpu.VMEM((WIDTH, tokens), LOW),
            rows_low,
            pltpu.SemaphoreType.DMA((12,)),
        ],
        compiler_params=pltpu.CompilerParams(vmem_limit_bytes=56 << 20),
        cost_estimate=spent(0.5),
        name="mlp",
    )(me, cot, normed2, table, resid, n2, scale2, attn, *sources)


def attend_back_kernel(
    me_ref, d_attn_in, heads_in, qkv_in, probs_in, conv_in, source0, source1, source2, source3,
    d_qkv_out, keep, send,
    w_out, d_attn, heads, qkv, probs, conv, d_heads, d_qkv, grads, sems,
):
    me = me_ref[0]
    crops = d_attn.shape[0] // LENGTH
    soon = [move(heads_in, heads, sems.at[3]), move(d_attn_in, d_attn, sems.at[4])]
    fetch_blocks(
        (source0, source1, source2, source3), me, (3,),
        (lambda block: (w_out.at[block_rows(block)], sems.at[0]),),
    )
    later = [move(qkv_in, qkv, sems.at[5]), move(probs_in, probs, sems.at[6])]
    for copy in soon:
        copy.wait()
    grads[3] = tn(heads[...], d_attn[...]).astype(LOW)
    whole_wait(w_out, sems.at[0])
    d_heads[...] = nt(d_attn[...], w_out[...]).astype(LOW)
    convs = move(conv_in, conv, sems.at[7])
    for copy in later:
        copy.wait()

    def attend(crop, carry):
        rows = pl.ds(pl.multiple_of(crop * LENGTH, LENGTH), LENGTH)
        for h in range(HEADS):
            lanes = slice(h * HEAD_DIM, (h + 1) * HEAD_DIM)
            shares, grad = probs[crop, h], d_heads[rows, lanes]
            d_probs = nt(grad, qkv[2, rows, lanes])
            d_qkv[2, rows, lanes] = tn(shares.astype(LOW), grad).astype(LOW)
            d_scores = shares * (d_probs - jnp.sum(shares * d_probs, axis=1, keepdims=True))
            d_scores = d_scores.astype(LOW)
            d_qkv[0, rows, lanes] = (nn(d_scores, qkv[1, rows, lanes]) * FACTOR).astype(LOW)
            d_qkv[1, rows, lanes] = (tn(d_scores, qkv[0, rows, lanes]) * FACTOR).astype(LOW)
        return carry

    lax.fori_loop(0, crops, attend, 0, unroll=True)
    leaving = move(d_qkv, d_qkv_out, sems.at[1])
    convs.wait()
    for k in range(3):
        grads[k] = tn(conv[k], d_qkv[k]).astype(LOW)
    store_blocks(
        (keep, send), me, slice(None), lambda block: grads.at[:, block_rows(block)], sems.at[2]
    )
    leaving.wait()
    whole_wait(grads, sems.at[2])


def attend_back(me, d_attn, heads, qkv, probs, conv, sources):
    tokens = heads.shape[0]
    pieces = (BLOCKS // 2, 4, ROWS, WIDTH)
    rows_low = pltpu.VMEM((tokens, WIDTH), LOW)
    return pl.pallas_call(
        attend_back_kernel,
        in_specs=[SMEM] + [HBM] * 5 + [ANY] * 4,
        out_specs=[HBM] * 3,
        out_shape=[
            shape(3, tokens, WIDTH, kind=LOW),
            shape(*pieces, kind=LOW),
            shape(*pieces, kind=LOW),
        ],
        scratch_shapes=[
            pltpu.VMEM((WIDTH, WIDTH), LOW),
            rows_low,
            rows_low,
            pltpu.VMEM(qkv.shape, LOW),
            pltpu.VMEM(probs.shape, FULL),
            pltpu.VMEM(conv.shape, LOW),
            rows_low,
            pltpu.VMEM(qkv.shape, LOW),
            pltpu.VMEM((4, WIDTH, WIDTH), LOW),
            pltpu.SemaphoreType.DMA((8,)),
        ],
        compiler_params=pltpu.CompilerParams(vmem_limit_bytes=56 << 20),
        cost_estimate=spent(10),
        name="attend_back",
    )(me, d_attn, heads, qkv, probs, conv, *sources)


def front_back_kernel(
    me_ref, table, small, d_qkv_in, n1_in, scale1_in, d_resid_in, source0, source1, source2, source3,
    both,
    weights, d_qkv, n1, scale1, d_resid, d_conv, sums, sems,
):
    me = me_ref[0]
    tokens = n1.shape[0]
    crops = tokens // LENGTH
    soon = move(d_qkv_in, d_qkv, sems.at[0])
    fetch_blocks(
        (source0, source1, source2, source3), me, (slice(0, 3),),
        (lambda block: (weights.at[:, block_rows(block)], sems.at[1]),),
    )
    later = [
        move(n1_in, n1, sems.at[2]),
        move(scale1_in, scale1, sems.at[3]),
        move(d_resid_in, d_resid, sems.at[4]),
    ]
    sums[...] = jnp.zeros_like(sums)
    soon.wait()
    whole_wait(weights, sems.at[1])
    for k in range(3):
        d_conv[k] = nt(d_qkv[k], weights[k])
    for copy in later:
        copy.wait()

    def back(crop, carry):
        rows = pl.ds(pl.multiple_of(crop * LENGTH, LENGTH), LENGTH)
        middle = jnp.zeros((LENGTH, 1), FULL)
        along = jnp.zeros((LENGTH, 1), FULL)
        for at in range(0, WIDTH, 128):
            lanes = slice(at, at + 128)
            gain = table[GAIN1 : GAIN1 + 1, lanes]
            normal = n1[rows, lanes]
            normed = normal * gain + table[SHIFT1 : SHIFT1 + 1, lanes]
            before, after = down_one(normed), up_one(normed)
            parts = [0.0, 0.0, 0.0]
            for k, start in enumerate((KERNEL_Q, KERNEL_K, KERNEL_V)):
                grad = d_conv[k, rows, lanes]
                for j, seen in enumerate((before, normed, after)):
                    sums[start + j : start + j + 1, lanes] += jnp.sum(grad * seen, axis=0, keepdims=True)
                    parts[j] = parts[j] + table[start + j : start + j + 1, lanes] * grad
            total = up_one(parts[0]) + parts[1] + down_one(parts[2])
            sums[GAIN1 : GAIN1 + 1, lanes] += jnp.sum(total * normal, axis=0, keepdims=True)
            sums[SHIFT1 : SHIFT1 + 1, lanes] += jnp.sum(total, axis=0, keepdims=True)
            s = gain * total
            d_conv[0, rows, lanes] = s
            middle += jnp.sum(s, axis=1, keepdims=True)
            along += jnp.sum(s * normal, axis=1, keepdims=True)
        middle, along = middle / WIDTH, along / WIDTH
        for at in range(0, WIDTH, 128):
            lanes = slice(at, at + 128)
            d_conv[1, rows, lanes] = d_resid[rows, lanes] + (
                d_conv[0, rows, lanes] - middle - n1[rows, lanes] * along
            ) * scale1[rows, :]
        return carry

    lax.fori_loop(0, crops, back, 0, unroll=True)
    for at in range(0, tokens, 128):
        both[:, at : at + 128] = d_conv[1, at : at + 128, :].astype(LOW).T
    sums[GAIN2 : SHIFT2 + 1, :] = small[0:2, :]
    sums[SCALE_ATTN : SCALE_ATTN + 1, :] = small[2:3, :]
    sums[SCALE_MLP : SCALE_MLP + 1, :] = small[3:4, :]
    high = sums[0:16, :].astype(LOW).astype(FULL)
    sums[16:32, :] = sums[0:16, :] - high
    both[:, tokens : tokens + 128] = sums[...].astype(LOW).T


def front_back(me, table, d_qkv, scale1, small, n1, d_resid, sources):
    tokens = n1.shape[0]
    rows_full = pltpu.VMEM((tokens, WIDTH), FULL)
    return pl.pallas_call(
        front_back_kernel,
        in_specs=[SMEM] + [VMEM] * 2 + [HBM] * 4 + [ANY] * 4,
        out_specs=VMEM,
        out_shape=shape(WIDTH, tokens + 128, kind=LOW),
        scratch_shapes=[
            pltpu.VMEM((3, WIDTH, WIDTH), LOW),
            pltpu.VMEM(d_qkv.shape, LOW),
            rows_full,
            pltpu.VMEM((tokens, 1), FULL),
            rows_full,
            pltpu.VMEM((3, tokens, WIDTH), FULL),
            pltpu.VMEM((128, WIDTH), FULL),
            pltpu.SemaphoreType.DMA((5,)),
        ],
        compiler_params=pltpu.CompilerParams(vmem_limit_bytes=56 << 20),
        cost_estimate=spent(8),
        name="front_back",
    )(me, table, small, d_qkv, n1, scale1, d_resid, *sources)


def unpack_kernel(arrived, frames, *rest):
    vectors, kernels, square = rest[:6], rest[6:9], rest[9]
    count, _, columns = arrived.shape
    columns -= 128
    total = jnp.zeros((ROWS, 128), FULL)
    for at in range(count):
        frames[:, at * columns : (at + 1) * columns] = arrived[at, :, 0:columns]
        total += arrived[at, :, columns : columns + 128].astype(FULL)
    square[...] = jnp.zeros_like(square)
    square[0:ROWS, :] = total
    sums = square[...].T
    sums = sums[0:16, :] + sums[16:32, :]
    for at, one in enumerate(vectors):
        one[...] = sums[at : at + 1, 0:ROWS]
    for at, one in zip((KERNEL_Q, KERNEL_K, KERNEL_V), kernels):
        one[...] = sums[at : at + 3, 0:ROWS]


def unpack(arrived):
    count, rows, columns = arrived.shape
    found = pl.pallas_call(
        unpack_kernel,
        in_specs=[VMEM],
        out_specs=[VMEM] * 10,
        out_shape=[shape(rows, count * (columns - 128), kind=LOW)]
        + [shape(1, rows)] * 6
        + [shape(3, rows)] * 3,
        scratch_shapes=[pltpu.VMEM((128, 128), FULL)],
        cost_estimate=spent(0.5),
        name="unpack",
    )(arrived)
    return found[0], [one.reshape(rows) for one in found[1:7]], [one.T for one in found[7:]]


def pack_kernel(
    gain1, shift1, scale_attn, gain2, shift2, scale_mlp, kernel_q, kernel_k, kernel_v,
    w_query, w_key, w_value, w_out, w_up, w_down,
    attn_shard, mlp_shard, table,
):
    table[...] = jnp.zeros_like(table)
    for at, one in enumerate((gain1, shift1, scale_attn, gain2, shift2, scale_mlp)):
        table[at : at + 1, 0:ROWS] = one[...].astype(FULL)
    for at, one in ((KERNEL_Q, kernel_q), (KERNEL_K, kernel_k), (KERNEL_V, kernel_v)):
        table[at : at + 3, 0:ROWS] = one[...].astype(FULL)
    attn_shard[4] = jnp.zeros((ROWS, WIDTH), LOW)
    attn_shard[4, :, 0:128] = table[...].T[0:ROWS, :].astype(LOW)
    for at, one in ((0, w_query), (1, w_key), (2, w_value), (3, w_out)):
        attn_shard[at] = one[...]
    for chunk in range(CHUNKS):
        mlp_shard[chunk] = w_up[:, chunk * WIDTH : (chunk + 1) * WIDTH]
        mlp_shard[CHUNKS + chunk] = w_down[chunk * ROWS : (chunk + 1) * ROWS, :]


def pack(vectors, kernels, matrices):
    return pl.pallas_call(
        pack_kernel,
        in_specs=[VMEM] * 15,
        out_specs=[VMEM] * 2,
        out_shape=[
            shape(5, ROWS, WIDTH, kind=LOW),
            shape(2 * CHUNKS, ROWS, WIDTH, kind=LOW),
        ],
        scratch_shapes=[pltpu.VMEM((128, 128), FULL)],
        name="pack",
    )(*[one.reshape(1, -1) for one in vectors], *[one.T for one in kernels], *matrices)


FIVE = 6


def permute(values, even, odd):
    count = lax.axis_size("dev")
    return lax.ppermute(
        values, "dev", [(at, at ^ (odd if at & 1 else even)) for at in range(count)]
    )


def after(first, *others):
    return lax.optimization_barrier((first,) + others)


def grown(blocks, even, odd, before=None):
    others = permute(blocks, even, odd)
    if before is not None:
        others = after(before, others)[1]
    return jnp.concatenate((blocks, others))


def upper(*parts):
    count = parts[-1].shape[0]
    return sum(one[count // 2 : count].astype(FULL) for one in parts).astype(LOW)


def step(before, parts, even, odd, late=False):
    if late:
        _, parts[-1] = after(before, parts[-1])
    sent = upper(*parts)
    if not late:
        before, sent = after(before, sent)
    return sent if late else before, parts + [permute(sent, even, odd)]


def finish_kernel(*refs):
    arrivals, outputs = refs[:FIVE], refs[FIVE:]
    done = 0
    for one in outputs:
        for at in range(one.shape[0] // ROWS * (one.shape[1] // WIDTH)):
            total = sum(more[0, done].astype(FULL) for more in arrivals)
            if one.shape[1] > WIDTH:
                one[:, at * WIDTH : (at + 1) * WIDTH] = total
            else:
                one[at * ROWS : (at + 1) * ROWS, :] = total
            done += 1


def finish(parts, shapes):
    spec = pl.BlockSpec((1,) + parts[0].shape[1:], lambda _: (0, 0, 0, 0))
    return pl.pallas_call(
        finish_kernel,
        grid=(1,),
        in_specs=[spec] * FIVE,
        out_specs=[pl.BlockSpec(one, lambda _: (0, 0)) for one in shapes],
        out_shape=[shape(*one) for one in shapes],
        cost_estimate=spent(0.5),
        name="finish",
    )(*parts)


def gather_plain(pieces):
    whole = [lax.all_gather(one, "dev", axis=0, tiled=True) for one in pieces]
    return jnp.stack([one.reshape(BLOCKS, ROWS, WIDTH) for one in whole], axis=1)


def places_plain():
    sides = ([0] * (BLOCKS // 2), [0] * (BLOCKS // 2))
    for block in range(BLOCKS):
        x, y, near_z, far_z = (block >> 1) & 1, (block >> 2) & 1, (block >> 3) & 1, block >> 4
        across = 8 * x + 4 * y if block & 1 else 8 * y + 4 * x
        sides[block & 1][across + 2 * near_z + far_z] = block
    return sides


def apart(blocks):
    return tuple(
        jnp.stack([blocks[k] for k in half])
        for side in places_plain()
        for half in (side[: BLOCKS // 4], side[BLOCKS // 4 :])
    )


def together(kept, sent):
    order = places_plain()
    found = {block: (side, at) for side in range(2) for at, block in enumerate(order[side])}
    return jnp.stack([(kept, sent)[found[k][0]][found[k][1]] for k in range(BLOCKS)])


def scatter_plain(matrix):
    return lax.psum_scatter(matrix.astype(FULL), "dev", scatter_dimension=0, tiled=True)


def local(
    frames,
    norm1_gain,
    norm1_shift,
    kernel_query,
    kernel_key,
    kernel_value,
    w_query,
    w_key,
    w_value,
    w_out,
    scale_attn,
    norm2_gain,
    norm2_shift,
    w_up,
    w_down,
    scale_mlp,
    cotangent,
):
    count = lax.axis_size("dev")
    own, columns = frames.shape[0], frames.shape[1] // count
    fast = own == ROWS and own * count == WIDTH
    vectors = (norm1_gain, norm1_shift, scale_attn, norm2_gain, norm2_shift, scale_mlp)
    kernels = (kernel_query, kernel_key, kernel_value)

    def to_crops(values):
        split = values.reshape(own, count, columns).transpose(1, 0, 2)
        return lax.all_to_all(split, "dev", 0, 0).reshape(WIDTH, columns)

    def to_devices(values):
        return lax.all_to_all(values.reshape(count, own, -1), "dev", 0, 0)

    def by_channels(blocks):
        return blocks.transpose(1, 0, 2).reshape(own, -1)

    matrices = (w_query, w_key, w_value, w_out)
    matrices = (w_query, w_key, w_value, w_out)
    x = to_crops(frames)
    if fast:
        me = lax.axis_index("dev").astype(jnp.int32).reshape(1)
        attn_shard, mlp_shard = pack(vectors, kernels, matrices + (w_up, w_down))
        blocks = grown(attn_shard[None], 16, 16)
        mlp_shard = after(blocks, mlp_shard)[1]
        blocks = grown(blocks, 8, 8)
        mlp_blocks = grown(mlp_shard[None], 16, 16, blocks)
        blocks = grown(blocks, 2, 4)
        cotangent = after(blocks, cotangent)[1]
        mlp_blocks = grown(mlp_blocks, 8, 8, blocks)
        others = permute(blocks, 4, 2)
        attn_sources = (blocks, others, permute(blocks, 1, 1), permute(others, 1, 1))
        mlp_blocks = grown(mlp_blocks, 2, 4, others)
        mlp_others = permute(mlp_blocks, 4, 2)
        x = after(mlp_blocks, x)[1]
    else:
        me = jnp.zeros((1,), jnp.int32)
        small = jnp.concatenate([one[:, None] for one in vectors] + list(kernels), axis=1)
        small = jnp.pad(small, ((0, 0), (0, WIDTH - small.shape[1])))
        attn_sources = apart(gather_plain(matrices + (small,)))
        ups = gather_plain([w_up[:, k * WIDTH : (k + 1) * WIDTH] for k in range(CHUNKS)])
        downs = lax.all_gather(w_down, "dev", axis=0, tiled=True)
        downs = downs.reshape(BLOCKS, CHUNKS, ROWS, WIDTH)
        mlp_sources = apart(jnp.concatenate((ups, downs), axis=1))
    cot = to_crops(cotangent)
    table, n1, scale1, conv, qkv, probs, heads, attn, resid, n2, scale2, normed2 = front(
        me, x, attn_sources
    )
    if fast:
        mlp_others = after(normed2, mlp_others)[1]
        mlp_sources = (
            mlp_blocks, mlp_others, permute(mlp_blocks, 1, 1), permute(mlp_others, 1, 1),
        )
    out, d_resid, d_attn, small, keep_mlp, send_mlp = mlp(
        me, cot, normed2, table, resid, n2, scale2, attn, mlp_sources
    )
    out = to_devices(out)
    if fast:
        mlp_parts = [keep_mlp, permute(send_mlp, 1, 1)]
        d_attn, mlp_parts = step(d_attn, mlp_parts, 4, 2)
    d_qkv, keep, send = attend_back(
        me, d_attn, heads, qkv, probs, conv, attn_sources
    )
    if fast:
        parts = [keep, permute(send, 1, 1)]
        now, mlp_parts = step(d_qkv, mlp_parts, 2, 4, True)
        now, parts = step(now, parts, 4, 2, True)
        _, d_qkv = after(now, d_qkv)
    both = front_back(me, table, d_qkv, scale1, small, n1, d_resid, attn_sources)
    arrived = to_devices(both)
    if fast:
        _, out = after(both, out)
        now, mlp_parts = step(both, mlp_parts, 8, 8, True)
        now, parts = step(now, parts, 2, 4, True)
        now, mlp_parts = step(now, mlp_parts, 16, 16, True)
        now, parts = step(now, parts, 8, 8, True)
        now, parts = step(now, parts, 16, 16, True)
        _, out = after(now, out)
        output = by_channels(out)
        _, mlp_parts[-1] = after(output, mlp_parts[-1])
        grad_up, grad_down = finish(mlp_parts, ((own, HIDDEN), (CHUNKS * own, WIDTH)))
        _, parts[-1] = after(grad_up, parts[-1])
        grad_query, grad_key, grad_value, grad_out = finish(parts, ((own, WIDTH),) * 4)
        _, arrived = after(grad_query, arrived)
        frames_grad, vector_grads, kernel_grads = unpack(arrived)
    else:
        output = by_channels(out)
        blocks = together(keep_mlp, send_mlp)
        ups = blocks[:, :CHUNKS].transpose(0, 2, 1, 3).reshape(WIDTH, HIDDEN)
        grad_up = scatter_plain(ups)
        grad_down = scatter_plain(blocks[:, CHUNKS:].reshape(HIDDEN, WIDTH))
        blocks = together(keep, send)
        grad_query, grad_key, grad_value, grad_out = (
            scatter_plain(blocks[:, k].reshape(WIDTH, WIDTH)) for k in range(4)
        )
        frames_grad = by_channels(arrived[:, :, :columns])
        sums = jnp.sum(arrived[:, :, columns:].astype(FULL), axis=0)
        sums = sums[:, 0:16] + sums[:, 16:32]
        vector_grads = [sums[:, k] for k in range(6)]
        kernel_grads = [sums[:, k : k + 3] for k in (KERNEL_Q, KERNEL_K, KERNEL_V)]
    return (
        output,
        frames_grad,
        vector_grads[GAIN1],
        vector_grads[SHIFT1],
        *kernel_grads,
        grad_query,
        grad_key,
        grad_value,
        grad_out,
        vector_grads[SCALE_ATTN],
        vector_grads[GAIN2],
        vector_grads[SHIFT2],
        grad_up,
        grad_down,
        vector_grads[SCALE_MLP],
    )


def solution(mesh):
    in_specs = (
        P("dev", None),
        P("dev"),
        P("dev"),
        P("dev", None),
        P("dev", None),
        P("dev", None),
        P("dev", None),
        P("dev", None),
        P("dev", None),
        P("dev", None),
        P("dev"),
        P("dev"),
        P("dev"),
        P("dev", None),
        P("dev", None),
        P("dev"),
        P("dev", None),
    )
    out_specs = (
        P("dev", None),
        P("dev", None),
        P("dev"),
        P("dev"),
        P("dev", None),
        P("dev", None),
        P("dev", None),
        P("dev", None),
        P("dev", None),
        P("dev", None),
        P("dev", None),
        P("dev"),
        P("dev"),
        P("dev"),
        P("dev", None),
        P("dev", None),
        P("dev"),
    )
    return jax.shard_map(local, mesh=mesh, in_specs=in_specs, out_specs=out_specs, check_vma=False)
```

```python
import functools
import math

import jax
import jax.numpy as jnp
from jax import lax
from jax.experimental import pallas as pl
from jax.experimental.pallas import tpu as pltpu
from jax.sharding import PartitionSpec as P

HEADS = 4
HEAD_DIM = 128
LENGTH = 160
WINDOW = 19
WIDTH = 512
HIDDEN = 2048
FACTOR = HEAD_DIM ** (-0.5)
EPSILON = 1e-05
ROWS = 16
BLOCKS = WIDTH // ROWS
CHUNKS = HIDDEN // WIDTH
LOW = jnp.bfloat16
FULL = jnp.float32

VMEM = pl.BlockSpec(memory_space=pltpu.VMEM)
ANY = pl.BlockSpec(memory_space=pl.ANY)
HBM = pl.BlockSpec(memory_space=pltpu.HBM)
SMEM = pl.BlockSpec(memory_space=pltpu.SMEM)

GAIN1, SHIFT1, SCALE_ATTN, GAIN2, SHIFT2, SCALE_MLP, KERNEL_Q, KERNEL_K, KERNEL_V = (
    0, 1, 2, 3, 4, 5, 6, 9, 12,
)


def nn(left, right):
    return jnp.dot(left, right, preferred_element_type=FULL)


def nt(left, right):
    return lax.dot_general(left, right, (((1,), (1,)), ((), ())), preferred_element_type=FULL)


def tn(left, right):
    return lax.dot_general(left, right, (((0,), (0,)), ((), ())), preferred_element_type=FULL)


def block_at(side, at, me):
    far = 16 * (at & 1) + 8 * (at >> 1 & 1)
    low, high = at >> 2 & 1, at >> 3
    first, second = 2 * low + 4 * high, 4 * low + 2 * high
    return me ^ (jnp.where((me & 1) ^ side == 0, first, second) + far + side)


def block_rows(block, rows=ROWS):
    return pl.ds(pl.multiple_of(block * rows, rows), rows)


def fetch_blocks(sources, me, pieces, copy_to):
    for piece, target in zip(pieces, copy_to):
        for number, source in enumerate(sources):
            for at in range(BLOCKS // 4):
                block = block_at(number // 2, number % 2 * (BLOCKS // 4) + at, me)
                into, sem = target(block)
                pltpu.make_async_copy(source.at[at, piece], into, sem).start()


def store_blocks(targets, me, piece, copy_from, sem):
    keep, *sends = targets
    for side in range(2):
        for at in range(BLOCKS // 2):
            source = copy_from(block_at(side, at, me))
            half = BLOCKS // 4
            target = sends[at // half].at[at % half, piece] if side else keep.at[at, piece]
            pltpu.make_async_copy(source, target, sem).start()


def whole_wait(ref, sem):
    pltpu.make_async_copy(ref, ref, sem).wait()


def move(source, target, sem):
    copy = pltpu.make_async_copy(source, target, sem)
    copy.start()
    return copy


def down_one(values):
    at = lax.broadcasted_iota(jnp.int32, values.shape, 0)
    return jnp.where(at == 0, 0.0, pltpu.roll(values, 1, 0))


def up_one(values):
    at = lax.broadcasted_iota(jnp.int32, values.shape, 0)
    last = values.shape[0] - 1
    return jnp.where(at == last, 0.0, pltpu.roll(values, last, 0))


def normalise(values):
    center = jnp.mean(values, axis=1, keepdims=True)
    centered = values - center
    scale = lax.rsqrt(jnp.mean(centered * centered, axis=1, keepdims=True) + EPSILON)
    return centered * scale, scale


def row(table, index):
    return table[index : index + 1, :]


def front_kernel(
    me_ref, x_ref, source0, source1, source2, source3,
    table_out, n1_out, scale1_out, conv_out, qkv_out, probs_out, heads_out, attn_out, resid_out,
    n2_out, scale2_out, normed2_out,
    weights, x_rows, table, n1, scale1, conv, qkv, probs, heads, attn, resid, n2, scale2, normed2,
    in_sem, sems,
):
    me = me_ref[0]
    tokens = x_ref.shape[1]
    crops = tokens // LENGTH
    copies = []

    def send(source, target):
        copies.append(move(source, target, sems.at[len(copies)]))

    fetch_blocks(
        (source0, source1, source2, source3), me, (slice(None),),
        (lambda block: (weights.at[:, block_rows(block)], in_sem.at[0]),),
    )
    for at in range(0, tokens, 128):
        x_rows[at : at + 128, :] = x_ref[:, at : at + 128].T.astype(FULL)

    def norm_one(at, carry):
        rows = pl.ds(pl.multiple_of(at * 80, 80), 80)
        n1[rows, :], scale1[rows, :] = normalise(x_rows[rows, :])
        return carry

    lax.fori_loop(0, tokens // 80, norm_one, 0, unroll=True)
    send(n1, n1_out)
    send(scale1, scale1_out)
    whole_wait(weights, in_sem.at[0])
    table[...] = weights[4, :, 0:128].astype(FULL).T[0:16, :]
    send(table, table_out)

    def convolve(crop, carry):
        rows = pl.ds(pl.multiple_of(crop * LENGTH, LENGTH), LENGTH)
        for at in range(0, WIDTH, 128):
            lanes = slice(at, at + 128)
            normed = n1[rows, lanes] * table[GAIN1 : GAIN1 + 1, lanes] + table[SHIFT1 : SHIFT1 + 1, lanes]
            before, after = down_one(normed), up_one(normed)
            for k, start in enumerate((KERNEL_Q, KERNEL_K, KERNEL_V)):
                conv[k, rows, lanes] = (
                    table[start : start + 1, lanes] * before
                    + table[start + 1 : start + 2, lanes] * normed
                    + table[start + 2 : start + 3, lanes] * after
                ).astype(LOW)
        return carry

    lax.fori_loop(0, crops, convolve, 0, unroll=True)
    send(conv, conv_out)
    for k in range(3):
        qkv[k] = nn(conv[k], weights[k]).astype(LOW)
    send(qkv, qkv_out)

    near_t = lax.broadcasted_iota(jnp.int32, (LENGTH, LENGTH), 0)
    near_u = lax.broadcasted_iota(jnp.int32, (LENGTH, LENGTH), 1)
    nearby = jnp.abs(near_t - near_u) <= WINDOW // 2

    def attend(crop, carry):
        rows = pl.ds(pl.multiple_of(crop * LENGTH, LENGTH), LENGTH)
        for h in range(HEADS):
            lanes = slice(h * HEAD_DIM, (h + 1) * HEAD_DIM)
            scores = jnp.where(nearby, nt(qkv[0, rows, lanes], qkv[1, rows, lanes]) * FACTOR, -1e30)
            powers = jnp.exp(scores - jnp.max(scores, axis=1, keepdims=True))
            shares = powers / jnp.sum(powers, axis=1, keepdims=True)
            probs[crop, h] = shares
            heads[rows, lanes] = nn(shares.astype(LOW), qkv[2, rows, lanes]).astype(LOW)
        return carry

    lax.fori_loop(0, crops, attend, 0, unroll=True)
    send(probs, probs_out)
    send(heads, heads_out)
    attn[...] = nn(heads[...], weights[3])
    send(attn, attn_out)

    def norm_two(at, carry):
        rows = pl.ds(pl.multiple_of(at * 80, 80), 80)
        mixed = x_rows[rows, :] + row(table, SCALE_ATTN) * attn[rows, :]
        resid[rows, :] = mixed
        normal, scale = normalise(mixed)
        n2[rows, :], scale2[rows, :] = normal, scale
        normed2[rows, :] = (normal * row(table, GAIN2) + row(table, SHIFT2)).astype(LOW)
        return carry

    lax.fori_loop(0, tokens // 80, norm_two, 0, unroll=True)
    send(normed2, normed2_out)
    send(resid, resid_out)
    send(n2, n2_out)
    send(scale2, scale2_out)
    for copy in copies:
        copy.wait()


def front(me, x, sources):
    tokens = x.shape[1]
    crops = tokens // LENGTH
    shapes = [
        shape(16, WIDTH),
        shape(tokens, WIDTH),
        shape(tokens, 1),
        shape(3, tokens, WIDTH, kind=LOW),
        shape(3, tokens, WIDTH, kind=LOW),
        shape(crops, HEADS, LENGTH, LENGTH),
        shape(tokens, WIDTH, kind=LOW),
        shape(tokens, WIDTH),
        shape(tokens, WIDTH),
        shape(tokens, WIDTH),
        shape(tokens, 1),
        shape(tokens, WIDTH, kind=LOW),
    ]
    return pl.pallas_call(
        front_kernel,
        in_specs=[SMEM, VMEM] + [ANY] * 4,
        out_specs=[HBM] * 12,
        out_shape=shapes,
        scratch_shapes=[
            pltpu.VMEM((5, WIDTH, WIDTH), LOW),
            pltpu.VMEM((tokens, WIDTH), FULL),
        ]
        + [pltpu.VMEM(one.shape, one.dtype) for one in shapes]
        + [pltpu.SemaphoreType.DMA((1,)), pltpu.SemaphoreType.DMA((12,))],
        compiler_params=pltpu.CompilerParams(vmem_limit_bytes=56 << 20),
        cost_estimate=spent(0.5),
        name="front",
    )(me, x, *sources)


def spent(microseconds):
    return pl.CostEstimate(flops=int(microseconds * 1.15e9), bytes_accessed=0, transcendentals=0)


def shape(*dims, kind=FULL):
    return jax.ShapeDtypeStruct(dims, kind)


def gelu_both(values):
    below = 0.5 + 0.5 * lax.erf(values * math.sqrt(0.5))
    bell = jnp.exp(-0.5 * values * values)
    return values * below, below + values * bell * (0.5 * math.sqrt(2 / math.pi))


def mlp_kernel(
    me_ref, cot_in, normed2_in, table, resid_in, n2_in, scale2_in, attn_in, source0, source1, source2, source3,
    out, d_resid_out, d_attn_out, small, keep, send_low, send_high,
    up, down, normed2_t, cot_rows, d_branch, branch, active, slope, d_hidden, d_normed2, grad_up,
    grad_down, resid, n2, scale2, attn, d_resid, d_attn, cot_ref, normed2, sems,
):
    me = me_ref[0]
    tokens = cot_ref.shape[1]
    first = move(normed2_in, normed2, sems.at[10])
    second = move(cot_in, cot_ref, sems.at[11])

    fetch_blocks(
        (source0, source1, source2, source3), me, (slice(0, CHUNKS), slice(CHUNKS, 2 * CHUNKS)),
        (
            lambda block: (up.at[:, block_rows(block)], sems.at[0]),
            lambda block: (down.at[block_rows(block, CHUNKS)], sems.at[1]),
        ),
    )
    scale_mlp = row(table, SCALE_MLP)
    first.wait()
    second.wait()
    for at in range(0, tokens, 128):
        rows = slice(at, at + 128)
        cot_rows[rows, :] = cot_ref[:, rows].T
        d_branch[rows, :] = (scale_mlp * cot_rows[rows, :].astype(FULL)).astype(LOW)
        normed2_t[:, rows] = normed2[rows, :].T
    whole_wait(up, sems.at[0])

    for chunk in range(CHUNKS):
        rows = slice(chunk * BLOCKS, (chunk + 1) * BLOCKS)
        hidden = nn(normed2[...], up[chunk])
        value, slope[...] = gelu_both(hidden)
        active[...] = value.astype(LOW)
        if chunk == 0:
            whole_wait(down, sems.at[1])
            arrivals = [
                move(source, target, sems.at[4 + at])
                for at, (source, target) in enumerate(
                    ((resid_in, resid), (n2_in, n2), (scale2_in, scale2), (attn_in, attn))
                )
            ]
        down_rows = down[rows].reshape(WIDTH, WIDTH)
        d_active = nt(d_branch[...], down_rows)
        d_hidden[...] = (d_active * slope[...]).astype(LOW)
        added = nn(active[...], down_rows)
        back = nt(d_hidden[...], up[chunk])
        branch[...] = added if chunk == 0 else branch[...] + added
        d_normed2[...] = back if chunk == 0 else d_normed2[...] + back
        grad_up[chunk] = nn(normed2_t[...], d_hidden[...]).astype(LOW)
        grad_down[rows] = tn(active[...], d_branch[...]).astype(LOW).reshape(BLOCKS, ROWS, WIDTH)

    store_blocks(
        (keep, send_low, send_high), me, slice(0, CHUNKS), lambda block: grad_up.at[:, block_rows(block)],
        sems.at[3],
    )
    store_blocks(
        (keep, send_low, send_high), me, slice(CHUNKS, 2 * CHUNKS),
        lambda block: grad_down.at[block_rows(block, CHUNKS)], sems.at[2],
    )
    for copy in arrivals:
        copy.wait()

    def norm_back(at, sums):
        rows = pl.ds(pl.multiple_of(at * 80, 80), 80)
        grad, normal, cot = d_normed2[rows, :], n2[rows, :], cot_rows[rows, :].astype(FULL)
        s = row(table, GAIN2) * grad
        along = jnp.mean(s * normal, axis=1, keepdims=True)
        middle = jnp.mean(s, axis=1, keepdims=True)
        total = cot + (s - middle - normal * along) * scale2[rows, :]
        d_resid[rows, :] = total
        d_attn[rows, :] = (row(table, SCALE_ATTN) * total).astype(LOW)
        terms = (grad * normal, grad, total * attn[rows, :], cot * branch[rows, :])
        return tuple(one + jnp.sum(more, axis=0, keepdims=True) for one, more in zip(sums, terms))

    sums = lax.fori_loop(0, tokens // 80, norm_back, (jnp.zeros((1, WIDTH), FULL),) * 4, unroll=True)
    leaving = [
        move(d_attn, d_attn_out, sems.at[8]),
        move(d_resid, d_resid_out, sems.at[9]),
    ]
    for at, one in enumerate(sums):
        small[at : at + 1, :] = one
    for at in range(0, tokens, 128):
        rows = slice(at, at + 128)
        out[:, rows] = (resid[rows, :] + scale_mlp * branch[rows, :]).astype(LOW).T
    whole_wait(grad_down, sems.at[2])
    whole_wait(grad_up, sems.at[3])
    for copy in leaving:
        copy.wait()


def mlp(me, cot, normed2, table, resid, n2, scale2, attn, sources):
    tokens = cot.shape[1]
    pieces = (BLOCKS // 2, 2 * CHUNKS, ROWS, WIDTH)
    halves = (BLOCKS // 4,) + pieces[1:]
    rows_full, rows_low = pltpu.VMEM((tokens, WIDTH), FULL), pltpu.VMEM((tokens, WIDTH), LOW)
    return pl.pallas_call(
        mlp_kernel,
        in_specs=[SMEM, HBM, HBM, VMEM] + [HBM] * 4 + [ANY] * 4,
        out_specs=[VMEM, HBM, HBM, VMEM, HBM, HBM, HBM],
        out_shape=[
            shape(WIDTH, tokens, kind=LOW),
            shape(tokens, WIDTH),
            shape(tokens, WIDTH, kind=LOW),
            shape(8, WIDTH),
            shape(*pieces, kind=LOW),
            shape(*halves, kind=LOW),
            shape(*halves, kind=LOW),
        ],
        scratch_shapes=[
            pltpu.VMEM((CHUNKS, WIDTH, WIDTH), LOW),
            pltpu.VMEM((HIDDEN // ROWS, ROWS, WIDTH), LOW),
            pltpu.VMEM((WIDTH, tokens), LOW),
            rows_low,
            rows_low,
            rows_full,
            rows_low,
            rows_full,
            rows_low,
            rows_full,
            pltpu.VMEM((CHUNKS, WIDTH, WIDTH), LOW),
            pltpu.VMEM((HIDDEN // ROWS, ROWS, WIDTH), LOW),
            rows_full,
            rows_full,
            pltpu.VMEM((tokens, 1), FULL),
            rows_full,
            rows_full,
            rows_low,
            pltpu.VMEM((WIDTH, tokens), LOW),
            rows_low,
            pltpu.SemaphoreType.DMA((12,)),
        ],
        compiler_params=pltpu.CompilerParams(vmem_limit_bytes=56 << 20),
        cost_estimate=spent(0.5),
        name="mlp",
    )(me, cot, normed2, table, resid, n2, scale2, attn, *sources)


def attend_back_kernel(
    me_ref, d_attn_in, heads_in, qkv_in, probs_in, conv_in, source0, source1, source2, source3,
    d_qkv_out, keep, send_low, send_high,
    w_out, d_attn, heads, qkv, probs, conv, d_heads, d_qkv, grads, sems,
):
    me = me_ref[0]
    crops = d_attn.shape[0] // LENGTH
    soon = [move(heads_in, heads, sems.at[3]), move(d_attn_in, d_attn, sems.at[4])]
    fetch_blocks(
        (source0, source1, source2, source3), me, (3,),
        (lambda block: (w_out.at[block_rows(block)], sems.at[0]),),
    )
    later = [move(qkv_in, qkv, sems.at[5]), move(probs_in, probs, sems.at[6])]
    for copy in soon:
        copy.wait()
    grads[3] = tn(heads[...], d_attn[...]).astype(LOW)
    whole_wait(w_out, sems.at[0])
    d_heads[...] = nt(d_attn[...], w_out[...]).astype(LOW)
    convs = move(conv_in, conv, sems.at[7])
    for copy in later:
        copy.wait()

    def attend(crop, carry):
        rows = pl.ds(pl.multiple_of(crop * LENGTH, LENGTH), LENGTH)
        for h in range(HEADS):
            lanes = slice(h * HEAD_DIM, (h + 1) * HEAD_DIM)
            shares, grad = probs[crop, h], d_heads[rows, lanes]
            d_probs = nt(grad, qkv[2, rows, lanes])
            d_qkv[2, rows, lanes] = tn(shares.astype(LOW), grad).astype(LOW)
            d_scores = shares * (d_probs - jnp.sum(shares * d_probs, axis=1, keepdims=True))
            d_scores = d_scores.astype(LOW)
            d_qkv[0, rows, lanes] = (nn(d_scores, qkv[1, rows, lanes]) * FACTOR).astype(LOW)
            d_qkv[1, rows, lanes] = (tn(d_scores, qkv[0, rows, lanes]) * FACTOR).astype(LOW)
        return carry

    lax.fori_loop(0, crops, attend, 0, unroll=True)
    leaving = move(d_qkv, d_qkv_out, sems.at[1])
    convs.wait()
    for k in range(3):
        grads[k] = tn(conv[k], d_qkv[k]).astype(LOW)
    store_blocks(
        (keep, send_low, send_high), me, slice(None), lambda block: grads.at[:, block_rows(block)], sems.at[2]
    )
    leaving.wait()
    whole_wait(grads, sems.at[2])


def attend_back(me, d_attn, heads, qkv, probs, conv, sources):
    tokens = heads.shape[0]
    pieces = (BLOCKS // 2, 4, ROWS, WIDTH)
    halves = (BLOCKS // 4,) + pieces[1:]
    rows_low = pltpu.VMEM((tokens, WIDTH), LOW)
    return pl.pallas_call(
        attend_back_kernel,
        in_specs=[SMEM] + [HBM] * 5 + [ANY] * 4,
        out_specs=[HBM] * 4,
        out_shape=[
            shape(3, tokens, WIDTH, kind=LOW),
            shape(*pieces, kind=LOW),
            shape(*halves, kind=LOW),
            shape(*halves, kind=LOW),
        ],
        scratch_shapes=[
            pltpu.VMEM((WIDTH, WIDTH), LOW),
            rows_low,
            rows_low,
            pltpu.VMEM(qkv.shape, LOW),
            pltpu.VMEM(probs.shape, FULL),
            pltpu.VMEM(conv.shape, LOW),
            rows_low,
            pltpu.VMEM(qkv.shape, LOW),
            pltpu.VMEM((4, WIDTH, WIDTH), LOW),
            pltpu.SemaphoreType.DMA((8,)),
        ],
        compiler_params=pltpu.CompilerParams(vmem_limit_bytes=56 << 20),
        cost_estimate=spent(10),
        name="attend_back",
    )(me, d_attn, heads, qkv, probs, conv, *sources)


def front_back_kernel(
    me_ref, table, small, d_qkv_in, n1_in, scale1_in, d_resid_in, source0, source1, source2, source3,
    both,
    weights, d_qkv, n1, scale1, d_resid, d_conv, sums, sems,
):
    me = me_ref[0]
    tokens = n1.shape[0]
    crops = tokens // LENGTH
    soon = move(d_qkv_in, d_qkv, sems.at[0])
    fetch_blocks(
        (source0, source1, source2, source3), me, (slice(0, 3),),
        (lambda block: (weights.at[:, block_rows(block)], sems.at[1]),),
    )
    later = [
        move(n1_in, n1, sems.at[2]),
        move(scale1_in, scale1, sems.at[3]),
        move(d_resid_in, d_resid, sems.at[4]),
    ]
    sums[...] = jnp.zeros_like(sums)
    soon.wait()
    whole_wait(weights, sems.at[1])
    for k in range(3):
        d_conv[k] = nt(d_qkv[k], weights[k])
    for copy in later:
        copy.wait()

    def back(crop, carry):
        rows = pl.ds(pl.multiple_of(crop * LENGTH, LENGTH), LENGTH)
        middle = jnp.zeros((LENGTH, 1), FULL)
        along = jnp.zeros((LENGTH, 1), FULL)
        for at in range(0, WIDTH, 128):
            lanes = slice(at, at + 128)
            gain = table[GAIN1 : GAIN1 + 1, lanes]
            normal = n1[rows, lanes]
            normed = normal * gain + table[SHIFT1 : SHIFT1 + 1, lanes]
            before, after = down_one(normed), up_one(normed)
            parts = [0.0, 0.0, 0.0]
            for k, start in enumerate((KERNEL_Q, KERNEL_K, KERNEL_V)):
                grad = d_conv[k, rows, lanes]
                for j, seen in enumerate((before, normed, after)):
                    sums[start + j : start + j + 1, lanes] += jnp.sum(grad * seen, axis=0, keepdims=True)
                    parts[j] = parts[j] + table[start + j : start + j + 1, lanes] * grad
            total = up_one(parts[0]) + parts[1] + down_one(parts[2])
            sums[GAIN1 : GAIN1 + 1, lanes] += jnp.sum(total * normal, axis=0, keepdims=True)
            sums[SHIFT1 : SHIFT1 + 1, lanes] += jnp.sum(total, axis=0, keepdims=True)
            s = gain * total
            d_conv[0, rows, lanes] = s
            middle += jnp.sum(s, axis=1, keepdims=True)
            along += jnp.sum(s * normal, axis=1, keepdims=True)
        middle, along = middle / WIDTH, along / WIDTH
        for at in range(0, WIDTH, 128):
            lanes = slice(at, at + 128)
            d_conv[1, rows, lanes] = d_resid[rows, lanes] + (
                d_conv[0, rows, lanes] - middle - n1[rows, lanes] * along
            ) * scale1[rows, :]
        return carry

    lax.fori_loop(0, crops, back, 0, unroll=True)
    for at in range(0, tokens, 128):
        both[:, at : at + 128] = d_conv[1, at : at + 128, :].astype(LOW).T
    sums[GAIN2 : SHIFT2 + 1, :] = small[0:2, :]
    sums[SCALE_ATTN : SCALE_ATTN + 1, :] = small[2:3, :]
    sums[SCALE_MLP : SCALE_MLP + 1, :] = small[3:4, :]
    high = sums[0:16, :].astype(LOW).astype(FULL)
    sums[16:32, :] = sums[0:16, :] - high
    both[:, tokens : tokens + 128] = sums[...].astype(LOW).T


def front_back(me, table, d_qkv, scale1, small, n1, d_resid, sources):
    tokens = n1.shape[0]
    rows_full = pltpu.VMEM((tokens, WIDTH), FULL)
    return pl.pallas_call(
        front_back_kernel,
        in_specs=[SMEM] + [VMEM] * 2 + [HBM] * 4 + [ANY] * 4,
        out_specs=VMEM,
        out_shape=shape(WIDTH, tokens + 128, kind=LOW),
        scratch_shapes=[
            pltpu.VMEM((3, WIDTH, WIDTH), LOW),
            pltpu.VMEM(d_qkv.shape, LOW),
            rows_full,
            pltpu.VMEM((tokens, 1), FULL),
            rows_full,
            pltpu.VMEM((3, tokens, WIDTH), FULL),
            pltpu.VMEM((128, WIDTH), FULL),
            pltpu.SemaphoreType.DMA((5,)),
        ],
        compiler_params=pltpu.CompilerParams(vmem_limit_bytes=56 << 20),
        cost_estimate=spent(8),
        name="front_back",
    )(me, table, small, d_qkv, n1, scale1, d_resid, *sources)


def unpack_kernel(arrived, frames, *rest):
    vectors, kernels, square = rest[:6], rest[6:9], rest[9]
    count, _, columns = arrived.shape
    columns -= 128
    total = jnp.zeros((ROWS, 128), FULL)
    for at in range(count):
        frames[:, at * columns : (at + 1) * columns] = arrived[at, :, 0:columns]
        total += arrived[at, :, columns : columns + 128].astype(FULL)
    square[...] = jnp.zeros_like(square)
    square[0:ROWS, :] = total
    sums = square[...].T
    sums = sums[0:16, :] + sums[16:32, :]
    for at, one in enumerate(vectors):
        one[...] = sums[at : at + 1, 0:ROWS]
    for at, one in zip((KERNEL_Q, KERNEL_K, KERNEL_V), kernels):
        one[...] = sums[at : at + 3, 0:ROWS]


def unpack(arrived):
    count, rows, columns = arrived.shape
    found = pl.pallas_call(
        unpack_kernel,
        in_specs=[VMEM],
        out_specs=[VMEM] * 10,
        out_shape=[shape(rows, count * (columns - 128), kind=LOW)]
        + [shape(1, rows)] * 6
        + [shape(3, rows)] * 3,
        scratch_shapes=[pltpu.VMEM((128, 128), FULL)],
        cost_estimate=spent(0.5),
        name="unpack",
    )(arrived)
    return found[0], [one.reshape(rows) for one in found[1:7]], [one.T for one in found[7:]]


def pack_kernel(
    gain1, shift1, scale_attn, gain2, shift2, scale_mlp, kernel_q, kernel_k, kernel_v,
    w_query, w_key, w_value, w_out, w_up, w_down,
    attn_shard, mlp_shard, table,
):
    table[...] = jnp.zeros_like(table)
    for at, one in enumerate((gain1, shift1, scale_attn, gain2, shift2, scale_mlp)):
        table[at : at + 1, 0:ROWS] = one[...].astype(FULL)
    for at, one in ((KERNEL_Q, kernel_q), (KERNEL_K, kernel_k), (KERNEL_V, kernel_v)):
        table[at : at + 3, 0:ROWS] = one[...].astype(FULL)
    attn_shard[4] = jnp.zeros((ROWS, WIDTH), LOW)
    attn_shard[4, :, 0:128] = table[...].T[0:ROWS, :].astype(LOW)
    for at, one in ((0, w_query), (1, w_key), (2, w_value), (3, w_out)):
        attn_shard[at] = one[...]
    for chunk in range(CHUNKS):
        mlp_shard[chunk] = w_up[:, chunk * WIDTH : (chunk + 1) * WIDTH]
        mlp_shard[CHUNKS + chunk] = w_down[chunk * ROWS : (chunk + 1) * ROWS, :]


def pack(vectors, kernels, matrices):
    return pl.pallas_call(
        pack_kernel,
        in_specs=[VMEM] * 15,
        out_specs=[VMEM] * 2,
        out_shape=[
            shape(5, ROWS, WIDTH, kind=LOW),
            shape(2 * CHUNKS, ROWS, WIDTH, kind=LOW),
        ],
        scratch_shapes=[pltpu.VMEM((128, 128), FULL)],
        name="pack",
    )(*[one.reshape(1, -1) for one in vectors], *[one.T for one in kernels], *matrices)


FIVE = 6


def permute(values, even, odd):
    count = lax.axis_size("dev")
    return lax.ppermute(
        values, "dev", [(at, at ^ (odd if at & 1 else even)) for at in range(count)]
    )


def after(first, *others):
    return lax.optimization_barrier((first,) + others)


def grown(blocks, even, odd, before=None):
    others = permute(blocks, even, odd)
    if before is not None:
        others = after(before, others)[1]
    return jnp.concatenate((blocks, others))


def upper(*parts):
    count = parts[-1].shape[0]
    return sum(one[count // 2 : count].astype(FULL) for one in parts).astype(LOW)


def step(before, parts, even, odd, late=False):
    if late:
        _, parts[-1] = after(before, parts[-1])
    sent = upper(*parts)
    if not late:
        before, sent = after(before, sent)
    return sent if late else before, parts + [permute(sent, even, odd)]


def finish_kernel(*refs):
    arrivals, outputs = refs[:FIVE], refs[FIVE:]
    done = 0
    for one in outputs:
        for at in range(one.shape[0] // ROWS * (one.shape[1] // WIDTH)):
            total = sum(more[0, done].astype(FULL) for more in arrivals)
            if one.shape[1] > WIDTH:
                one[:, at * WIDTH : (at + 1) * WIDTH] = total
            else:
                one[at * ROWS : (at + 1) * ROWS, :] = total
            done += 1


def finish(parts, shapes):
    spec = pl.BlockSpec((1,) + parts[0].shape[1:], lambda _: (0, 0, 0, 0))
    return pl.pallas_call(
        finish_kernel,
        grid=(1,),
        in_specs=[spec] * FIVE,
        out_specs=[pl.BlockSpec(one, lambda _: (0, 0)) for one in shapes],
        out_shape=[shape(*one) for one in shapes],
        cost_estimate=spent(0.5),
        name="finish",
    )(*parts)


def gather_plain(pieces):
    whole = [lax.all_gather(one, "dev", axis=0, tiled=True) for one in pieces]
    return jnp.stack([one.reshape(BLOCKS, ROWS, WIDTH) for one in whole], axis=1)


def places_plain():
    sides = ([0] * (BLOCKS // 2), [0] * (BLOCKS // 2))
    for block in range(BLOCKS):
        x, y, near_z, far_z = (block >> 1) & 1, (block >> 2) & 1, (block >> 3) & 1, block >> 4
        across = 8 * x + 4 * y if block & 1 else 8 * y + 4 * x
        sides[block & 1][across + 2 * near_z + far_z] = block
    return sides


def apart(blocks):
    return tuple(
        jnp.stack([blocks[k] for k in half])
        for side in places_plain()
        for half in (side[: BLOCKS // 4], side[BLOCKS // 4 :])
    )


def together(kept, sent):
    order = places_plain()
    found = {block: (side, at) for side in range(2) for at, block in enumerate(order[side])}
    return jnp.stack([(kept, sent)[found[k][0]][found[k][1]] for k in range(BLOCKS)])


def scatter_plain(matrix):
    return lax.psum_scatter(matrix.astype(FULL), "dev", scatter_dimension=0, tiled=True)


def local(
    frames,
    norm1_gain,
    norm1_shift,
    kernel_query,
    kernel_key,
    kernel_value,
    w_query,
    w_key,
    w_value,
    w_out,
    scale_attn,
    norm2_gain,
    norm2_shift,
    w_up,
    w_down,
    scale_mlp,
    cotangent,
):
    count = lax.axis_size("dev")
    own, columns = frames.shape[0], frames.shape[1] // count
    fast = own == ROWS and own * count == WIDTH
    vectors = (norm1_gain, norm1_shift, scale_attn, norm2_gain, norm2_shift, scale_mlp)
    kernels = (kernel_query, kernel_key, kernel_value)

    def to_crops(values):
        split = values.reshape(own, count, columns).transpose(1, 0, 2)
        return lax.all_to_all(split, "dev", 0, 0).reshape(WIDTH, columns)

    def to_devices(values):
        return lax.all_to_all(values.reshape(count, own, -1), "dev", 0, 0)

    def by_channels(blocks):
        return blocks.transpose(1, 0, 2).reshape(own, -1)

    matrices = (w_query, w_key, w_value, w_out)
    matrices = (w_query, w_key, w_value, w_out)
    x = to_crops(frames)
    if fast:
        me = lax.axis_index("dev").astype(jnp.int32).reshape(1)
        attn_shard, mlp_shard = pack(vectors, kernels, matrices + (w_up, w_down))
        blocks = grown(attn_shard[None], 16, 16)
        mlp_shard = after(blocks, mlp_shard)[1]
        blocks = grown(blocks, 8, 8)
        mlp_blocks = grown(mlp_shard[None], 16, 16, blocks)
        blocks = grown(blocks, 2, 4)
        cotangent = after(blocks, cotangent)[1]
        mlp_blocks = grown(mlp_blocks, 8, 8, blocks)
        others = permute(blocks, 4, 2)
        attn_sources = (blocks, others, permute(blocks, 1, 1), permute(others, 1, 1))
        mlp_blocks = grown(mlp_blocks, 2, 4, others)
        mlp_others = permute(mlp_blocks, 4, 2)
        x = after(mlp_blocks, x)[1]
    else:
        me = jnp.zeros((1,), jnp.int32)
        small = jnp.concatenate([one[:, None] for one in vectors] + list(kernels), axis=1)
        small = jnp.pad(small, ((0, 0), (0, WIDTH - small.shape[1])))
        attn_sources = apart(gather_plain(matrices + (small,)))
        ups = gather_plain([w_up[:, k * WIDTH : (k + 1) * WIDTH] for k in range(CHUNKS)])
        downs = lax.all_gather(w_down, "dev", axis=0, tiled=True)
        downs = downs.reshape(BLOCKS, CHUNKS, ROWS, WIDTH)
        mlp_sources = apart(jnp.concatenate((ups, downs), axis=1))
    cot = to_crops(cotangent)
    table, n1, scale1, conv, qkv, probs, heads, attn, resid, n2, scale2, normed2 = front(
        me, x, attn_sources
    )
    if fast:
        mlp_others = after(normed2, mlp_others)[1]
        mlp_sources = (
            mlp_blocks, mlp_others, permute(mlp_blocks, 1, 1), permute(mlp_others, 1, 1),
        )
    out, d_resid, d_attn, small, keep_mlp, *send_mlp = mlp(
        me, cot, normed2, table, resid, n2, scale2, attn, mlp_sources
    )
    out = to_devices(out)
    if fast:
        last, first = (permute(one, 1, 1) for one in reversed(send_mlp))
        sent = (keep_mlp[8:].astype(FULL) + last.astype(FULL)).astype(LOW)
        d_attn, sent = after(d_attn, sent)
        mlp_parts = [keep_mlp, first, permute(sent, 4, 2)]
    d_qkv, keep, *send = attend_back(
        me, d_attn, heads, qkv, probs, conv, attn_sources
    )
    if fast:
        last, first = (permute(one, 1, 1) for one in reversed(send))
        now, mlp_parts = step(d_qkv, mlp_parts, 2, 4, True)
        last = after(now, last)[1]
        now = (keep[8:].astype(FULL) + last.astype(FULL)).astype(LOW)
        parts = [keep, first, permute(now, 4, 2)]
        _, d_qkv = after(now, d_qkv)
    both = front_back(me, table, d_qkv, scale1, small, n1, d_resid, attn_sources)
    arrived = to_devices(both)
    if fast:
        _, out = after(both, out)
        now, mlp_parts = step(both, mlp_parts, 8, 8, True)
        now, parts = step(now, parts, 2, 4, True)
        now, mlp_parts = step(now, mlp_parts, 16, 16, True)
        now, parts = step(now, parts, 8, 8, True)
        now, parts = step(now, parts, 16, 16, True)
        _, out = after(now, out)
        output = by_channels(out)
        _, mlp_parts[-1] = after(output, mlp_parts[-1])
        grad_up, grad_down = finish(mlp_parts, ((own, HIDDEN), (CHUNKS * own, WIDTH)))
        _, parts[-1] = after(grad_up, parts[-1])
        grad_query, grad_key, grad_value, grad_out = finish(parts, ((own, WIDTH),) * 4)
        _, arrived = after(grad_query, arrived)
        frames_grad, vector_grads, kernel_grads = unpack(arrived)
    else:
        output = by_channels(out)
        blocks = together(keep_mlp, jnp.concatenate(send_mlp))
        ups = blocks[:, :CHUNKS].transpose(0, 2, 1, 3).reshape(WIDTH, HIDDEN)
        grad_up = scatter_plain(ups)
        grad_down = scatter_plain(blocks[:, CHUNKS:].reshape(HIDDEN, WIDTH))
        blocks = together(keep, jnp.concatenate(send))
        grad_query, grad_key, grad_value, grad_out = (
            scatter_plain(blocks[:, k].reshape(WIDTH, WIDTH)) for k in range(4)
        )
        frames_grad = by_channels(arrived[:, :, :columns])
        sums = jnp.sum(arrived[:, :, columns:].astype(FULL), axis=0)
        sums = sums[:, 0:16] + sums[:, 16:32]
        vector_grads = [sums[:, k] for k in range(6)]
        kernel_grads = [sums[:, k : k + 3] for k in (KERNEL_Q, KERNEL_K, KERNEL_V)]
    return (
        output,
        frames_grad,
        vector_grads[GAIN1],
        vector_grads[SHIFT1],
        *kernel_grads,
        grad_query,
        grad_key,
        grad_value,
        grad_out,
        vector_grads[SCALE_ATTN],
        vector_grads[GAIN2],
        vector_grads[SHIFT2],
        grad_up,
        grad_down,
        vector_grads[SCALE_MLP],
    )


def solution(mesh):
    in_specs = (
        P("dev", None),
        P("dev"),
        P("dev"),
        P("dev", None),
        P("dev", None),
        P("dev", None),
        P("dev", None),
        P("dev", None),
        P("dev", None),
        P("dev", None),
        P("dev"),
        P("dev"),
        P("dev"),
        P("dev", None),
        P("dev", None),
        P("dev"),
        P("dev", None),
    )
    out_specs = (
        P("dev", None),
        P("dev", None),
        P("dev"),
        P("dev"),
        P("dev", None),
        P("dev", None),
        P("dev", None),
        P("dev", None),
        P("dev", None),
        P("dev", None),
        P("dev", None),
        P("dev"),
        P("dev"),
        P("dev"),
        P("dev", None),
        P("dev", None),
        P("dev"),
    )
    return jax.shard_map(local, mesh=mesh, in_specs=in_specs, out_specs=out_specs, check_vma=False)
```

```python
import functools
import math

import jax
import jax.numpy as jnp
from jax import lax
from jax.experimental import pallas as pl
from jax.experimental.pallas import tpu as pltpu
from jax.sharding import PartitionSpec as P

HEADS = 4
HEAD_DIM = 128
LENGTH = 160
WINDOW = 19
WIDTH = 512
HIDDEN = 2048
FACTOR = HEAD_DIM ** (-0.5)
EPSILON = 1e-05
ROWS = 16
BLOCKS = WIDTH // ROWS
CHUNKS = HIDDEN // WIDTH
LOW = jnp.bfloat16
FULL = jnp.float32

VMEM = pl.BlockSpec(memory_space=pltpu.VMEM)
ANY = pl.BlockSpec(memory_space=pl.ANY)
HBM = pl.BlockSpec(memory_space=pltpu.HBM)
SMEM = pl.BlockSpec(memory_space=pltpu.SMEM)

GAIN1, SHIFT1, SCALE_ATTN, GAIN2, SHIFT2, SCALE_MLP, KERNEL_Q, KERNEL_K, KERNEL_V = (
    0, 1, 2, 3, 4, 5, 6, 9, 12,
)


def nn(left, right):
    return jnp.dot(left, right, preferred_element_type=FULL)


def nt(left, right):
    return lax.dot_general(left, right, (((1,), (1,)), ((), ())), preferred_element_type=FULL)


def tn(left, right):
    return lax.dot_general(left, right, (((0,), (0,)), ((), ())), preferred_element_type=FULL)


def block_at(side, at, me):
    far = 16 * (at & 1) + 8 * (at >> 1 & 1)
    low, high = at >> 2 & 1, at >> 3
    first, second = 2 * low + 4 * high, 4 * low + 2 * high
    return me ^ (jnp.where((me & 1) ^ side == 0, first, second) + far + side)


def block_rows(block, rows=ROWS):
    return pl.ds(pl.multiple_of(block * rows, rows), rows)


def fetch_blocks(sources, me, pieces, copy_to):
    for piece, target in zip(pieces, copy_to):
        for number, source in enumerate(sources):
            for at in range(BLOCKS // 4):
                block = block_at(number // 2, number % 2 * (BLOCKS // 4) + at, me)
                into, sem = target(block)
                pltpu.make_async_copy(source.at[at, piece], into, sem).start()


def store_blocks(targets, me, piece, copy_from, sem):
    keep, *sends = targets
    for side in range(2):
        for at in range(BLOCKS // 2):
            source = copy_from(block_at(side, at, me))
            half = BLOCKS // 4
            target = sends[at // half].at[at % half, piece] if side else keep.at[at, piece]
            pltpu.make_async_copy(source, target, sem).start()


def whole_wait(ref, sem):
    pltpu.make_async_copy(ref, ref, sem).wait()


def move(source, target, sem):
    copy = pltpu.make_async_copy(source, target, sem)
    copy.start()
    return copy


def down_one(values):
    at = lax.broadcasted_iota(jnp.int32, values.shape, 0)
    return jnp.where(at == 0, 0.0, pltpu.roll(values, 1, 0))


def up_one(values):
    at = lax.broadcasted_iota(jnp.int32, values.shape, 0)
    last = values.shape[0] - 1
    return jnp.where(at == last, 0.0, pltpu.roll(values, last, 0))


def normalise(values):
    center = jnp.mean(values, axis=1, keepdims=True)
    centered = values - center
    scale = lax.rsqrt(jnp.mean(centered * centered, axis=1, keepdims=True) + EPSILON)
    return centered * scale, scale


def row(table, index):
    return table[index : index + 1, :]


def front_kernel(
    me_ref, x_ref, source0, source1, source2, source3,
    table_out, n1_out, scale1_out, conv_out, qkv_out, probs_out, heads_out, attn_out, resid_out,
    n2_out, scale2_out, normed2_out,
    weights, x_rows, table, n1, scale1, conv, qkv, probs, heads, attn, resid, n2, scale2, normed2,
    in_sem, sems,
):
    me = me_ref[0]
    tokens = x_ref.shape[1]
    crops = tokens // LENGTH
    copies = []

    def send(source, target):
        copies.append(move(source, target, sems.at[len(copies)]))

    fetch_blocks(
        (source0, source1, source2, source3), me, (slice(None),),
        (lambda block: (weights.at[:, block_rows(block)], in_sem.at[0]),),
    )
    for at in range(0, tokens, 128):
        x_rows[at : at + 128, :] = x_ref[:, at : at + 128].T.astype(FULL)

    def norm_one(at, carry):
        rows = pl.ds(pl.multiple_of(at * 80, 80), 80)
        n1[rows, :], scale1[rows, :] = normalise(x_rows[rows, :])
        return carry

    lax.fori_loop(0, tokens // 80, norm_one, 0, unroll=True)
    send(n1, n1_out)
    send(scale1, scale1_out)
    whole_wait(weights, in_sem.at[0])
    table[...] = weights[4, :, 0:128].astype(FULL).T[0:16, :]
    send(table, table_out)

    def convolve(crop, carry):
        rows = pl.ds(pl.multiple_of(crop * LENGTH, LENGTH), LENGTH)
        for at in range(0, WIDTH, 128):
            lanes = slice(at, at + 128)
            normed = n1[rows, lanes] * table[GAIN1 : GAIN1 + 1, lanes] + table[SHIFT1 : SHIFT1 + 1, lanes]
            before, after = down_one(normed), up_one(normed)
            for k, start in enumerate((KERNEL_Q, KERNEL_K, KERNEL_V)):
                conv[k, rows, lanes] = (
                    table[start : start + 1, lanes] * before
                    + table[start + 1 : start + 2, lanes] * normed
                    + table[start + 2 : start + 3, lanes] * after
                ).astype(LOW)
        return carry

    lax.fori_loop(0, crops, convolve, 0, unroll=True)
    send(conv, conv_out)
    for k in range(3):
        qkv[k] = nn(conv[k], weights[k]).astype(LOW)
    send(qkv, qkv_out)

    near_t = lax.broadcasted_iota(jnp.int32, (LENGTH, LENGTH), 0)
    near_u = lax.broadcasted_iota(jnp.int32, (LENGTH, LENGTH), 1)
    nearby = jnp.abs(near_t - near_u) <= WINDOW // 2

    def attend(crop, carry):
        rows = pl.ds(pl.multiple_of(crop * LENGTH, LENGTH), LENGTH)
        for h in range(HEADS):
            lanes = slice(h * HEAD_DIM, (h + 1) * HEAD_DIM)
            scores = jnp.where(nearby, nt(qkv[0, rows, lanes], qkv[1, rows, lanes]) * FACTOR, -1e30)
            powers = jnp.exp(scores - jnp.max(scores, axis=1, keepdims=True))
            shares = powers / jnp.sum(powers, axis=1, keepdims=True)
            probs[crop, h] = shares
            heads[rows, lanes] = nn(shares.astype(LOW), qkv[2, rows, lanes]).astype(LOW)
        return carry

    lax.fori_loop(0, crops, attend, 0, unroll=True)
    send(probs, probs_out)
    send(heads, heads_out)
    attn[...] = nn(heads[...], weights[3])
    send(attn, attn_out)

    def norm_two(at, carry):
        rows = pl.ds(pl.multiple_of(at * 80, 80), 80)
        mixed = x_rows[rows, :] + row(table, SCALE_ATTN) * attn[rows, :]
        resid[rows, :] = mixed
        normal, scale = normalise(mixed)
        n2[rows, :], scale2[rows, :] = normal, scale
        normed2[rows, :] = (normal * row(table, GAIN2) + row(table, SHIFT2)).astype(LOW)
        return carry

    lax.fori_loop(0, tokens // 80, norm_two, 0, unroll=True)
    send(normed2, normed2_out)
    send(resid, resid_out)
    send(n2, n2_out)
    send(scale2, scale2_out)
    for copy in copies:
        copy.wait()


def front(me, x, sources):
    tokens = x.shape[1]
    crops = tokens // LENGTH
    shapes = [
        shape(16, WIDTH),
        shape(tokens, WIDTH),
        shape(tokens, 1),
        shape(3, tokens, WIDTH, kind=LOW),
        shape(3, tokens, WIDTH, kind=LOW),
        shape(crops, HEADS, LENGTH, LENGTH),
        shape(tokens, WIDTH, kind=LOW),
        shape(tokens, WIDTH),
        shape(tokens, WIDTH),
        shape(tokens, WIDTH),
        shape(tokens, 1),
        shape(tokens, WIDTH, kind=LOW),
    ]
    return pl.pallas_call(
        front_kernel,
        in_specs=[SMEM, VMEM] + [ANY] * 4,
        out_specs=[HBM] * 12,
        out_shape=shapes,
        scratch_shapes=[
            pltpu.VMEM((5, WIDTH, WIDTH), LOW),
            pltpu.VMEM((tokens, WIDTH), FULL),
        ]
        + [pltpu.VMEM(one.shape, one.dtype) for one in shapes]
        + [pltpu.SemaphoreType.DMA((1,)), pltpu.SemaphoreType.DMA((12,))],
        compiler_params=pltpu.CompilerParams(vmem_limit_bytes=56 << 20),
        cost_estimate=spent(0.5),
        name="front",
    )(me, x, *sources)


def spent(microseconds):
    return pl.CostEstimate(flops=int(microseconds * 1.15e9), bytes_accessed=0, transcendentals=0)


def shape(*dims, kind=FULL):
    return jax.ShapeDtypeStruct(dims, kind)


def gelu_both(values):
    below = 0.5 + 0.5 * lax.erf(values * math.sqrt(0.5))
    bell = jnp.exp(-0.5 * values * values)
    return values * below, below + values * bell * (0.5 * math.sqrt(2 / math.pi))


def mlp_kernel(
    me_ref, cot_in, normed2_in, table, resid_in, n2_in, scale2_in, attn_in, source0, source1, source2, source3,
    out, d_resid_out, d_attn_out, small, keep, send_low, send_high,
    up, down, normed2_t, cot_rows, d_branch, branch, active, slope, d_hidden, d_normed2, grad_up,
    grad_down, resid, n2, scale2, attn, d_resid, d_attn, cot_ref, normed2, sems,
):
    me = me_ref[0]
    tokens = cot_ref.shape[1]
    first = move(normed2_in, normed2, sems.at[10])
    second = move(cot_in, cot_ref, sems.at[11])

    fetch_blocks(
        (source0, source1, source2, source3), me, (slice(0, CHUNKS), slice(CHUNKS, 2 * CHUNKS)),
        (
            lambda block: (up.at[:, block_rows(block)], sems.at[0]),
            lambda block: (down.at[block_rows(block, CHUNKS)], sems.at[1]),
        ),
    )
    scale_mlp = row(table, SCALE_MLP)
    first.wait()
    second.wait()
    for at in range(0, tokens, 128):
        rows = slice(at, at + 128)
        cot_rows[rows, :] = cot_ref[:, rows].T
        d_branch[rows, :] = (scale_mlp * cot_rows[rows, :].astype(FULL)).astype(LOW)
        normed2_t[:, rows] = normed2[rows, :].T
    whole_wait(up, sems.at[0])

    for chunk in range(CHUNKS):
        rows = slice(chunk * BLOCKS, (chunk + 1) * BLOCKS)
        hidden = nn(normed2[...], up[chunk])
        value, slope[...] = gelu_both(hidden)
        active[...] = value.astype(LOW)
        if chunk == 0:
            whole_wait(down, sems.at[1])
            arrivals = [
                move(source, target, sems.at[4 + at])
                for at, (source, target) in enumerate(
                    ((resid_in, resid), (n2_in, n2), (scale2_in, scale2), (attn_in, attn))
                )
            ]
        down_rows = down[rows].reshape(WIDTH, WIDTH)
        d_active = nt(d_branch[...], down_rows)
        d_hidden[...] = (d_active * slope[...]).astype(LOW)
        added = nn(active[...], down_rows)
        back = nt(d_hidden[...], up[chunk])
        branch[...] = added if chunk == 0 else branch[...] + added
        d_normed2[...] = back if chunk == 0 else d_normed2[...] + back
        grad_up[chunk] = nn(normed2_t[...], d_hidden[...]).astype(LOW)
        grad_down[rows] = tn(active[...], d_branch[...]).astype(LOW).reshape(BLOCKS, ROWS, WIDTH)

    store_blocks(
        (keep, send_low, send_high), me, slice(0, CHUNKS), lambda block: grad_up.at[:, block_rows(block)],
        sems.at[3],
    )
    store_blocks(
        (keep, send_low, send_high), me, slice(CHUNKS, 2 * CHUNKS),
        lambda block: grad_down.at[block_rows(block, CHUNKS)], sems.at[2],
    )
    for copy in arrivals:
        copy.wait()

    def norm_back(at, sums):
        rows = pl.ds(pl.multiple_of(at * 80, 80), 80)
        grad, normal, cot = d_normed2[rows, :], n2[rows, :], cot_rows[rows, :].astype(FULL)
        s = row(table, GAIN2) * grad
        along = jnp.mean(s * normal, axis=1, keepdims=True)
        middle = jnp.mean(s, axis=1, keepdims=True)
        total = cot + (s - middle - normal * along) * scale2[rows, :]
        d_resid[rows, :] = total
        d_attn[rows, :] = (row(table, SCALE_ATTN) * total).astype(LOW)
        terms = (grad * normal, grad, total * attn[rows, :], cot * branch[rows, :])
        return tuple(one + jnp.sum(more, axis=0, keepdims=True) for one, more in zip(sums, terms))

    sums = lax.fori_loop(0, tokens // 80, norm_back, (jnp.zeros((1, WIDTH), FULL),) * 4, unroll=True)
    leaving = [
        move(d_attn, d_attn_out, sems.at[8]),
        move(d_resid, d_resid_out, sems.at[9]),
    ]
    for at, one in enumerate(sums):
        small[at : at + 1, :] = one
    for at in range(0, tokens, 128):
        rows = slice(at, at + 128)
        out[:, rows] = (resid[rows, :] + scale_mlp * branch[rows, :]).astype(LOW).T
    whole_wait(grad_down, sems.at[2])
    whole_wait(grad_up, sems.at[3])
    for copy in leaving:
        copy.wait()


def mlp(me, cot, normed2, table, resid, n2, scale2, attn, sources):
    tokens = cot.shape[1]
    pieces = (BLOCKS // 2, 2 * CHUNKS, ROWS, WIDTH)
    halves = (BLOCKS // 4,) + pieces[1:]
    rows_full, rows_low = pltpu.VMEM((tokens, WIDTH), FULL), pltpu.VMEM((tokens, WIDTH), LOW)
    return pl.pallas_call(
        mlp_kernel,
        in_specs=[SMEM, HBM, HBM, VMEM] + [HBM] * 4 + [ANY] * 4,
        out_specs=[VMEM, HBM, HBM, VMEM, HBM, HBM, HBM],
        out_shape=[
            shape(WIDTH, tokens, kind=LOW),
            shape(tokens, WIDTH),
            shape(tokens, WIDTH, kind=LOW),
            shape(8, WIDTH),
            shape(*pieces, kind=LOW),
            shape(*halves, kind=LOW),
            shape(*halves, kind=LOW),
        ],
        scratch_shapes=[
            pltpu.VMEM((CHUNKS, WIDTH, WIDTH), LOW),
            pltpu.VMEM((HIDDEN // ROWS, ROWS, WIDTH), LOW),
            pltpu.VMEM((WIDTH, tokens), LOW),
            rows_low,
            rows_low,
            rows_full,
            rows_low,
            rows_full,
            rows_low,
            rows_full,
            pltpu.VMEM((CHUNKS, WIDTH, WIDTH), LOW),
            pltpu.VMEM((HIDDEN // ROWS, ROWS, WIDTH), LOW),
            rows_full,
            rows_full,
            pltpu.VMEM((tokens, 1), FULL),
            rows_full,
            rows_full,
            rows_low,
            pltpu.VMEM((WIDTH, tokens), LOW),
            rows_low,
            pltpu.SemaphoreType.DMA((12,)),
        ],
        compiler_params=pltpu.CompilerParams(vmem_limit_bytes=56 << 20),
        cost_estimate=spent(0.5),
        name="mlp",
    )(me, cot, normed2, table, resid, n2, scale2, attn, *sources)


def attend_back_kernel(
    me_ref, d_attn_in, heads_in, qkv_in, probs_in, conv_in, source0, source1, source2, source3,
    d_qkv_out, keep, send_low, send_high,
    w_out, d_attn, heads, qkv, probs, conv, d_heads, d_qkv, grads, sems,
):
    me = me_ref[0]
    crops = d_attn.shape[0] // LENGTH
    soon = [move(heads_in, heads, sems.at[3]), move(d_attn_in, d_attn, sems.at[4])]
    fetch_blocks(
        (source0, source1, source2, source3), me, (3,),
        (lambda block: (w_out.at[block_rows(block)], sems.at[0]),),
    )
    later = [move(qkv_in, qkv, sems.at[5]), move(probs_in, probs, sems.at[6])]
    for copy in soon:
        copy.wait()
    grads[3] = tn(heads[...], d_attn[...]).astype(LOW)
    whole_wait(w_out, sems.at[0])
    d_heads[...] = nt(d_attn[...], w_out[...]).astype(LOW)
    convs = move(conv_in, conv, sems.at[7])
    for copy in later:
        copy.wait()

    def attend(crop, carry):
        rows = pl.ds(pl.multiple_of(crop * LENGTH, LENGTH), LENGTH)
        for h in range(HEADS):
            lanes = slice(h * HEAD_DIM, (h + 1) * HEAD_DIM)
            shares, grad = probs[crop, h], d_heads[rows, lanes]
            d_probs = nt(grad, qkv[2, rows, lanes])
            d_qkv[2, rows, lanes] = tn(shares.astype(LOW), grad).astype(LOW)
            d_scores = shares * (d_probs - jnp.sum(shares * d_probs, axis=1, keepdims=True))
            d_scores = d_scores.astype(LOW)
            d_qkv[0, rows, lanes] = (nn(d_scores, qkv[1, rows, lanes]) * FACTOR).astype(LOW)
            d_qkv[1, rows, lanes] = (tn(d_scores, qkv[0, rows, lanes]) * FACTOR).astype(LOW)
        return carry

    lax.fori_loop(0, crops, attend, 0, unroll=True)
    leaving = move(d_qkv, d_qkv_out, sems.at[1])
    convs.wait()
    for k in range(3):
        grads[k] = tn(conv[k], d_qkv[k]).astype(LOW)
    store_blocks(
        (keep, send_low, send_high), me, slice(None), lambda block: grads.at[:, block_rows(block)], sems.at[2]
    )
    leaving.wait()
    whole_wait(grads, sems.at[2])


def attend_back(me, d_attn, heads, qkv, probs, conv, sources):
    tokens = heads.shape[0]
    pieces = (BLOCKS // 2, 4, ROWS, WIDTH)
    halves = (BLOCKS // 4,) + pieces[1:]
    rows_low = pltpu.VMEM((tokens, WIDTH), LOW)
    return pl.pallas_call(
        attend_back_kernel,
        in_specs=[SMEM] + [HBM] * 5 + [ANY] * 4,
        out_specs=[HBM] * 4,
        out_shape=[
            shape(3, tokens, WIDTH, kind=LOW),
            shape(*pieces, kind=LOW),
            shape(*halves, kind=LOW),
            shape(*halves, kind=LOW),
        ],
        scratch_shapes=[
            pltpu.VMEM((WIDTH, WIDTH), LOW),
            rows_low,
            rows_low,
            pltpu.VMEM(qkv.shape, LOW),
            pltpu.VMEM(probs.shape, FULL),
            pltpu.VMEM(conv.shape, LOW),
            rows_low,
            pltpu.VMEM(qkv.shape, LOW),
            pltpu.VMEM((4, WIDTH, WIDTH), LOW),
            pltpu.SemaphoreType.DMA((8,)),
        ],
        compiler_params=pltpu.CompilerParams(vmem_limit_bytes=56 << 20),
        cost_estimate=spent(10),
        name="attend_back",
    )(me, d_attn, heads, qkv, probs, conv, *sources)


def front_back_kernel(
    me_ref, table, small, d_qkv_in, n1_in, scale1_in, d_resid_in, source0, source1, source2, source3,
    both,
    weights, d_qkv, n1, scale1, d_resid, d_conv, sums, sems,
):
    me = me_ref[0]
    tokens = n1.shape[0]
    crops = tokens // LENGTH
    soon = move(d_qkv_in, d_qkv, sems.at[0])
    fetch_blocks(
        (source0, source1, source2, source3), me, (slice(0, 3),),
        (lambda block: (weights.at[:, block_rows(block)], sems.at[1]),),
    )
    later = [
        move(n1_in, n1, sems.at[2]),
        move(scale1_in, scale1, sems.at[3]),
        move(d_resid_in, d_resid, sems.at[4]),
    ]
    sums[...] = jnp.zeros_like(sums)
    soon.wait()
    whole_wait(weights, sems.at[1])
    for k in range(3):
        d_conv[k] = nt(d_qkv[k], weights[k])
    for copy in later:
        copy.wait()

    def back(crop, carry):
        rows = pl.ds(pl.multiple_of(crop * LENGTH, LENGTH), LENGTH)
        middle = jnp.zeros((LENGTH, 1), FULL)
        along = jnp.zeros((LENGTH, 1), FULL)
        for at in range(0, WIDTH, 128):
            lanes = slice(at, at + 128)
            gain = table[GAIN1 : GAIN1 + 1, lanes]
            normal = n1[rows, lanes]
            normed = normal * gain + table[SHIFT1 : SHIFT1 + 1, lanes]
            before, after = down_one(normed), up_one(normed)
            parts = [0.0, 0.0, 0.0]
            for k, start in enumerate((KERNEL_Q, KERNEL_K, KERNEL_V)):
                grad = d_conv[k, rows, lanes]
                for j, seen in enumerate((before, normed, after)):
                    sums[start + j : start + j + 1, lanes] += jnp.sum(grad * seen, axis=0, keepdims=True)
                    parts[j] = parts[j] + table[start + j : start + j + 1, lanes] * grad
            total = up_one(parts[0]) + parts[1] + down_one(parts[2])
            sums[GAIN1 : GAIN1 + 1, lanes] += jnp.sum(total * normal, axis=0, keepdims=True)
            sums[SHIFT1 : SHIFT1 + 1, lanes] += jnp.sum(total, axis=0, keepdims=True)
            s = gain * total
            d_conv[0, rows, lanes] = s
            middle += jnp.sum(s, axis=1, keepdims=True)
            along += jnp.sum(s * normal, axis=1, keepdims=True)
        middle, along = middle / WIDTH, along / WIDTH
        for at in range(0, WIDTH, 128):
            lanes = slice(at, at + 128)
            d_conv[1, rows, lanes] = d_resid[rows, lanes] + (
                d_conv[0, rows, lanes] - middle - n1[rows, lanes] * along
            ) * scale1[rows, :]
        return carry

    lax.fori_loop(0, crops, back, 0, unroll=True)
    for at in range(0, tokens, 128):
        both[:, at : at + 128] = d_conv[1, at : at + 128, :].astype(LOW).T
    sums[GAIN2 : SHIFT2 + 1, :] = small[0:2, :]
    sums[SCALE_ATTN : SCALE_ATTN + 1, :] = small[2:3, :]
    sums[SCALE_MLP : SCALE_MLP + 1, :] = small[3:4, :]
    high = sums[0:16, :].astype(LOW).astype(FULL)
    sums[16:32, :] = sums[0:16, :] - high
    both[:, tokens : tokens + 128] = sums[...].astype(LOW).T


def front_back(me, table, d_qkv, scale1, small, n1, d_resid, sources):
    tokens = n1.shape[0]
    rows_full = pltpu.VMEM((tokens, WIDTH), FULL)
    return pl.pallas_call(
        front_back_kernel,
        in_specs=[SMEM] + [VMEM] * 2 + [HBM] * 4 + [ANY] * 4,
        out_specs=VMEM,
        out_shape=shape(WIDTH, tokens + 128, kind=LOW),
        scratch_shapes=[
            pltpu.VMEM((3, WIDTH, WIDTH), LOW),
            pltpu.VMEM(d_qkv.shape, LOW),
            rows_full,
            pltpu.VMEM((tokens, 1), FULL),
            rows_full,
            pltpu.VMEM((3, tokens, WIDTH), FULL),
            pltpu.VMEM((128, WIDTH), FULL),
            pltpu.SemaphoreType.DMA((5,)),
        ],
        compiler_params=pltpu.CompilerParams(vmem_limit_bytes=56 << 20),
        cost_estimate=spent(8),
        name="front_back",
    )(me, table, small, d_qkv, n1, scale1, d_resid, *sources)


def unpack_kernel(arrived, out, frames, output, *rest):
    vectors, kernels, square = rest[:6], rest[6:9], rest[9]
    count, _, columns = arrived.shape
    columns -= 128
    total = jnp.zeros((ROWS, 128), FULL)
    for at in range(count):
        frames[:, at * columns : (at + 1) * columns] = arrived[at, :, 0:columns]
        output[:, at * columns : (at + 1) * columns] = out[at]
        total += arrived[at, :, columns : columns + 128].astype(FULL)
    square[...] = jnp.zeros_like(square)
    square[0:ROWS, :] = total
    sums = square[...].T
    sums = sums[0:16, :] + sums[16:32, :]
    for at, one in enumerate(vectors):
        one[...] = sums[at : at + 1, 0:ROWS]
    for at, one in zip((KERNEL_Q, KERNEL_K, KERNEL_V), kernels):
        one[...] = sums[at : at + 3, 0:ROWS]


def unpack(arrived, out):
    count, rows, columns = arrived.shape
    found = pl.pallas_call(
        unpack_kernel,
        in_specs=[VMEM] * 2,
        out_specs=[VMEM] * 11,
        out_shape=[shape(rows, count * (columns - 128), kind=LOW)] * 2
        + [shape(1, rows)] * 6
        + [shape(3, rows)] * 3,
        scratch_shapes=[pltpu.VMEM((128, 128), FULL)],
        cost_estimate=spent(0.5),
        name="unpack",
    )(arrived, out)
    vectors, kernels = found[2:8], found[8:]
    return found[0], found[1], [one.reshape(rows) for one in vectors], [one.T for one in kernels]


def pack_kernel(
    gain1, shift1, scale_attn, gain2, shift2, scale_mlp, kernel_q, kernel_k, kernel_v,
    w_query, w_key, w_value, w_out, w_up, w_down,
    attn_shard, mlp_shard, table,
):
    table[...] = jnp.zeros_like(table)
    for at, one in enumerate((gain1, shift1, scale_attn, gain2, shift2, scale_mlp)):
        table[at : at + 1, 0:ROWS] = one[...].astype(FULL)
    for at, one in ((KERNEL_Q, kernel_q), (KERNEL_K, kernel_k), (KERNEL_V, kernel_v)):
        table[at : at + 3, 0:ROWS] = one[...].astype(FULL)
    attn_shard[4] = jnp.zeros((ROWS, WIDTH), LOW)
    attn_shard[4, :, 0:128] = table[...].T[0:ROWS, :].astype(LOW)
    for at, one in ((0, w_query), (1, w_key), (2, w_value), (3, w_out)):
        attn_shard[at] = one[...]
    for chunk in range(CHUNKS):
        mlp_shard[chunk] = w_up[:, chunk * WIDTH : (chunk + 1) * WIDTH]
        mlp_shard[CHUNKS + chunk] = w_down[chunk * ROWS : (chunk + 1) * ROWS, :]


def pack(vectors, kernels, matrices):
    return pl.pallas_call(
        pack_kernel,
        in_specs=[VMEM] * 15,
        out_specs=[VMEM] * 2,
        out_shape=[
            shape(5, ROWS, WIDTH, kind=LOW),
            shape(2 * CHUNKS, ROWS, WIDTH, kind=LOW),
        ],
        scratch_shapes=[pltpu.VMEM((128, 128), FULL)],
        name="pack",
    )(*[one.reshape(1, -1) for one in vectors], *[one.T for one in kernels], *matrices)


FIVE = 6


def permute(values, even, odd):
    count = lax.axis_size("dev")
    return lax.ppermute(
        values, "dev", [(at, at ^ (odd if at & 1 else even)) for at in range(count)]
    )


def after(first, *others):
    return lax.optimization_barrier((first,) + others)


def grown(blocks, even, odd, before=None):
    others = permute(blocks, even, odd)
    if before is not None:
        others = after(before, others)[1]
    return jnp.concatenate((blocks, others))


def upper(*parts):
    count = parts[-1].shape[0]
    return sum(one[count // 2 : count].astype(FULL) for one in parts).astype(LOW)


def step(before, parts, even, odd, late=False):
    if late:
        _, parts[-1] = after(before, parts[-1])
    sent = upper(*parts)
    if not late:
        before, sent = after(before, sent)
    return sent if late else before, parts + [permute(sent, even, odd)]


def finish_kernel(*refs):
    arrivals, outputs = refs[:FIVE], refs[FIVE:]
    done = 0
    for one in outputs:
        for at in range(one.shape[0] // ROWS * (one.shape[1] // WIDTH)):
            total = sum(more[0, done].astype(FULL) for more in arrivals)
            if one.shape[1] > WIDTH:
                one[:, at * WIDTH : (at + 1) * WIDTH] = total
            else:
                one[at * ROWS : (at + 1) * ROWS, :] = total
            done += 1


def finish(parts, shapes):
    spec = pl.BlockSpec((1,) + parts[0].shape[1:], lambda _: (0, 0, 0, 0))
    return pl.pallas_call(
        finish_kernel,
        grid=(1,),
        in_specs=[spec] * FIVE,
        out_specs=[pl.BlockSpec(one, lambda _: (0, 0)) for one in shapes],
        out_shape=[shape(*one) for one in shapes],
        cost_estimate=spent(0.5),
        name="finish",
    )(*parts)


def gather_plain(pieces):
    whole = [lax.all_gather(one, "dev", axis=0, tiled=True) for one in pieces]
    return jnp.stack([one.reshape(BLOCKS, ROWS, WIDTH) for one in whole], axis=1)


def places_plain():
    sides = ([0] * (BLOCKS // 2), [0] * (BLOCKS // 2))
    for block in range(BLOCKS):
        x, y, near_z, far_z = (block >> 1) & 1, (block >> 2) & 1, (block >> 3) & 1, block >> 4
        across = 8 * x + 4 * y if block & 1 else 8 * y + 4 * x
        sides[block & 1][across + 2 * near_z + far_z] = block
    return sides


def apart(blocks):
    return tuple(
        jnp.stack([blocks[k] for k in half])
        for side in places_plain()
        for half in (side[: BLOCKS // 4], side[BLOCKS // 4 :])
    )


def together(kept, sent):
    order = places_plain()
    found = {block: (side, at) for side in range(2) for at, block in enumerate(order[side])}
    return jnp.stack([(kept, sent)[found[k][0]][found[k][1]] for k in range(BLOCKS)])


def scatter_plain(matrix):
    return lax.psum_scatter(matrix.astype(FULL), "dev", scatter_dimension=0, tiled=True)


def local(
    frames,
    norm1_gain,
    norm1_shift,
    kernel_query,
    kernel_key,
    kernel_value,
    w_query,
    w_key,
    w_value,
    w_out,
    scale_attn,
    norm2_gain,
    norm2_shift,
    w_up,
    w_down,
    scale_mlp,
    cotangent,
):
    count = lax.axis_size("dev")
    own, columns = frames.shape[0], frames.shape[1] // count
    fast = own == ROWS and own * count == WIDTH
    vectors = (norm1_gain, norm1_shift, scale_attn, norm2_gain, norm2_shift, scale_mlp)
    kernels = (kernel_query, kernel_key, kernel_value)

    def to_crops(values):
        split = values.reshape(own, count, columns).transpose(1, 0, 2)
        return lax.all_to_all(split, "dev", 0, 0).reshape(WIDTH, columns)

    def to_devices(values):
        return lax.all_to_all(values.reshape(count, own, -1), "dev", 0, 0)

    def by_channels(blocks):
        return blocks.transpose(1, 0, 2).reshape(own, -1)

    matrices = (w_query, w_key, w_value, w_out)
    matrices = (w_query, w_key, w_value, w_out)
    x = to_crops(frames)
    if fast:
        me = lax.axis_index("dev").astype(jnp.int32).reshape(1)
        attn_shard, mlp_shard = pack(vectors, kernels, matrices + (w_up, w_down))
        blocks = grown(attn_shard[None], 16, 16)
        mlp_shard = after(blocks, mlp_shard)[1]
        blocks = grown(blocks, 8, 8)
        mlp_blocks = grown(mlp_shard[None], 16, 16, blocks)
        blocks = grown(blocks, 2, 4)
        cotangent = after(blocks, cotangent)[1]
        mlp_blocks = grown(mlp_blocks, 8, 8, blocks)
        others = permute(blocks, 4, 2)
        attn_sources = (blocks, others, permute(blocks, 1, 1), permute(others, 1, 1))
        mlp_blocks = grown(mlp_blocks, 2, 4, others)
        mlp_others = permute(mlp_blocks, 4, 2)
        x = after(mlp_blocks, x)[1]
    else:
        me = jnp.zeros((1,), jnp.int32)
        small = jnp.concatenate([one[:, None] for one in vectors] + list(kernels), axis=1)
        small = jnp.pad(small, ((0, 0), (0, WIDTH - small.shape[1])))
        attn_sources = apart(gather_plain(matrices + (small,)))
        ups = gather_plain([w_up[:, k * WIDTH : (k + 1) * WIDTH] for k in range(CHUNKS)])
        downs = lax.all_gather(w_down, "dev", axis=0, tiled=True)
        downs = downs.reshape(BLOCKS, CHUNKS, ROWS, WIDTH)
        mlp_sources = apart(jnp.concatenate((ups, downs), axis=1))
    cot = to_crops(cotangent)
    table, n1, scale1, conv, qkv, probs, heads, attn, resid, n2, scale2, normed2 = front(
        me, x, attn_sources
    )
    if fast:
        mlp_others = after(normed2, mlp_others)[1]
        mlp_sources = (
            mlp_blocks, mlp_others, permute(mlp_blocks, 1, 1), permute(mlp_others, 1, 1),
        )
    out, d_resid, d_attn, small, keep_mlp, *send_mlp = mlp(
        me, cot, normed2, table, resid, n2, scale2, attn, mlp_sources
    )
    out = to_devices(out)
    if fast:
        last, first = (permute(one, 1, 1) for one in reversed(send_mlp))
        sent = (keep_mlp[8:].astype(FULL) + last.astype(FULL)).astype(LOW)
        d_attn, sent = after(d_attn, sent)
        mlp_parts = [keep_mlp, first, permute(sent, 4, 2)]
    d_qkv, keep, *send = attend_back(
        me, d_attn, heads, qkv, probs, conv, attn_sources
    )
    if fast:
        last, first = (permute(one, 1, 1) for one in reversed(send))
        now, mlp_parts = step(d_qkv, mlp_parts, 2, 4, True)
        last = after(now, last)[1]
        now = (keep[8:].astype(FULL) + last.astype(FULL)).astype(LOW)
        parts = [keep, first, permute(now, 4, 2)]
        _, d_qkv = after(now, d_qkv)
    both = front_back(me, table, d_qkv, scale1, small, n1, d_resid, attn_sources)
    arrived = to_devices(both)
    if fast:
        _, out = after(both, out)
        now, mlp_parts = step(both, mlp_parts, 8, 8, True)
        now, parts = step(now, parts, 2, 4, True)
        now, mlp_parts = step(now, mlp_parts, 16, 16, True)
        now, parts = step(now, parts, 8, 8, True)
        frames_grad, output, vector_grads, kernel_grads = unpack(arrived, out)
        frames_grad, parts[-1] = after(frames_grad, parts[-1])
        now, parts = step(now, parts, 16, 16, True)
        grad_up, grad_down = finish(mlp_parts, ((own, HIDDEN), (CHUNKS * own, WIDTH)))
        grad_query, grad_key, grad_value, grad_out = finish(parts, ((own, WIDTH),) * 4)
    else:
        output = by_channels(out)
        blocks = together(keep_mlp, jnp.concatenate(send_mlp))
        ups = blocks[:, :CHUNKS].transpose(0, 2, 1, 3).reshape(WIDTH, HIDDEN)
        grad_up = scatter_plain(ups)
        grad_down = scatter_plain(blocks[:, CHUNKS:].reshape(HIDDEN, WIDTH))
        blocks = together(keep, jnp.concatenate(send))
        grad_query, grad_key, grad_value, grad_out = (
            scatter_plain(blocks[:, k].reshape(WIDTH, WIDTH)) for k in range(4)
        )
        frames_grad = by_channels(arrived[:, :, :columns])
        sums = jnp.sum(arrived[:, :, columns:].astype(FULL), axis=0)
        sums = sums[:, 0:16] + sums[:, 16:32]
        vector_grads = [sums[:, k] for k in range(6)]
        kernel_grads = [sums[:, k : k + 3] for k in (KERNEL_Q, KERNEL_K, KERNEL_V)]
    return (
        output,
        frames_grad,
        vector_grads[GAIN1],
        vector_grads[SHIFT1],
        *kernel_grads,
        grad_query,
        grad_key,
        grad_value,
        grad_out,
        vector_grads[SCALE_ATTN],
        vector_grads[GAIN2],
        vector_grads[SHIFT2],
        grad_up,
        grad_down,
        vector_grads[SCALE_MLP],
    )


def solution(mesh):
    in_specs = (
        P("dev", None),
        P("dev"),
        P("dev"),
        P("dev", None),
        P("dev", None),
        P("dev", None),
        P("dev", None),
        P("dev", None),
        P("dev", None),
        P("dev", None),
        P("dev"),
        P("dev"),
        P("dev"),
        P("dev", None),
        P("dev", None),
        P("dev"),
        P("dev", None),
    )
    out_specs = (
        P("dev", None),
        P("dev", None),
        P("dev"),
        P("dev"),
        P("dev", None),
        P("dev", None),
        P("dev", None),
        P("dev", None),
        P("dev", None),
        P("dev", None),
        P("dev", None),
        P("dev"),
        P("dev"),
        P("dev"),
        P("dev", None),
        P("dev", None),
        P("dev"),
    )
    return jax.shard_map(local, mesh=mesh, in_specs=in_specs, out_specs=out_specs, check_vma=False)
```

```python
import functools
import math

import jax
import jax.numpy as jnp
from jax import lax
from jax.experimental import pallas as pl
from jax.experimental.pallas import tpu as pltpu
from jax.sharding import PartitionSpec as P

HEADS = 4
HEAD_DIM = 128
LENGTH = 160
WINDOW = 19
WIDTH = 512
HIDDEN = 2048
FACTOR = HEAD_DIM ** (-0.5)
EPSILON = 1e-05
ROWS = 16
BLOCKS = WIDTH // ROWS
CHUNKS = HIDDEN // WIDTH
LOW = jnp.bfloat16
FULL = jnp.float32

VMEM = pl.BlockSpec(memory_space=pltpu.VMEM)
ANY = pl.BlockSpec(memory_space=pl.ANY)
HBM = pl.BlockSpec(memory_space=pltpu.HBM)
SMEM = pl.BlockSpec(memory_space=pltpu.SMEM)

GAIN1, SHIFT1, SCALE_ATTN, GAIN2, SHIFT2, SCALE_MLP, KERNEL_Q, KERNEL_K, KERNEL_V = (
    0, 1, 2, 3, 4, 5, 6, 9, 12,
)


def nn(left, right):
    return jnp.dot(left, right, preferred_element_type=FULL)


def nt(left, right):
    return lax.dot_general(left, right, (((1,), (1,)), ((), ())), preferred_element_type=FULL)


def tn(left, right):
    return lax.dot_general(left, right, (((0,), (0,)), ((), ())), preferred_element_type=FULL)


def block_at(side, at, me):
    far = 16 * (at & 1) + 8 * (at >> 1 & 1)
    low, high = at >> 2 & 1, at >> 3
    first, second = 2 * low + 4 * high, 4 * low + 2 * high
    return me ^ (jnp.where((me & 1) ^ side == 0, first, second) + far + side)


def block_rows(block, rows=ROWS):
    return pl.ds(pl.multiple_of(block * rows, rows), rows)


def fetch_blocks(sources, me, pieces, copy_to):
    for piece, target in zip(pieces, copy_to):
        for number, source in enumerate(sources):
            for at in range(BLOCKS // 4):
                block = block_at(number // 2, number % 2 * (BLOCKS // 4) + at, me)
                into, sem = target(block)
                pltpu.make_async_copy(source.at[at, piece], into, sem).start()


def store_blocks(targets, me, piece, copy_from, sem):
    keep, *sends = targets
    for side in range(2):
        for at in range(BLOCKS // 2):
            source = copy_from(block_at(side, at, me))
            half = BLOCKS // 4
            target = sends[at // half].at[at % half, piece] if side else keep.at[at, piece]
            pltpu.make_async_copy(source, target, sem).start()


def whole_wait(ref, sem):
    pltpu.make_async_copy(ref, ref, sem).wait()


def move(source, target, sem):
    copy = pltpu.make_async_copy(source, target, sem)
    copy.start()
    return copy


def down_one(values):
    at = lax.broadcasted_iota(jnp.int32, values.shape, 0)
    return jnp.where(at == 0, 0.0, pltpu.roll(values, 1, 0))


def up_one(values):
    at = lax.broadcasted_iota(jnp.int32, values.shape, 0)
    last = values.shape[0] - 1
    return jnp.where(at == last, 0.0, pltpu.roll(values, last, 0))


def normalise(values):
    center = jnp.mean(values, axis=1, keepdims=True)
    centered = values - center
    scale = lax.rsqrt(jnp.mean(centered * centered, axis=1, keepdims=True) + EPSILON)
    return centered * scale, scale


def row(table, index):
    return table[index : index + 1, :]


def front_kernel(
    me_ref, x_ref, source0, source1, source2, source3,
    table_out, n1_out, scale1_out, conv_out, qkv_out, probs_out, heads_out, attn_out, resid_out,
    n2_out, scale2_out, normed2_out,
    weights, x_rows, table, n1, scale1, conv, qkv, probs, heads, attn, resid, n2, scale2, normed2,
    in_sem, sems,
):
    me = me_ref[0]
    tokens = x_ref.shape[1]
    crops = tokens // LENGTH
    copies = []

    def send(source, target):
        copies.append(move(source, target, sems.at[len(copies)]))

    fetch_blocks(
        (source0, source1, source2, source3), me, (slice(None),),
        (lambda block: (weights.at[:, block_rows(block)], in_sem.at[0]),),
    )
    for at in range(0, tokens, 128):
        x_rows[at : at + 128, :] = x_ref[:, at : at + 128].T.astype(FULL)

    def norm_one(at, carry):
        rows = pl.ds(pl.multiple_of(at * 80, 80), 80)
        n1[rows, :], scale1[rows, :] = normalise(x_rows[rows, :])
        return carry

    lax.fori_loop(0, tokens // 80, norm_one, 0, unroll=True)
    send(n1, n1_out)
    send(scale1, scale1_out)
    whole_wait(weights, in_sem.at[0])
    table[...] = weights[4, :, 0:128].astype(FULL).T[0:16, :]
    send(table, table_out)

    def convolve(crop, carry):
        rows = pl.ds(pl.multiple_of(crop * LENGTH, LENGTH), LENGTH)
        for at in range(0, WIDTH, 128):
            lanes = slice(at, at + 128)
            normed = n1[rows, lanes] * table[GAIN1 : GAIN1 + 1, lanes] + table[SHIFT1 : SHIFT1 + 1, lanes]
            before, after = down_one(normed), up_one(normed)
            for k, start in enumerate((KERNEL_Q, KERNEL_K, KERNEL_V)):
                conv[k, rows, lanes] = (
                    table[start : start + 1, lanes] * before
                    + table[start + 1 : start + 2, lanes] * normed
                    + table[start + 2 : start + 3, lanes] * after
                ).astype(LOW)
        return carry

    lax.fori_loop(0, crops, convolve, 0, unroll=True)
    send(conv, conv_out)
    for k in range(3):
        qkv[k] = nn(conv[k], weights[k]).astype(LOW)
    send(qkv, qkv_out)

    near_t = lax.broadcasted_iota(jnp.int32, (LENGTH, LENGTH), 0)
    near_u = lax.broadcasted_iota(jnp.int32, (LENGTH, LENGTH), 1)
    nearby = jnp.abs(near_t - near_u) <= WINDOW // 2

    def attend(crop, carry):
        rows = pl.ds(pl.multiple_of(crop * LENGTH, LENGTH), LENGTH)
        for h in range(HEADS):
            lanes = slice(h * HEAD_DIM, (h + 1) * HEAD_DIM)
            scores = jnp.where(nearby, nt(qkv[0, rows, lanes], qkv[1, rows, lanes]) * FACTOR, -1e30)
            powers = jnp.exp(scores - jnp.max(scores, axis=1, keepdims=True))
            shares = powers / jnp.sum(powers, axis=1, keepdims=True)
            probs[crop, h] = shares
            heads[rows, lanes] = nn(shares.astype(LOW), qkv[2, rows, lanes]).astype(LOW)
        return carry

    lax.fori_loop(0, crops, attend, 0, unroll=True)
    send(probs, probs_out)
    send(heads, heads_out)
    attn[...] = nn(heads[...], weights[3])
    send(attn, attn_out)

    def norm_two(at, carry):
        rows = pl.ds(pl.multiple_of(at * 80, 80), 80)
        mixed = x_rows[rows, :] + row(table, SCALE_ATTN) * attn[rows, :]
        resid[rows, :] = mixed
        normal, scale = normalise(mixed)
        n2[rows, :], scale2[rows, :] = normal, scale
        normed2[rows, :] = (normal * row(table, GAIN2) + row(table, SHIFT2)).astype(LOW)
        return carry

    lax.fori_loop(0, tokens // 80, norm_two, 0, unroll=True)
    send(normed2, normed2_out)
    send(resid, resid_out)
    send(n2, n2_out)
    send(scale2, scale2_out)
    for copy in copies:
        copy.wait()


def front(me, x, sources):
    tokens = x.shape[1]
    crops = tokens // LENGTH
    shapes = [
        shape(16, WIDTH),
        shape(tokens, WIDTH),
        shape(tokens, 1),
        shape(3, tokens, WIDTH, kind=LOW),
        shape(3, tokens, WIDTH, kind=LOW),
        shape(crops, HEADS, LENGTH, LENGTH),
        shape(tokens, WIDTH, kind=LOW),
        shape(tokens, WIDTH),
        shape(tokens, WIDTH),
        shape(tokens, WIDTH),
        shape(tokens, 1),
        shape(tokens, WIDTH, kind=LOW),
    ]
    return pl.pallas_call(
        front_kernel,
        in_specs=[SMEM, VMEM] + [ANY] * 4,
        out_specs=[HBM] * 12,
        out_shape=shapes,
        scratch_shapes=[
            pltpu.VMEM((5, WIDTH, WIDTH), LOW),
            pltpu.VMEM((tokens, WIDTH), FULL),
        ]
        + [pltpu.VMEM(one.shape, one.dtype) for one in shapes]
        + [pltpu.SemaphoreType.DMA((1,)), pltpu.SemaphoreType.DMA((12,))],
        compiler_params=pltpu.CompilerParams(vmem_limit_bytes=56 << 20),
        cost_estimate=spent(0.5),
        name="front",
    )(me, x, *sources)


def spent(microseconds):
    return pl.CostEstimate(flops=int(microseconds * 1.15e9), bytes_accessed=0, transcendentals=0)


def shape(*dims, kind=FULL):
    return jax.ShapeDtypeStruct(dims, kind)


def gelu_both(values):
    below = 0.5 + 0.5 * lax.erf(values * math.sqrt(0.5))
    bell = jnp.exp(-0.5 * values * values)
    return values * below, below + values * bell * (0.5 * math.sqrt(2 / math.pi))


def mlp_kernel(
    me_ref, cot_in, normed2_in, table, resid_in, n2_in, scale2_in, attn_in, source0, source1, source2, source3,
    out, d_resid_out, d_attn_out, small, keep, send_low, send_high,
    up, down, normed2_t, cot_rows, d_branch, branch, active, slope, d_hidden, d_normed2, grad_up,
    grad_down, resid, n2, scale2, attn, d_resid, d_attn, cot_ref, normed2, sems,
):
    me = me_ref[0]
    tokens = cot_ref.shape[1]
    first = move(normed2_in, normed2, sems.at[10])
    second = move(cot_in, cot_ref, sems.at[11])

    fetch_blocks(
        (source0, source1, source2, source3), me, (slice(0, CHUNKS), slice(CHUNKS, 2 * CHUNKS)),
        (
            lambda block: (up.at[:, block_rows(block)], sems.at[0]),
            lambda block: (down.at[block_rows(block, CHUNKS)], sems.at[1]),
        ),
    )
    scale_mlp = row(table, SCALE_MLP)
    first.wait()
    second.wait()
    for at in range(0, tokens, 128):
        rows = slice(at, at + 128)
        cot_rows[rows, :] = cot_ref[:, rows].T
        d_branch[rows, :] = (scale_mlp * cot_rows[rows, :].astype(FULL)).astype(LOW)
        normed2_t[:, rows] = normed2[rows, :].T
    whole_wait(up, sems.at[0])

    for chunk in range(CHUNKS):
        rows = slice(chunk * BLOCKS, (chunk + 1) * BLOCKS)
        hidden = nn(normed2[...], up[chunk])
        value, slope[...] = gelu_both(hidden)
        active[...] = value.astype(LOW)
        if chunk == 0:
            whole_wait(down, sems.at[1])
            arrivals = [
                move(source, target, sems.at[4 + at])
                for at, (source, target) in enumerate(
                    ((resid_in, resid), (n2_in, n2), (scale2_in, scale2), (attn_in, attn))
                )
            ]
        down_rows = down[rows].reshape(WIDTH, WIDTH)
        d_active = nt(d_branch[...], down_rows)
        d_hidden[...] = (d_active * slope[...]).astype(LOW)
        added = nn(active[...], down_rows)
        back = nt(d_hidden[...], up[chunk])
        branch[...] = added if chunk == 0 else branch[...] + added
        d_normed2[...] = back if chunk == 0 else d_normed2[...] + back
        grad_up[chunk] = nn(normed2_t[...], d_hidden[...]).astype(LOW)
        grad_down[rows] = tn(active[...], d_branch[...]).astype(LOW).reshape(BLOCKS, ROWS, WIDTH)

    store_blocks(
        (keep, send_low, send_high), me, slice(0, CHUNKS), lambda block: grad_up.at[:, block_rows(block)],
        sems.at[3],
    )
    store_blocks(
        (keep, send_low, send_high), me, slice(CHUNKS, 2 * CHUNKS),
        lambda block: grad_down.at[block_rows(block, CHUNKS)], sems.at[2],
    )
    for copy in arrivals:
        copy.wait()

    def norm_back(at, sums):
        rows = pl.ds(pl.multiple_of(at * 80, 80), 80)
        grad, normal, cot = d_normed2[rows, :], n2[rows, :], cot_rows[rows, :].astype(FULL)
        s = row(table, GAIN2) * grad
        along = jnp.mean(s * normal, axis=1, keepdims=True)
        middle = jnp.mean(s, axis=1, keepdims=True)
        total = cot + (s - middle - normal * along) * scale2[rows, :]
        d_resid[rows, :] = total
        d_attn[rows, :] = (row(table, SCALE_ATTN) * total).astype(LOW)
        terms = (grad * normal, grad, total * attn[rows, :], cot * branch[rows, :])
        return tuple(one + jnp.sum(more, axis=0, keepdims=True) for one, more in zip(sums, terms))

    sums = lax.fori_loop(0, tokens // 80, norm_back, (jnp.zeros((1, WIDTH), FULL),) * 4, unroll=True)
    leaving = [
        move(d_attn, d_attn_out, sems.at[8]),
        move(d_resid, d_resid_out, sems.at[9]),
    ]
    for at, one in enumerate(sums):
        small[at : at + 1, :] = one
    for at in range(0, tokens, 128):
        rows = slice(at, at + 128)
        out[:, rows] = (resid[rows, :] + scale_mlp * branch[rows, :]).astype(LOW).T
    whole_wait(grad_down, sems.at[2])
    whole_wait(grad_up, sems.at[3])
    for copy in leaving:
        copy.wait()


def mlp(me, cot, normed2, table, resid, n2, scale2, attn, sources):
    tokens = cot.shape[1]
    pieces = (BLOCKS // 2, 2 * CHUNKS, ROWS, WIDTH)
    halves = (BLOCKS // 4,) + pieces[1:]
    rows_full, rows_low = pltpu.VMEM((tokens, WIDTH), FULL), pltpu.VMEM((tokens, WIDTH), LOW)
    return pl.pallas_call(
        mlp_kernel,
        in_specs=[SMEM, HBM, HBM, VMEM] + [HBM] * 4 + [ANY] * 4,
        out_specs=[VMEM, HBM, HBM, VMEM, HBM, HBM, HBM],
        out_shape=[
            shape(WIDTH, tokens, kind=LOW),
            shape(tokens, WIDTH),
            shape(tokens, WIDTH, kind=LOW),
            shape(8, WIDTH),
            shape(*pieces, kind=LOW),
            shape(*halves, kind=LOW),
            shape(*halves, kind=LOW),
        ],
        scratch_shapes=[
            pltpu.VMEM((CHUNKS, WIDTH, WIDTH), LOW),
            pltpu.VMEM((HIDDEN // ROWS, ROWS, WIDTH), LOW),
            pltpu.VMEM((WIDTH, tokens), LOW),
            rows_low,
            rows_low,
            rows_full,
            rows_low,
            rows_full,
            rows_low,
            rows_full,
            pltpu.VMEM((CHUNKS, WIDTH, WIDTH), LOW),
            pltpu.VMEM((HIDDEN // ROWS, ROWS, WIDTH), LOW),
            rows_full,
            rows_full,
            pltpu.VMEM((tokens, 1), FULL),
            rows_full,
            rows_full,
            rows_low,
            pltpu.VMEM((WIDTH, tokens), LOW),
            rows_low,
            pltpu.SemaphoreType.DMA((12,)),
        ],
        compiler_params=pltpu.CompilerParams(vmem_limit_bytes=56 << 20),
        cost_estimate=spent(0.5),
        name="mlp",
    )(me, cot, normed2, table, resid, n2, scale2, attn, *sources)


def attend_back_kernel(
    me_ref, d_attn_in, heads_in, qkv_in, probs_in, conv_in, source0, source1, source2, source3,
    d_qkv_out, keep, send_low, send_high,
    w_out, d_attn, heads, qkv, probs, conv, d_heads, d_qkv, grads, sems,
):
    me = me_ref[0]
    crops = d_attn.shape[0] // LENGTH
    soon = [move(heads_in, heads, sems.at[3]), move(d_attn_in, d_attn, sems.at[4])]
    fetch_blocks(
        (source0, source1, source2, source3), me, (3,),
        (lambda block: (w_out.at[block_rows(block)], sems.at[0]),),
    )
    later = [move(qkv_in, qkv, sems.at[5]), move(probs_in, probs, sems.at[6])]
    for copy in soon:
        copy.wait()
    grads[3] = tn(heads[...], d_attn[...]).astype(LOW)
    whole_wait(w_out, sems.at[0])
    d_heads[...] = nt(d_attn[...], w_out[...]).astype(LOW)
    convs = move(conv_in, conv, sems.at[7])
    for copy in later:
        copy.wait()

    def attend(crop, carry):
        rows = pl.ds(pl.multiple_of(crop * LENGTH, LENGTH), LENGTH)
        for h in range(HEADS):
            lanes = slice(h * HEAD_DIM, (h + 1) * HEAD_DIM)
            shares, grad = probs[crop, h], d_heads[rows, lanes]
            d_probs = nt(grad, qkv[2, rows, lanes])
            d_qkv[2, rows, lanes] = tn(shares.astype(LOW), grad).astype(LOW)
            d_scores = shares * (d_probs - jnp.sum(shares * d_probs, axis=1, keepdims=True))
            d_scores = d_scores.astype(LOW)
            d_qkv[0, rows, lanes] = (nn(d_scores, qkv[1, rows, lanes]) * FACTOR).astype(LOW)
            d_qkv[1, rows, lanes] = (tn(d_scores, qkv[0, rows, lanes]) * FACTOR).astype(LOW)
        return carry

    lax.fori_loop(0, crops, attend, 0, unroll=True)
    leaving = move(d_qkv, d_qkv_out, sems.at[1])
    convs.wait()
    for k in range(3):
        grads[k] = tn(conv[k], d_qkv[k]).astype(LOW)
    store_blocks(
        (keep, send_low, send_high), me, slice(None), lambda block: grads.at[:, block_rows(block)], sems.at[2]
    )
    leaving.wait()
    whole_wait(grads, sems.at[2])


def attend_back(me, d_attn, heads, qkv, probs, conv, sources):
    tokens = heads.shape[0]
    pieces = (BLOCKS // 2, 4, ROWS, WIDTH)
    halves = (BLOCKS // 4,) + pieces[1:]
    rows_low = pltpu.VMEM((tokens, WIDTH), LOW)
    return pl.pallas_call(
        attend_back_kernel,
        in_specs=[SMEM] + [HBM] * 5 + [ANY] * 4,
        out_specs=[HBM] * 4,
        out_shape=[
            shape(3, tokens, WIDTH, kind=LOW),
            shape(*pieces, kind=LOW),
            shape(*halves, kind=LOW),
            shape(*halves, kind=LOW),
        ],
        scratch_shapes=[
            pltpu.VMEM((WIDTH, WIDTH), LOW),
            rows_low,
            rows_low,
            pltpu.VMEM(qkv.shape, LOW),
            pltpu.VMEM(probs.shape, FULL),
            pltpu.VMEM(conv.shape, LOW),
            rows_low,
            pltpu.VMEM(qkv.shape, LOW),
            pltpu.VMEM((4, WIDTH, WIDTH), LOW),
            pltpu.SemaphoreType.DMA((8,)),
        ],
        compiler_params=pltpu.CompilerParams(vmem_limit_bytes=56 << 20),
        cost_estimate=spent(10),
        name="attend_back",
    )(me, d_attn, heads, qkv, probs, conv, *sources)


def front_back_kernel(
    me_ref, table, small, d_qkv_in, n1_in, scale1_in, d_resid_in, source0, source1, source2, source3,
    both_out,
    weights, d_qkv, n1, scale1, d_resid, d_conv, sums, both, sems,
):
    me = me_ref[0]
    tokens = n1.shape[0]
    crops = tokens // LENGTH
    soon = [move(d_qkv_in.at[k], d_qkv.at[k], sems.at[5 + k]) for k in range(3)]
    fetch_blocks(
        (source0, source1, source2, source3), me, (slice(0, 3),),
        (lambda block: (weights.at[:, block_rows(block)], sems.at[1]),),
    )
    later = [
        move(n1_in, n1, sems.at[2]),
        move(scale1_in, scale1, sems.at[3]),
        move(d_resid_in, d_resid, sems.at[4]),
    ]
    sums[...] = jnp.zeros_like(sums)
    whole_wait(weights, sems.at[1])
    for k in range(3):
        soon[k].wait()
        d_conv[k] = nt(d_qkv[k], weights[k])
    for copy in later:
        copy.wait()

    def back(crop, carry):
        rows = pl.ds(pl.multiple_of(crop * LENGTH, LENGTH), LENGTH)
        middle = jnp.zeros((LENGTH, 1), FULL)
        along = jnp.zeros((LENGTH, 1), FULL)
        for at in range(0, WIDTH, 128):
            lanes = slice(at, at + 128)
            gain = table[GAIN1 : GAIN1 + 1, lanes]
            normal = n1[rows, lanes]
            normed = normal * gain + table[SHIFT1 : SHIFT1 + 1, lanes]
            before, after = down_one(normed), up_one(normed)
            parts = [0.0, 0.0, 0.0]
            for k, start in enumerate((KERNEL_Q, KERNEL_K, KERNEL_V)):
                grad = d_conv[k, rows, lanes]
                for j, seen in enumerate((before, normed, after)):
                    sums[start + j : start + j + 1, lanes] += jnp.sum(grad * seen, axis=0, keepdims=True)
                    parts[j] = parts[j] + table[start + j : start + j + 1, lanes] * grad
            total = up_one(parts[0]) + parts[1] + down_one(parts[2])
            sums[GAIN1 : GAIN1 + 1, lanes] += jnp.sum(total * normal, axis=0, keepdims=True)
            sums[SHIFT1 : SHIFT1 + 1, lanes] += jnp.sum(total, axis=0, keepdims=True)
            s = gain * total
            d_conv[0, rows, lanes] = s
            middle += jnp.sum(s, axis=1, keepdims=True)
            along += jnp.sum(s * normal, axis=1, keepdims=True)
        middle, along = middle / WIDTH, along / WIDTH
        for at in range(0, WIDTH, 128):
            lanes = slice(at, at + 128)
            d_conv[1, rows, lanes] = d_resid[rows, lanes] + (
                d_conv[0, rows, lanes] - middle - n1[rows, lanes] * along
            ) * scale1[rows, :]
        return carry

    lax.fori_loop(0, crops, back, 0, unroll=True)
    leaving = []
    for at in range(0, tokens, 128):
        lanes = slice(at, at + 128)
        both[:, lanes] = d_conv[1, lanes, :].astype(LOW).T
        leaving.append(move(both.at[:, lanes], both_out.at[:, lanes], sems.at[8 + at // 128]))
    sums[GAIN2 : SHIFT2 + 1, :] = small[0:2, :]
    sums[SCALE_ATTN : SCALE_ATTN + 1, :] = small[2:3, :]
    sums[SCALE_MLP : SCALE_MLP + 1, :] = small[3:4, :]
    high = sums[0:16, :].astype(LOW).astype(FULL)
    sums[16:32, :] = sums[0:16, :] - high
    lanes = slice(tokens, tokens + 128)
    both[:, lanes] = sums[...].astype(LOW).T
    leaving.append(move(both.at[:, lanes], both_out.at[:, lanes], sems.at[8 + tokens // 128]))
    for copy in leaving:
        copy.wait()


def front_back(me, table, d_qkv, scale1, small, n1, d_resid, sources):
    tokens = n1.shape[0]
    rows_full = pltpu.VMEM((tokens, WIDTH), FULL)
    return pl.pallas_call(
        front_back_kernel,
        in_specs=[SMEM] + [VMEM] * 2 + [HBM] * 4 + [ANY] * 4,
        out_specs=HBM,
        out_shape=shape(WIDTH, tokens + 128, kind=LOW),
        scratch_shapes=[
            pltpu.VMEM((3, WIDTH, WIDTH), LOW),
            pltpu.VMEM(d_qkv.shape, LOW),
            rows_full,
            pltpu.VMEM((tokens, 1), FULL),
            rows_full,
            pltpu.VMEM((3, tokens, WIDTH), FULL),
            pltpu.VMEM((128, WIDTH), FULL),
            pltpu.VMEM((WIDTH, tokens + 128), LOW),
            pltpu.SemaphoreType.DMA((9 + tokens // 128,)),
        ],
        compiler_params=pltpu.CompilerParams(vmem_limit_bytes=56 << 20),
        cost_estimate=spent(8),
        name="front_back",
    )(me, table, small, d_qkv, n1, scale1, d_resid, *sources)


def unpack_kernel(arrived, out, frames, output, *rest):
    vectors, kernels, square = rest[:6], rest[6:9], rest[9]
    count, _, columns = arrived.shape
    columns -= 128
    total = jnp.zeros((ROWS, 128), FULL)
    for at in range(count):
        frames[:, at * columns : (at + 1) * columns] = arrived[at, :, 0:columns]
        output[:, at * columns : (at + 1) * columns] = out[at]
        total += arrived[at, :, columns : columns + 128].astype(FULL)
    square[...] = jnp.zeros_like(square)
    square[0:ROWS, :] = total
    sums = square[...].T
    sums = sums[0:16, :] + sums[16:32, :]
    for at, one in enumerate(vectors):
        one[...] = sums[at : at + 1, 0:ROWS]
    for at, one in zip((KERNEL_Q, KERNEL_K, KERNEL_V), kernels):
        one[...] = sums[at : at + 3, 0:ROWS]


def unpack(arrived, out):
    count, rows, columns = arrived.shape
    found = pl.pallas_call(
        unpack_kernel,
        in_specs=[VMEM] * 2,
        out_specs=[VMEM] * 11,
        out_shape=[shape(rows, count * (columns - 128), kind=LOW)] * 2
        + [shape(1, rows)] * 6
        + [shape(3, rows)] * 3,
        scratch_shapes=[pltpu.VMEM((128, 128), FULL)],
        cost_estimate=spent(0.5),
        name="unpack",
    )(arrived, out)
    vectors, kernels = found[2:8], found[8:]
    return found[0], found[1], [one.reshape(rows) for one in vectors], [one.T for one in kernels]


def pack_kernel(
    gain1, shift1, scale_attn, gain2, shift2, scale_mlp, kernel_q, kernel_k, kernel_v,
    w_query, w_key, w_value, w_out, w_up, w_down,
    attn_shard, mlp_shard, table,
):
    table[...] = jnp.zeros_like(table)
    for at, one in enumerate((gain1, shift1, scale_attn, gain2, shift2, scale_mlp)):
        table[at : at + 1, 0:ROWS] = one[...].astype(FULL)
    for at, one in ((KERNEL_Q, kernel_q), (KERNEL_K, kernel_k), (KERNEL_V, kernel_v)):
        table[at : at + 3, 0:ROWS] = one[...].astype(FULL)
    attn_shard[4] = jnp.zeros((ROWS, WIDTH), LOW)
    attn_shard[4, :, 0:128] = table[...].T[0:ROWS, :].astype(LOW)
    for at, one in ((0, w_query), (1, w_key), (2, w_value), (3, w_out)):
        attn_shard[at] = one[...]
    for chunk in range(CHUNKS):
        mlp_shard[chunk] = w_up[:, chunk * WIDTH : (chunk + 1) * WIDTH]
        mlp_shard[CHUNKS + chunk] = w_down[chunk * ROWS : (chunk + 1) * ROWS, :]


def pack(vectors, kernels, matrices):
    return pl.pallas_call(
        pack_kernel,
        in_specs=[VMEM] * 15,
        out_specs=[VMEM] * 2,
        out_shape=[
            shape(5, ROWS, WIDTH, kind=LOW),
            shape(2 * CHUNKS, ROWS, WIDTH, kind=LOW),
        ],
        scratch_shapes=[pltpu.VMEM((128, 128), FULL)],
        name="pack",
    )(*[one.reshape(1, -1) for one in vectors], *[one.T for one in kernels], *matrices)


FIVE = 6


def permute(values, even, odd):
    count = lax.axis_size("dev")
    return lax.ppermute(
        values, "dev", [(at, at ^ (odd if at & 1 else even)) for at in range(count)]
    )


def after(first, *others):
    return lax.optimization_barrier((first,) + others)


def grown(blocks, even, odd, before=None):
    others = permute(blocks, even, odd)
    if before is not None:
        others = after(before, others)[1]
    return jnp.concatenate((blocks, others))


def upper(*parts):
    count = parts[-1].shape[0]
    return sum(one[count // 2 : count].astype(FULL) for one in parts).astype(LOW)


def step(before, parts, even, odd, late=False):
    if late:
        _, parts[-1] = after(before, parts[-1])
    sent = upper(*parts)
    if not late:
        before, sent = after(before, sent)
    return sent if late else before, parts + [permute(sent, even, odd)]


def finish_kernel(*refs):
    arrivals, outputs = refs[:FIVE], refs[FIVE:]
    done = 0
    for one in outputs:
        for at in range(one.shape[0] // ROWS * (one.shape[1] // WIDTH)):
            total = sum(more[0, done].astype(FULL) for more in arrivals)
            if one.shape[1] > WIDTH:
                one[:, at * WIDTH : (at + 1) * WIDTH] = total
            else:
                one[at * ROWS : (at + 1) * ROWS, :] = total
            done += 1


def finish(parts, shapes):
    spec = pl.BlockSpec((1,) + parts[0].shape[1:], lambda _: (0, 0, 0, 0))
    return pl.pallas_call(
        finish_kernel,
        grid=(1,),
        in_specs=[spec] * FIVE,
        out_specs=[pl.BlockSpec(one, lambda _: (0, 0)) for one in shapes],
        out_shape=[shape(*one) for one in shapes],
        cost_estimate=spent(0.5),
        name="finish",
    )(*parts)


def gather_plain(pieces):
    whole = [lax.all_gather(one, "dev", axis=0, tiled=True) for one in pieces]
    return jnp.stack([one.reshape(BLOCKS, ROWS, WIDTH) for one in whole], axis=1)


def places_plain():
    sides = ([0] * (BLOCKS // 2), [0] * (BLOCKS // 2))
    for block in range(BLOCKS):
        x, y, near_z, far_z = (block >> 1) & 1, (block >> 2) & 1, (block >> 3) & 1, block >> 4
        across = 8 * x + 4 * y if block & 1 else 8 * y + 4 * x
        sides[block & 1][across + 2 * near_z + far_z] = block
    return sides


def apart(blocks):
    return tuple(
        jnp.stack([blocks[k] for k in half])
        for side in places_plain()
        for half in (side[: BLOCKS // 4], side[BLOCKS // 4 :])
    )


def together(kept, sent):
    order = places_plain()
    found = {block: (side, at) for side in range(2) for at, block in enumerate(order[side])}
    return jnp.stack([(kept, sent)[found[k][0]][found[k][1]] for k in range(BLOCKS)])


def scatter_plain(matrix):
    return lax.psum_scatter(matrix.astype(FULL), "dev", scatter_dimension=0, tiled=True)


def local(
    frames,
    norm1_gain,
    norm1_shift,
    kernel_query,
    kernel_key,
    kernel_value,
    w_query,
    w_key,
    w_value,
    w_out,
    scale_attn,
    norm2_gain,
    norm2_shift,
    w_up,
    w_down,
    scale_mlp,
    cotangent,
):
    count = lax.axis_size("dev")
    own, columns = frames.shape[0], frames.shape[1] // count
    fast = own == ROWS and own * count == WIDTH
    vectors = (norm1_gain, norm1_shift, scale_attn, norm2_gain, norm2_shift, scale_mlp)
    kernels = (kernel_query, kernel_key, kernel_value)

    def to_crops(values):
        split = values.reshape(own, count, columns).transpose(1, 0, 2)
        return lax.all_to_all(split, "dev", 0, 0).reshape(WIDTH, columns)

    def to_devices(values):
        return lax.all_to_all(values.reshape(count, own, -1), "dev", 0, 0)

    def by_channels(blocks):
        return blocks.transpose(1, 0, 2).reshape(own, -1)

    matrices = (w_query, w_key, w_value, w_out)
    matrices = (w_query, w_key, w_value, w_out)
    x = to_crops(frames)
    if fast:
        me = lax.axis_index("dev").astype(jnp.int32).reshape(1)
        attn_shard, mlp_shard = pack(vectors, kernels, matrices + (w_up, w_down))
        blocks = grown(attn_shard[None], 16, 16)
        mlp_shard = after(blocks, mlp_shard)[1]
        blocks = grown(blocks, 8, 8)
        mlp_blocks = grown(mlp_shard[None], 16, 16, blocks)
        blocks = grown(blocks, 2, 4)
        cotangent = after(blocks, cotangent)[1]
        mlp_blocks = grown(mlp_blocks, 8, 8, blocks)
        others = permute(blocks, 4, 2)
        attn_sources = (blocks, others, permute(blocks, 1, 1), permute(others, 1, 1))
        mlp_blocks = grown(mlp_blocks, 2, 4, others)
        mlp_others = permute(mlp_blocks, 4, 2)
        x = after(mlp_blocks, x)[1]
    else:
        me = jnp.zeros((1,), jnp.int32)
        small = jnp.concatenate([one[:, None] for one in vectors] + list(kernels), axis=1)
        small = jnp.pad(small, ((0, 0), (0, WIDTH - small.shape[1])))
        attn_sources = apart(gather_plain(matrices + (small,)))
        ups = gather_plain([w_up[:, k * WIDTH : (k + 1) * WIDTH] for k in range(CHUNKS)])
        downs = lax.all_gather(w_down, "dev", axis=0, tiled=True)
        downs = downs.reshape(BLOCKS, CHUNKS, ROWS, WIDTH)
        mlp_sources = apart(jnp.concatenate((ups, downs), axis=1))
    cot = to_crops(cotangent)
    table, n1, scale1, conv, qkv, probs, heads, attn, resid, n2, scale2, normed2 = front(
        me, x, attn_sources
    )
    if fast:
        mlp_others = after(normed2, mlp_others)[1]
        mlp_sources = (
            mlp_blocks, mlp_others, permute(mlp_blocks, 1, 1), permute(mlp_others, 1, 1),
        )
    out, d_resid, d_attn, small, keep_mlp, *send_mlp = mlp(
        me, cot, normed2, table, resid, n2, scale2, attn, mlp_sources
    )
    out = to_devices(out)
    if fast:
        last, first = (permute(one, 1, 1) for one in reversed(send_mlp))
        sent = (keep_mlp[8:].astype(FULL) + last.astype(FULL)).astype(LOW)
        d_attn, sent = after(d_attn, sent)
        mlp_parts = [keep_mlp, first, permute(sent, 4, 2)]
    d_qkv, keep, *send = attend_back(
        me, d_attn, heads, qkv, probs, conv, attn_sources
    )
    if fast:
        last, first = (permute(one, 1, 1) for one in reversed(send))
        now, mlp_parts = step(d_qkv, mlp_parts, 2, 4, True)
        last = after(now, last)[1]
        now = (keep[8:].astype(FULL) + last.astype(FULL)).astype(LOW)
        parts = [keep, first, permute(now, 4, 2)]
        _, d_qkv = after(now, d_qkv)
    both = front_back(me, table, d_qkv, scale1, small, n1, d_resid, attn_sources)
    arrived = to_devices(both)
    if fast:
        _, out = after(both, out)
        now, mlp_parts = step(both, mlp_parts, 8, 8, True)
        now, parts = step(now, parts, 2, 4, True)
        now, mlp_parts = step(now, mlp_parts, 16, 16, True)
        now, parts = step(now, parts, 8, 8, True)
        frames_grad, output, vector_grads, kernel_grads = unpack(arrived, out)
        frames_grad, parts[-1] = after(frames_grad, parts[-1])
        now, parts = step(now, parts, 16, 16, True)
        grad_up, grad_down = finish(mlp_parts, ((own, HIDDEN), (CHUNKS * own, WIDTH)))
        grad_query, grad_key, grad_value, grad_out = finish(parts, ((own, WIDTH),) * 4)
    else:
        output = by_channels(out)
        blocks = together(keep_mlp, jnp.concatenate(send_mlp))
        ups = blocks[:, :CHUNKS].transpose(0, 2, 1, 3).reshape(WIDTH, HIDDEN)
        grad_up = scatter_plain(ups)
        grad_down = scatter_plain(blocks[:, CHUNKS:].reshape(HIDDEN, WIDTH))
        blocks = together(keep, jnp.concatenate(send))
        grad_query, grad_key, grad_value, grad_out = (
            scatter_plain(blocks[:, k].reshape(WIDTH, WIDTH)) for k in range(4)
        )
        frames_grad = by_channels(arrived[:, :, :columns])
        sums = jnp.sum(arrived[:, :, columns:].astype(FULL), axis=0)
        sums = sums[:, 0:16] + sums[:, 16:32]
        vector_grads = [sums[:, k] for k in range(6)]
        kernel_grads = [sums[:, k : k + 3] for k in (KERNEL_Q, KERNEL_K, KERNEL_V)]
    return (
        output,
        frames_grad,
        vector_grads[GAIN1],
        vector_grads[SHIFT1],
        *kernel_grads,
        grad_query,
        grad_key,
        grad_value,
        grad_out,
        vector_grads[SCALE_ATTN],
        vector_grads[GAIN2],
        vector_grads[SHIFT2],
        grad_up,
        grad_down,
        vector_grads[SCALE_MLP],
    )


def solution(mesh):
    in_specs = (
        P("dev", None),
        P("dev"),
        P("dev"),
        P("dev", None),
        P("dev", None),
        P("dev", None),
        P("dev", None),
        P("dev", None),
        P("dev", None),
        P("dev", None),
        P("dev"),
        P("dev"),
        P("dev"),
        P("dev", None),
        P("dev", None),
        P("dev"),
        P("dev", None),
    )
    out_specs = (
        P("dev", None),
        P("dev", None),
        P("dev"),
        P("dev"),
        P("dev", None),
        P("dev", None),
        P("dev", None),
        P("dev", None),
        P("dev", None),
        P("dev", None),
        P("dev", None),
        P("dev"),
        P("dev"),
        P("dev"),
        P("dev", None),
        P("dev", None),
        P("dev"),
    )
    return jax.shard_map(local, mesh=mesh, in_specs=in_specs, out_specs=out_specs, check_vma=False)
```
